256 devices in a mesh: tensor: 16 (over x_lo, z), dw: 16 (over x_hi, y, core).
Axes of the slice: x: 4 (x_hi: 2, x_lo: 2; x = x_hi * 2 + x_lo), y: 4, z: 8, core: 2. Of those that a mesh axis runs over, the one named last changes fastest.
Arguments:
- tokens: bfloat16 [6144, 4096], P(('tensor', 'dw')), may hold values from -24 to 24
- out_grad: bfloat16 [6144, 4096], P(('tensor', 'dw')), may hold values from -24 to 24
- gate_weight: bfloat16 [4096, 8192], P('dw', 'tensor'), may hold values from -0.09375 to 0.09375
- up_weight: bfloat16 [4096, 8192], P('dw', 'tensor'), may hold values from -0.09375 to 0.09375
- down_weight: bfloat16 [8192, 4096], P('tensor', 'dw'), may hold values from -0.0625 to 0.0625
Outputs:
- grad_tokens: bfloat16 [6144, 4096], P(('tensor', 'dw'))
- grad_gate: bfloat16 [4096, 8192], P('dw', 'tensor')
- grad_up: bfloat16 [4096, 8192], P('dw', 'tensor')
- grad_down: bfloat16 [8192, 4096], P('tensor', 'dw')
The draws below stay inside these ranges and needn't reach their ends.
All inputs are finite; a program needn't handle non-finite values.
Results may differ from the reference program's by a relative error of at most 0.023.
Values may be sent and summed in bfloat16 or wider, within the bound.
No kernel may reach another device: no remote copies, remote signals or barrier semaphores. Data moves between devices by JAX's collectives and lax.ppermute only.
A program may use at most 128 MiB of HBM per device.

```python
import math
import jax
import jax.numpy as jnp
from jax import lax

D = 4096
FF = 8192
TOK_GRP = 384
TOKENS = 6144
N_TENSOR = 16
N_DW = 16


def raised(values, key, source, target, blocks, factor):
    owner, partner = [(jnp.arange(values.shape[axis_at]) // (values.shape[axis_at] // blocks)).reshape([-1 if axis == axis_at else 1 for axis in range(values.ndim)]) for axis_at in (source, target)]
    chosen = jax.random.permutation(key, blocks)[partner]
    strong = (owner == chosen) | (owner == (partner + blocks // 2) % blocks)
    return jnp.where(strong, factor * values, values)


def steps_of(stream_key, shape, pieces, least, largest):
    factor_of, own = 1.0, jax.random.fold_in(stream_key, 6)
    for dim, blocks in pieces:
        heights = jnp.exp(jax.random.uniform(jax.random.fold_in(own, dim), (blocks,), jnp.float32, least / len(pieces), largest / len(pieces)))
        factor_of = factor_of * jnp.repeat(heights, shape[dim] // blocks).reshape([-1 if axis == dim else 1 for axis in range(len(shape))])
    return factor_of


def bell_draw(key, extent, deviation, most, cuts=(), dtype=jnp.bfloat16):
    values = jax.random.normal(key, extent, jnp.float32) * deviation
    if len(cuts) > 0:
        values = steps_of(key, extent, cuts, -0.22, 0.18) * values
    return jnp.clip(values, min=-most, max=most).astype(dtype)


def heavy_noise(stream_key, extent, spread, limit, pieces, heavy, kind=jnp.bfloat16):
    values = spread * jax.random.normal(stream_key, extent, jnp.float32)
    if pieces:
        values = values * steps_of(stream_key, extent, pieces, -0.22, 0.18)
    return jnp.clip(raised(values, jax.random.fold_in(stream_key, 3), *heavy), -limit, limit).astype(kind)


def setup_inputs(seed: int = 0) -> dict:
    arg_keys = jax.random.split(jax.random.key(seed), 6)
    tokens = heavy_noise(arg_keys[0], (TOKENS, D), 1.0, 24.0, ((0, 256),), (0, 1, 256, 6.0))
    out_grad = heavy_noise(arg_keys[1], (TOKENS, D), 1.0, 24.0, ((0, 256),), (0, 1, 256, 6.0))
    gate_weight = bell_draw(arg_keys[2], (D, FF), D ** -0.5, 0.09375, ((0, 16), (1, 16)))
    up_weight = bell_draw(arg_keys[3], (D, FF), D ** -0.5, 0.09375, ((0, 16), (1, 16)))
    down_weight = bell_draw(arg_keys[4], (FF, D), FF ** -0.5, 0.0625, ((0, 16), (1, 16)))
    return dict(tokens=tokens, out_grad=out_grad, gate_weight=gate_weight, up_weight=up_weight, down_weight=down_weight)


def to_groups(array):
    tok_dev = TOK_GRP // N_TENSOR
    return array.reshape(N_TENSOR, N_DW, tok_dev, D).transpose(1, 0, 2, 3).reshape(N_DW, TOK_GRP, D)

def reference(tokens, out_grad, gate_weight, up_weight, down_weight):
    grad_scale = 1.0 / math.sqrt(TOKENS)
    tok_dev = TOK_GRP // N_TENSOR
    width = FF // N_TENSOR
    gate_cols = gate_weight.astype(jnp.float32).reshape(D, N_TENSOR, width)
    up_cols = up_weight.astype(jnp.float32).reshape(D, N_TENSOR, width)
    down_rows = down_weight.T

    def group_step(carry, inputs):
        tok_rows, grad_rows = inputs
        gate_act = jnp.dot(tok_rows, gate_weight, preferred_element_type=jnp.float32)
        up_act = jnp.dot(tok_rows, up_weight, preferred_element_type=jnp.float32)
        hidden_grad = jnp.dot(grad_rows, down_rows, preferred_element_type=jnp.float32)
        gate_sigmoid = jax.nn.sigmoid(gate_act)
        hidden = (gate_act * gate_sigmoid * up_act).astype(jnp.bfloat16)
        gate_grad = (hidden_grad * up_act * gate_sigmoid * (1.0 + gate_act * (1.0 - gate_sigmoid))).astype(jnp.bfloat16)
        up_grad = (hidden_grad * gate_act * gate_sigmoid).astype(jnp.bfloat16)
        gate_blocks = gate_grad.astype(jnp.float32).reshape(TOK_GRP, N_TENSOR, width)
        up_blocks = up_grad.astype(jnp.float32).reshape(TOK_GRP, N_TENSOR, width)
        input_parts = jnp.einsum('tnf,dnf->ntd', gate_blocks, gate_cols) + jnp.einsum('tnf,dnf->ntd', up_blocks, up_cols)
        rounded_parts = lax.optimization_barrier(input_parts.astype(jnp.bfloat16))
        input_grad = lax.optimization_barrier(jnp.sum(rounded_parts.astype(jnp.float32), axis=0)).astype(jnp.bfloat16)
        gate_part = (jnp.dot(tok_rows.T, gate_grad, preferred_element_type=jnp.float32) * grad_scale).astype(jnp.bfloat16)
        up_part = (jnp.dot(tok_rows.T, up_grad, preferred_element_type=jnp.float32) * grad_scale).astype(jnp.bfloat16)
        down_part = (jnp.dot(hidden.T, grad_rows, preferred_element_type=jnp.float32) * grad_scale).astype(jnp.bfloat16)
        gate_part, up_part, down_part = lax.optimization_barrier((gate_part, up_part, down_part))
        carry = (carry[0] + gate_part.astype(jnp.float32), carry[1] + up_part.astype(jnp.float32), carry[2] + down_part.astype(jnp.float32))
        return (carry, input_grad)
    initial = (jnp.zeros((D, FF), jnp.float32), jnp.zeros((D, FF), jnp.float32), jnp.zeros((FF, D), jnp.float32))
    sums, input_grads = lax.scan(group_step, initial, (to_groups(tokens), to_groups(out_grad)))
    grad_tokens = input_grads.reshape(N_DW, N_TENSOR, tok_dev, D).transpose(1, 0, 2, 3).reshape(TOKENS, D)
    return (grad_tokens, sums[0].astype(jnp.bfloat16), sums[1].astype(jnp.bfloat16), sums[2].astype(jnp.bfloat16))
```

```python
import math

import jax
import jax.numpy as jnp
from jax import lax
from jax.experimental import pallas as pl
from jax.experimental.pallas import tpu as pltpu
from jax.sharding import PartitionSpec as P

NXL, NZ, NXH, NY, NCORE = 2, 8, 2, 4, 2
BF16, F32 = jnp.bfloat16, jnp.float32
VMEM_LIMIT = 56 * 1024 * 1024

ORDER = ((1, 1), (1, 2), (0, 2), (1, 3), (0, 3), (0, 1), (1, 0), (0, 0))
CHUNKS = ((0, 1, 7, 2), (6, 3, 5, 4))


def move_tensor(x, dest):
    perm = []
    for xl in range(NXL):
        for z in range(NZ):
            a, b = dest(xl, z)
            perm.append((xl * NZ + z, a % NXL * NZ + b % NZ))
    return lax.ppermute(x, "tensor", perm)


def move_dw(x, dest):
    perm = []
    for xh in range(NXH):
        for y in range(NY):
            for c in range(NCORE):
                a, b, e = dest(xh, y, c)
                perm.append(
                    ((xh * NY + y) * NCORE + c, (a % NXH * NY + b % NY) * NCORE + e % NCORE)
                )
    return lax.ppermute(x, "dw", perm)


def z_up(x):
    return move_tensor(x, lambda xl, z: (xl, z + 1))


def z_down(x):
    return move_tensor(x, lambda xl, z: (xl, z - 1))


def swap_xl(x):
    return move_tensor(x, lambda xl, z: (xl + 1, z))


def y_up(x):
    return move_dw(x, lambda xh, y, c: (xh, y + 1, c))


def y_down(x):
    return move_dw(x, lambda xh, y, c: (xh, y - 1, c))


def swap_xh(x):
    return move_dw(x, lambda xh, y, c: (xh + 1, y, c))


def swap_core(x):
    return move_dw(x, lambda xh, y, c: (xh, y, c + 1))


def vmem():
    return pl.BlockSpec(memory_space=pltpu.VMEM)


def hbm():
    return pl.BlockSpec(memory_space=pl.ANY)


def call(kernel, outs, ins, out_specs, in_specs, scratch=(), flops=0, moved=0, name=None):
    return pl.pallas_call(
        kernel,
        out_shape=outs,
        in_specs=in_specs,
        out_specs=out_specs,
        scratch_shapes=list(scratch),
        compiler_params=pltpu.CompilerParams(vmem_limit_bytes=VMEM_LIMIT),
        cost_estimate=pl.CostEstimate(
            flops=int(flops), bytes_accessed=int(moved), transcendentals=0
        ),
        name=name,
    )(*ins)


def prep_tokens(table, tokens, out_grad):
    rows, width = tokens.shape
    half = width // NCORE
    block = half // len(ORDER)

    def kernel(table_ref, tok_ref, grad_ref, own_ref, other_ref):
        for j in range(len(ORDER)):
            cols = slice(j * block, (j + 1) * block)
            for k, out in enumerate((own_ref, other_ref)):
                at = pl.multiple_of(table_ref[k * len(ORDER) + j] * block, block)
                out[0, :, cols] = tok_ref[:, pl.ds(at, block)]
                out[1, :, cols] = grad_ref[:, pl.ds(at, block)]

    shape = jax.ShapeDtypeStruct((2, rows, half), BF16)
    return call(
        kernel, (shape, shape), (table, tokens, out_grad), (vmem(), vmem()),
        [pl.BlockSpec(memory_space=pltpu.SMEM), vmem(), vmem()],
        moved=8 * rows * width, name="prep_tokens",
    )


def prep_weights(gate, up, down):
    depth, width = gate.shape

    def kernel(gate_ref, up_ref, down_ref, out_ref):
        out_ref[:, :width] = gate_ref[...]
        out_ref[:, width : 2 * width] = up_ref[...]
        out_ref[:, 2 * width :] = down_ref[...].T

    return call(
        kernel, jax.ShapeDtypeStruct((depth, 3 * width), BF16), (gate, up, down), vmem(),
        [vmem()] * 3, moved=12 * depth * width, name="prep_weights",
    )


def start_all(copies):
    for c in copies:
        c.start()


def wait_all(copies):
    for c in copies:
        c.wait()


def forward(shards, weights):
    n_t, n_w = len(shards), len(weights)
    _, rows, half = shards[0].shape
    depth, width3 = weights[0].shape
    width2 = width3 // 3 * 2
    total = n_t * rows
    parts = 2
    per = n_w // parts

    def kernel(*refs):
        t_in, w_in = refs[:n_t], refs[n_t : n_t + n_w]
        out_ref, rows_ref, tbuf, wbuf, acc, tsem, wsem, osem = refs[n_t + n_w :]
        t_copies = [
            pltpu.make_async_copy(r, tbuf.at[:, pl.ds(i * rows, rows)], tsem.at[i])
            for i, r in enumerate(t_in)
        ]
        w_copies = [
            pltpu.make_async_copy(r, wbuf.at[pl.ds(j * depth, depth)], wsem.at[j])
            for j, r in enumerate(w_in)
        ]
        start_all(t_copies + w_copies)
        wait_all(t_copies)
        keep = pltpu.make_async_copy(tbuf, rows_ref, osem)
        keep.start()
        for p in range(parts):
            wait_all(w_copies[p * per : (p + 1) * per])
            ks = slice(p * per * depth, (p + 1) * per * depth)
            for k, cols in enumerate((slice(0, width2), slice(width2, width3))):
                term = jnp.dot(tbuf[k, :, ks], wbuf[ks, cols], preferred_element_type=F32)
                if p > 0:
                    term = term + acc[:, cols]
                if p < parts - 1:
                    acc[:, cols] = term
                else:
                    out_ref[:, cols] = term.astype(BF16)
        keep.wait()

    return call(
        kernel,
        (jax.ShapeDtypeStruct((total, width3), BF16), jax.ShapeDtypeStruct((2, total, half), BF16)),
        (*shards, *weights), (vmem(), hbm()), [hbm()] * (n_t + n_w),
        scratch=(
            pltpu.VMEM((2, total, half), BF16),
            pltpu.VMEM((half, width3), BF16),
            pltpu.VMEM((total, width3), F32),
            pltpu.SemaphoreType.DMA((n_t,)),
            pltpu.SemaphoreType.DMA((n_w,)),
            pltpu.SemaphoreType.DMA,
        ),
        flops=2 * total * half * width3,
        moved=2 * (4 * total * half + half * width3 + total * width3),
        name="forward",
    )


def backward(mine, other, weights, pieces, scale, prev=(), chunks=(), count=0):
    n_w, n_p, n_c = len(weights), len(prev), len(chunks)
    rows, width3 = mine.shape
    width = width3 // 3
    depth = weights[0].shape[0]
    half = n_w * depth
    per = rows // pieces
    total = rows * (n_p + 1)
    step = 16
    halves = 2

    def kernel(*refs):
        refs = list(refs)

        def take(n):
            got = refs[:n]
            del refs[:n]
            return got

        parts, w_in, prev_in, t_in = take(2), take(n_w), take(n_p), take(n_c)
        (acts_ref,), terms, grads = take(1), take(pieces), take(count)
        pbuf, abuf, wbuf, qbuf, tbuf, gbuf, psem, wsem, tsem, osem = refs
        here = n_p * rows
        p_copies = [pltpu.make_async_copy(r, pbuf.at[k], psem.at[k]) for k, r in enumerate(parts)]
        t_copies = [
            pltpu.make_async_copy(r, abuf.at[pl.ds(i * rows, rows)], tsem.at[i])
            for i, r in enumerate(prev_in)
        ] + [
            pltpu.make_async_copy(
                r.at[:, :, pl.ds(0, count * depth)], tbuf.at[:, pl.ds(i * rows, rows)], tsem.at[n_p + i]
            )
            for i, r in enumerate(t_in)
        ]
        w_copies = [
            pltpu.make_async_copy(
                r.at[:, pl.ds(0, 2 * width)], wbuf.at[pl.ds(j * depth, depth)], wsem.at[j]
            )
            for j, r in enumerate(w_in)
        ]
        start_all(p_copies + t_copies + w_copies)
        wait_all(p_copies)

        def one(i, _):
            src = pl.ds(pl.multiple_of(i * step, step), step)
            dst = pl.ds(pl.multiple_of(here + i * step, step), step)
            gate, up, grad = (
                pbuf[0, src, k * width : (k + 1) * width].astype(F32)
                + pbuf[1, src, k * width : (k + 1) * width].astype(F32)
                for k in range(3)
            )
            s = 0.5 + 0.5 * jnp.tanh(0.5 * gate)
            act = gate * s
            abuf[dst, 2 * width :] = (act * up).astype(BF16)
            abuf[dst, :width] = (grad * up * s * (1.0 + gate * (1.0 - s))).astype(BF16)
            abuf[dst, width : 2 * width] = (grad * act).astype(BF16)
            return 0

        lax.fori_loop(0, rows // step, one, 0)
        out = [pltpu.make_async_copy(abuf.at[pl.ds(here, rows)], acts_ref, osem.at[0])]
        out[0].start()
        if count:
            wait_all(t_copies)
            weight_terms(abuf, tbuf, gbuf, grads, osem, 1, 0, count, scale, out)
        cols = half // halves
        for h in range(halves):
            wait_all(w_copies[h * n_w // halves : (h + 1) * n_w // halves])
            for n in range(h * cols, (h + 1) * cols, depth):
                qbuf[:, n : n + depth] = lax.dot_general(
                    abuf[here : here + rows, : 2 * width], wbuf[n : n + depth, :],
                    (((1,), (1,)), ((), ())), preferred_element_type=F32,
                ).astype(BF16)
            for k, r in enumerate(terms):
                c = pltpu.make_async_copy(
                    qbuf.at[pl.ds(k * per, per), pl.ds(h * cols, cols)],
                    r.at[:, pl.ds(h * cols, cols)],
                    osem.at[1 + count + h * pieces + k],
                )
                c.start()
                out.append(c)
        wait_all(out)

    shapes = (
        [jax.ShapeDtypeStruct((rows, width3), BF16)]
        + [jax.ShapeDtypeStruct((per, half), BF16)] * pieces
        + [jax.ShapeDtypeStruct((depth, width3), BF16)] * count
    )
    got = call(
        kernel, shapes, (mine, other, *weights, *prev, *chunks), [hbm()] * len(shapes),
        [hbm()] * (2 + n_w + n_p + n_c),
        scratch=(
            pltpu.VMEM((2, rows, width3), BF16),
            pltpu.VMEM((total, width3), BF16),
            pltpu.VMEM((half, 2 * width), BF16),
            pltpu.VMEM((rows, half), BF16),
            pltpu.VMEM((2, total, max(count, 1) * depth), BF16),
            pltpu.VMEM((max(count, 1), depth, width3), BF16),
            pltpu.SemaphoreType.DMA((2,)),
            pltpu.SemaphoreType.DMA((n_w,)),
            pltpu.SemaphoreType.DMA((max(n_p + n_c, 1),)),
            pltpu.SemaphoreType.DMA((1 + count + halves * pieces,)),
        ),
        flops=4 * rows * half * width + 2 * total * count * depth * width3,
        moved=2 * (3 * rows * width3 + 2 * half * width + rows * half),
        name="backward",
    )
    return got[0], got[1 : 1 + pieces], got[1 + pieces :]


def weight_terms(abuf, tbuf, gbuf, grads, osem, sem, first, count, scale, out):
    depth, width3 = gbuf.shape[1:]
    width2 = width3 // 3 * 2
    dims = (((0,), (0,)), ((), ()))
    for j in range(first, first + count):
        cols = slice(j * depth, (j + 1) * depth)
        for k, w in enumerate((slice(0, width2), slice(width2, width3))):
            got = lax.dot_general(tbuf[k, :, cols], abuf[:, w], dims, preferred_element_type=F32)
            gbuf[j, :, w] = (got * scale).astype(BF16)
        c = pltpu.make_async_copy(gbuf.at[j], grads[j], osem.at[sem + j])
        c.start()
        out.append(c)


def weight_grads(acts, chunks, first, count, scale):
    n_a = len(acts)
    rows, width3 = acts[0].shape
    half = chunks[0].shape[2]
    depth = half // len(ORDER)
    group = 2
    groups = count // group
    total = n_a * rows

    def kernel(*refs):
        a_in, t_in, grads = refs[:n_a], refs[n_a : 2 * n_a], refs[2 * n_a : 2 * n_a + count]
        abuf, tbuf, gbuf, asem, tsem, osem = refs[2 * n_a + count :]
        a_copies = [
            pltpu.make_async_copy(r, abuf.at[pl.ds(i * rows, rows)], asem.at[i])
            for i, r in enumerate(a_in)
        ]
        t_copies = [
            [
                pltpu.make_async_copy(
                    r.at[:, :, pl.ds((first + g * group) * depth, group * depth)],
                    tbuf.at[:, pl.ds(i * rows, rows), pl.ds(g * group * depth, group * depth)],
                    tsem.at[g * n_a + i],
                )
                for i, r in enumerate(t_in)
            ]
            for g in range(groups)
        ]
        start_all(a_copies)
        for g in t_copies:
            start_all(g)
        wait_all(a_copies)
        out = []
        for g in range(groups):
            wait_all(t_copies[g])
            weight_terms(abuf, tbuf, gbuf, grads, osem, 0, g * group, group, scale, out)
        wait_all(out)

    shape = jax.ShapeDtypeStruct((depth, width3), BF16)
    return call(
        kernel, (shape,) * count, (*acts, *chunks), (hbm(),) * count, [hbm()] * (2 * n_a),
        scratch=(
            pltpu.VMEM((total, width3), BF16),
            pltpu.VMEM((2, total, count * depth), BF16),
            pltpu.VMEM((count, depth, width3), BF16),
            pltpu.SemaphoreType.DMA((n_a,)),
            pltpu.SemaphoreType.DMA((groups * n_a,)),
            pltpu.SemaphoreType.DMA((count,)),
        ),
        flops=2 * total * count * depth * width3,
        moved=2 * (total * width3 + 2 * total * count * depth + count * depth * width3),
        name="weight_grads",
    )


def tie(*arrays):
    return lax.optimization_barrier(arrays)


def add(*terms):
    total = terms[0].astype(F32)
    for t in terms[1:]:
        total = total + t.astype(F32)
    return total.astype(BF16)


def finish_weights(own, from_below, from_above, from_xh):
    depth, width3 = own.shape
    width = width3 // 3

    def kernel(a_ref, b_ref, c_ref, d_ref, gate_ref, up_ref, down_ref):
        def total(k):
            cols = slice(k * width, (k + 1) * width)
            return sum(r[:, cols].astype(F32) for r in (a_ref, b_ref, c_ref, d_ref)).astype(BF16)

        gate_ref[...] = total(0)
        up_ref[...] = total(1)
        down_ref[...] = total(2).T

    shapes = [jax.ShapeDtypeStruct(s, BF16) for s in ((depth, width), (depth, width), (width, depth))]
    return call(
        kernel, shapes, (own, from_below, from_above, from_xh), [vmem()] * 3, [vmem()] * 4,
        moved=30 * depth * width, name="finish_weights",
    )


def finish_tokens(table, own, other):
    rows, half = own.shape
    block = half // len(ORDER)

    def kernel(table_ref, own_ref, other_ref, out_ref):
        for j in range(len(ORDER)):
            cols = slice(j * block, (j + 1) * block)
            for k, r in enumerate((own_ref, other_ref)):
                at = pl.multiple_of(table_ref[k * len(ORDER) + j] * block, block)
                out_ref[:, pl.ds(at, block)] = r[:, cols]

    return call(
        kernel, jax.ShapeDtypeStruct((rows, NCORE * half), BF16), (table, own, other), vmem(),
        [pl.BlockSpec(memory_space=pltpu.SMEM), vmem(), vmem()],
        moved=8 * rows * half, name="finish_tokens",
    )


def body(tokens, out_grad, gate_weight, up_weight, down_weight):
    rows = tokens.shape[0]
    scale = 1.0 / math.sqrt(rows * lax.axis_size("tensor") * lax.axis_size("dw"))
    dw = lax.axis_index("dw")
    core, y, xh = dw % NCORE, dw // NCORE % NY, dw // (NCORE * NY)
    table = jnp.stack(
        [
            (((xh + dx) % NXH) * NY + (y + dy) % NY) * NCORE + c
            for c in (core, 1 - core)
            for dx, dy in ORDER
        ]
    ).astype(jnp.int32)

    own_part, other_part = prep_tokens(table, tokens, out_grad)
    got = swap_core(other_part)
    low = jnp.where(core == 0, own_part, got)
    high = jnp.where(core == 0, got, own_part)
    a = {0: jnp.concatenate([low, high], axis=1)}
    w = {(0, 0): prep_weights(gate_weight, up_weight, down_weight)}

    a[1], a[7] = z_down(a[0]), z_up(a[0])
    b = {0: swap_xl(a[0])}
    w[1, 0], w[0, 1], w[0, 3] = swap_xh(w[0, 0]), y_down(w[0, 0]), y_up(w[0, 0])
    t1, t7 = tie(a[1], a[7])
    a[2], a[6] = z_down(t1), z_up(t7)
    b0, t1, t7 = tie(b[0], t1, t7)
    b[1], b[7] = z_down(b0), z_up(b0)
    t2, t6, b0 = tie(a[2], a[6], b0)
    a[3], a[5] = z_down(t2), z_up(t6)
    s1, s7, t2, t6 = tie(b[1], b[7], t2, t6)
    b[2], b[6] = z_down(s1), z_up(s7)
    w10, w01, w03, s1, s7 = tie(w[1, 0], w[0, 1], w[0, 3], s1, s7)
    w[1, 1], w[1, 3], w[0, 2] = swap_xh(w01), y_up(w10), y_down(w01)
    t3, t5, w10, w01 = tie(a[3], a[5], w10, w01)
    a[4] = z_down(t3)
    s2, s6, t3, t5 = tie(b[2], b[6], t3, t5)
    b[3], b[5] = z_down(s2), z_up(s6)
    w13, s2, s6 = tie(w[1, 3], s2, s6)
    w[1, 2] = y_up(w13)
    s5, w13, _ = tie(b[5], w13, a[4])
    b[4] = z_up(s5)
    weights = [w[k] for k in ORDER]

    early, late = ([s[dz] for dz in chunk for s in (a, b)] for chunk in CHUNKS)
    part1, rows1 = forward(early, weights)
    other1 = swap_core(part1)
    part2, rows2 = forward(late, weights)
    other2 = swap_core(part2)
    acts1, terms1, _ = backward(part1, other1, weights, len(CHUNKS[0]), scale)
    acts2, terms2, first = backward(
        part2, other2, weights, len(CHUNKS[1]), scale, prev=(acts1,), chunks=(rows1, rows2), count=2
    )
    terms = dict(zip(CHUNKS[0] + CHUNKS[1], [*terms1, *terms2], strict=True))

    rest = weight_grads((acts1, acts2), (rows1, rows2), 2, len(ORDER) - 2, scale)
    p = dict(zip(ORDER, [*first, *rest], strict=True))
    r11 = y_up(p[1, 1])
    r12 = y_down(p[1, 2])
    r13 = y_down(add(p[1, 3], r12))
    p02, _ = tie(p[0, 2], r11)
    r02 = y_up(p02)
    p03, _ = tie(p[0, 3], r13)
    r03 = y_down(p03)
    r01 = y_up(add(p[0, 1], r02))
    from_xh = swap_xh(add(p[1, 0], r11, r13))
    grads = finish_weights(p[0, 0], r01, r03, from_xh)

    n = 2 * rows
    up = z_up(terms[4][:n])
    down = z_down(terms[4][n:])
    up = z_up(terms[3].at[:n].set(add(terms[3][:n], up)))
    down = z_down(terms[5].at[n:].set(add(terms[5][n:], down)))
    up = z_up(add(terms[2], up))
    down = z_down(add(terms[6], down))
    up = z_up(add(terms[1], up))
    down = z_down(add(terms[7], down))
    from_xl = swap_xl(add(terms[0][n:], up[n:], down[n:]))
    total = add(terms[0][:n], up[:n], down[:n], from_xl)
    mine = lax.dynamic_slice_in_dim(total, core * rows, rows)
    theirs = lax.dynamic_slice_in_dim(total, (1 - core) * rows, rows)
    grad_tokens = finish_tokens(table, mine, swap_core(theirs))
    return (grad_tokens, *grads)


def solution(mesh):
    placed = (
        P(("tensor", "dw"), None),
        P(("tensor", "dw"), None),
        P("dw", "tensor"),
        P("dw", "tensor"),
        P("tensor", "dw"),
    )
    return jax.shard_map(
        body,
        mesh=mesh,
        in_specs=placed,
        out_specs=(
            P(("tensor", "dw"), None),
            P("dw", "tensor"),
            P("dw", "tensor"),
            P("tensor", "dw"),
        ),
        check_vma=False,
    )
```

```python
import math

import jax
import jax.numpy as jnp
from jax import lax
from jax.experimental import pallas as pl
from jax.experimental.pallas import tpu as pltpu
from jax.sharding import PartitionSpec as P

NXL, NZ, NXH, NY, NCORE = 2, 8, 2, 4, 2
BF16, F32 = jnp.bfloat16, jnp.float32
VMEM_LIMIT = 26 * 1024 * 1024

ORDER = ((1, 1), (1, 2), (0, 2), (1, 3), (0, 3), (0, 1), (1, 0), (0, 0))
CHUNKS = ((0, 1, 7, 2, 6), (3, 5, 4))


def move_tensor(x, dest):
    perm = []
    for xl in range(NXL):
        for z in range(NZ):
            a, b = dest(xl, z)
            perm.append((xl * NZ + z, a % NXL * NZ + b % NZ))
    return lax.ppermute(x, "tensor", perm)


def move_dw(x, dest):
    perm = []
    for xh in range(NXH):
        for y in range(NY):
            for c in range(NCORE):
                a, b, e = dest(xh, y, c)
                perm.append(
                    ((xh * NY + y) * NCORE + c, (a % NXH * NY + b % NY) * NCORE + e % NCORE)
                )
    return lax.ppermute(x, "dw", perm)


def z_up(x):
    return move_tensor(x, lambda xl, z: (xl, z + 1))


def z_down(x):
    return move_tensor(x, lambda xl, z: (xl, z - 1))


def swap_xl(x):
    return move_tensor(x, lambda xl, z: (xl + 1, z))


def y_up(x):
    return move_dw(x, lambda xh, y, c: (xh, y + 1, c))


def y_down(x):
    return move_dw(x, lambda xh, y, c: (xh, y - 1, c))


def swap_xh(x):
    return move_dw(x, lambda xh, y, c: (xh + 1, y, c))


def swap_core(x):
    return move_dw(x, lambda xh, y, c: (xh, y, c + 1))


def vmem():
    return pl.BlockSpec(memory_space=pltpu.VMEM)


def hbm():
    return pl.BlockSpec(memory_space=pl.ANY)


def call(kernel, outs, ins, out_specs, in_specs, scratch=(), flops=0, moved=0, name=None):
    return pl.pallas_call(
        kernel,
        out_shape=outs,
        in_specs=in_specs,
        out_specs=out_specs,
        scratch_shapes=list(scratch),
        compiler_params=pltpu.CompilerParams(vmem_limit_bytes=VMEM_LIMIT),
        cost_estimate=pl.CostEstimate(flops=0, bytes_accessed=1024, transcendentals=0),
        name=name,
    )(*ins)


def prep_tokens(table, tokens, out_grad):
    rows, width = tokens.shape
    half = width // NCORE
    block = half // len(ORDER)

    def kernel(table_ref, tok_ref, grad_ref, own_ref, other_ref):
        for j in range(len(ORDER)):
            cols = slice(j * block, (j + 1) * block)
            for k, out in enumerate((own_ref, other_ref)):
                at = pl.multiple_of(table_ref[k * len(ORDER) + j] * block, block)
                out[0, :, cols] = tok_ref[:, pl.ds(at, block)]
                out[1, :, cols] = grad_ref[:, pl.ds(at, block)]

    shape = jax.ShapeDtypeStruct((2, rows, half), BF16)
    return call(
        kernel, (shape, shape), (table, tokens, out_grad), (vmem(), vmem()),
        [pl.BlockSpec(memory_space=pltpu.SMEM), vmem(), vmem()],
        moved=8 * rows * width, name="prep_tokens",
    )


def prep_weights(gate, up, down):
    depth, width = gate.shape

    def kernel(gate_ref, up_ref, down_ref, out_ref):
        out_ref[:, :width] = gate_ref[...]
        out_ref[:, width : 2 * width] = up_ref[...]
        out_ref[:, 2 * width :] = down_ref[...].T

    return call(
        kernel, jax.ShapeDtypeStruct((depth, 3 * width), BF16), (gate, up, down), vmem(),
        [vmem()] * 3, moved=12 * depth * width, name="prep_weights",
    )


def start_all(copies):
    for c in copies:
        c.start()


def wait_all(copies):
    for c in copies:
        c.wait()


def forward(pieces, rows, weights, splits):
    shards = [x for x, _ in pieces]
    n_t, n_w = len(pieces), len(weights)
    half = shards[0].shape[2]
    depth, width3 = weights[0].shape
    width, width2 = width3 // 3, width3 // 3 * 2
    total = n_t * rows
    each = total // splits
    parts = 2
    per = n_w // parts

    def kernel(*refs):
        t_in, w_in = refs[:n_t], refs[n_t : n_t + n_w]
        outs, (rows_ref, tbuf, wbuf, acc, tsem, wsem, osem) = refs[n_t + n_w :][: 3 * splits], refs[n_t + n_w + 3 * splits :]
        t_copies = [
            pltpu.make_async_copy(
                r.at[:, pl.ds(pieces[i][1], rows)], tbuf.at[:, pl.ds(i * rows, rows)], tsem.at[i]
            )
            for i, r in enumerate(t_in)
        ]
        w_copies = [
            pltpu.make_async_copy(r, wbuf.at[pl.ds(j * depth, depth)], wsem.at[j])
            for j, r in enumerate(w_in)
        ]
        start_all(t_copies + w_copies)
        wait_all(t_copies)
        keep = pltpu.make_async_copy(tbuf, rows_ref, osem)
        keep.start()
        for p in range(parts):
            wait_all(w_copies[p * per : (p + 1) * per])
            ks = slice(p * per * depth, (p + 1) * per * depth)
            for k, cols in enumerate((slice(0, width2), slice(width2, width3))):
                term = jnp.dot(tbuf[k, :, ks], wbuf[ks, cols], preferred_element_type=F32)
                if p > 0:
                    term = term + acc[:, cols]
                if p < parts - 1:
                    acc[:, cols] = term
                else:
                    for i in range(term.shape[1] // width):
                        part = term[:, i * width : (i + 1) * width].astype(BF16)
                        for h in range(splits):
                            outs[3 * h + 2 * k + i][...] = part[h * each : (h + 1) * each]
        keep.wait()

    *partial, chunk = call(
        kernel,
        (jax.ShapeDtypeStruct((each, width), BF16),) * (3 * splits)
        + (jax.ShapeDtypeStruct((2, total, half), BF16),),
        (*shards, *weights), (vmem(),) * (3 * splits) + (hbm(),), [hbm()] * (n_t + n_w),
        scratch=(
            pltpu.VMEM((2, total, half), BF16),
            pltpu.VMEM((half, width3), BF16),
            pltpu.VMEM((total, width3), F32),
            pltpu.SemaphoreType.DMA((n_t,)),
            pltpu.SemaphoreType.DMA((n_w,)),
            pltpu.SemaphoreType.DMA,
        ),
        flops=2 * total * half * width3,
        moved=2 * (4 * total * half + half * width3 + total * width3),
        name="forward",
    )
    return partial, chunk


def activate(a, b, src, out, dst, step):
    width = a[0].shape[1]
    gate, up, grad = (p[src, :].astype(F32) + q[src, :].astype(F32) for p, q in zip(a, b, strict=True))
    s = 0.5 + 0.5 * jnp.tanh(0.5 * gate)
    act = gate * s
    out[dst, 2 * width :] = (act * up).astype(BF16)
    out[dst, :width] = (grad * up * s * (1.0 + gate * (1.0 - s))).astype(BF16)
    out[dst, width : 2 * width] = (grad * act).astype(BF16)


def activations(mine, other):
    rows, width = mine[0].shape
    count = len(mine)
    splits = count // 3
    step = 16

    def kernel(*refs):
        a, b, out_ref = refs[:count], refs[count : 2 * count], refs[2 * count]
        for h in range(splits):

            def one(i, _, h=h):
                src = pl.ds(pl.multiple_of(i * step, step), step)
                dst = pl.ds(pl.multiple_of(h * rows + i * step, step), step)
                activate(a[3 * h : 3 * h + 3], b[3 * h : 3 * h + 3], src, out_ref, dst, step)
                return 0

            lax.fori_loop(0, rows // step, one, 0)

    return call(
        kernel, jax.ShapeDtypeStruct((splits * rows, 3 * width), BF16), (*mine, *other), vmem(),
        [vmem()] * (2 * count), flops=30 * splits * rows * width, moved=18 * splits * rows * width,
        name="activations",
    )


def term_columns(acts, wbuf, qbuf, terms, osem, h, cols, depth, per, out, sem=0):
    for n in range(h * cols, (h + 1) * cols, depth):
        qbuf[:, n : n + depth] = lax.dot_general(
            acts[...], wbuf[n : n + depth, :], (((1,), (1,)), ((), ())), preferred_element_type=F32
        ).astype(BF16)
    for k, r in enumerate(terms):
        c = pltpu.make_async_copy(
            qbuf.at[pl.ds(k * per, per), pl.ds(h * cols, cols)],
            r.at[:, pl.ds(h * cols, cols)],
            osem.at[sem + h * len(terms) + k],
        )
        c.start()
        out.append(c)


def backward(mine, other, weights, pieces, scale, prev=(), chunks=(), count=0):
    n_w, n_p, n_c = len(weights), len(prev), len(chunks)
    rows, width = mine[0].shape
    width3 = 3 * width
    depth = weights[0].shape[0]
    half = n_w * depth
    per = rows // pieces
    prev_rows = [r.shape[0] for r in prev]
    starts = [sum(prev_rows[:i]) for i in range(n_p + 1)]
    total = starts[-1] + rows
    step = 16
    halves = 2

    def kernel(*refs):
        refs = list(refs)

        def take(n):
            got = refs[:n]
            del refs[:n]
            return got

        parts, w_in, prev_in, t_in = take(6), take(n_w), take(n_p), take(n_c)
        (acts_ref,), terms, grads = take(1), take(pieces), take(count)
        pbuf, abuf, wbuf, qbuf, tbuf, gbuf, psem, wsem, tsem, osem = refs
        here = starts[-1]
        bufs = [pbuf.at[k] for k in range(6)]
        p_copies = [pltpu.make_async_copy(r, pbuf.at[k], psem.at[k]) for k, r in enumerate(parts)]
        t_copies = [
            pltpu.make_async_copy(r, abuf.at[pl.ds(starts[i], prev_rows[i])], tsem.at[i])
            for i, r in enumerate(prev_in)
        ] + [
            pltpu.make_async_copy(
                r.at[:, :, pl.ds(0, count * depth)],
                tbuf.at[:, pl.ds(starts[i], r.shape[1])],
                tsem.at[n_p + i],
            )
            for i, r in enumerate(t_in)
        ]
        w_copies = [
            pltpu.make_async_copy(
                r.at[:, pl.ds(0, 2 * width)], wbuf.at[pl.ds(j * depth, depth)], wsem.at[j]
            )
            for j, r in enumerate(w_in)
        ]
        start_all(p_copies + t_copies + w_copies)
        wait_all(p_copies)

        def one(i, _):
            src = pl.ds(pl.multiple_of(i * step, step), step)
            dst = pl.ds(pl.multiple_of(here + i * step, step), step)
            activate(bufs[:3], bufs[3:], src, abuf, dst, step)
            return 0

        lax.fori_loop(0, rows // step, one, 0)
        out = [pltpu.make_async_copy(abuf.at[pl.ds(here, rows)], acts_ref, osem.at[0])]
        out[0].start()
        if count:
            wait_all(t_copies)
            weight_terms(abuf, tbuf, gbuf, grads, osem, 1, 0, count, scale, out)
        cols = half // halves
        for h in range(halves):
            wait_all(w_copies[h * n_w // halves : (h + 1) * n_w // halves])
            term_columns(
                abuf.at[pl.ds(here, rows), pl.ds(0, 2 * width)],
                wbuf, qbuf, terms, osem, h, cols, depth, per, out, 1 + count,
            )
        wait_all(out)

    shapes = (
        [jax.ShapeDtypeStruct((rows, width3), BF16)]
        + [jax.ShapeDtypeStruct((per, half), BF16)] * pieces
        + [jax.ShapeDtypeStruct((depth, width3), BF16)] * count
    )
    got = call(
        kernel, shapes, (*mine, *other, *weights, *prev, *chunks), [hbm()] * len(shapes),
        [hbm()] * (6 + n_w + n_p + n_c),
        scratch=(
            pltpu.VMEM((6, rows, width), BF16),
            pltpu.VMEM((total, width3), BF16),
            pltpu.VMEM((half, 2 * width), BF16),
            pltpu.VMEM((rows, half), BF16),
            pltpu.VMEM((2, total, max(count, 1) * depth), BF16),
            pltpu.VMEM((max(count, 1), depth, width3), BF16),
            pltpu.SemaphoreType.DMA((6,)),
            pltpu.SemaphoreType.DMA((n_w,)),
            pltpu.SemaphoreType.DMA((max(n_p + n_c, 1),)),
            pltpu.SemaphoreType.DMA((1 + count + halves * pieces,)),
        ),
        flops=4 * rows * half * width + 2 * total * count * depth * width3,
        moved=2 * (3 * rows * width3 + 2 * half * width + rows * half),
        name="backward",
    )
    return got[0], got[1 : 1 + pieces], got[1 + pieces :]


def weight_terms(abuf, tbuf, gbuf, grads, osem, sem, first, count, scale, out):
    depth, width3 = gbuf.shape[1:]
    width2 = width3 // 3 * 2
    dims = (((0,), (0,)), ((), ()))
    for j in range(first, first + count):
        cols = slice(j * depth, (j + 1) * depth)
        for k, w in enumerate((slice(0, width2), slice(width2, width3))):
            got = lax.dot_general(tbuf[k, :, cols], abuf[:, w], dims, preferred_element_type=F32)
            gbuf[j, :, w] = (got * scale).astype(BF16)
        c = pltpu.make_async_copy(gbuf.at[j], grads[j], osem.at[sem + j])
        c.start()
        out.append(c)


def weight_grads(acts, chunks, weights, pieces, first, count, scale):
    n_a, n_w = len(acts), len(weights)
    width3 = acts[0].shape[1]
    width2 = width3 // 3 * 2
    rows = [r.shape[0] for r in acts]
    starts = [sum(rows[:i]) for i in range(n_a)]
    half = chunks[0].shape[2]
    depth = half // len(ORDER)
    group = 2
    groups = count // group
    total = sum(rows)
    per = rows[0] // pieces

    def kernel(*refs):
        refs = list(refs)

        def take(n):
            got = refs[:n]
            del refs[:n]
            return got

        a_in, t_in, w_in, grads, terms = take(n_a), take(n_a), take(n_w), take(count), take(pieces)
        abuf, tbuf, gbuf, wbuf, qbuf, asem, tsem, wsem, osem = refs
        a_copies = [
            pltpu.make_async_copy(r, abuf.at[pl.ds(starts[i], rows[i])], asem.at[i])
            for i, r in enumerate(a_in)
        ]
        t_copies = [
            [
                pltpu.make_async_copy(
                    r.at[:, :, pl.ds((first + g * group) * depth, group * depth)],
                    tbuf.at[:, pl.ds(starts[i], rows[i]), pl.ds(g * group * depth, group * depth)],
                    tsem.at[g * n_a + i],
                )
                for i, r in enumerate(t_in)
            ]
            for g in range(groups)
        ]
        w_copies = [
            pltpu.make_async_copy(
                r.at[:, pl.ds(0, width2)], wbuf.at[pl.ds(j * depth, depth)], wsem.at[j]
            )
            for j, r in enumerate(w_in)
        ]
        start_all(a_copies)
        for g in t_copies:
            start_all(g)
        start_all(w_copies)
        wait_all(a_copies)
        out = []
        for g in range(groups):
            wait_all(t_copies[g])
            weight_terms(abuf, tbuf, gbuf, grads, osem, 0, g * group, group, scale, out)
        wait_all(w_copies)
        for h in range(2):
            term_columns(
                abuf.at[pl.ds(0, rows[0]), pl.ds(0, width2)],
                wbuf, qbuf, terms, osem, h, half // 2, depth, per, out, count,
            )
        wait_all(out)

    shapes = [jax.ShapeDtypeStruct((depth, width3), BF16)] * count + [
        jax.ShapeDtypeStruct((per, half), BF16)
    ] * pieces
    got = call(
        kernel, shapes, (*acts, *chunks, *weights), [hbm()] * len(shapes), [hbm()] * (2 * n_a + n_w),
        scratch=(
            pltpu.VMEM((total, width3), BF16),
            pltpu.VMEM((2, total, count * depth), BF16),
            pltpu.VMEM((count, depth, width3), BF16),
            pltpu.VMEM((half, width2), BF16),
            pltpu.VMEM((rows[0], half), BF16),
            pltpu.SemaphoreType.DMA((n_a,)),
            pltpu.SemaphoreType.DMA((groups * n_a,)),
            pltpu.SemaphoreType.DMA((n_w,)),
            pltpu.SemaphoreType.DMA((count + 2 * pieces,)),
        ),
        flops=2 * total * count * depth * width3 + 2 * rows[0] * half * width2,
        moved=2 * (total * width3 + 2 * total * count * depth + count * depth * width3),
        name="weight_grads",
    )
    return got[:count], got[count:]


def tie(*arrays):
    return lax.optimization_barrier(arrays)


def add(*terms):
    total = terms[0].astype(F32)
    for t in terms[1:]:
        total = total + t.astype(F32)
    return total.astype(BF16)


def finish_weights(own, from_below, from_above, from_xh):
    depth, width3 = own.shape
    width = width3 // 3

    def kernel(a_ref, b_ref, c_ref, d_ref, gate_ref, up_ref, down_ref):
        def total(k):
            cols = slice(k * width, (k + 1) * width)
            return sum(r[:, cols].astype(F32) for r in (a_ref, b_ref, c_ref, d_ref)).astype(BF16)

        gate_ref[...] = total(0)
        up_ref[...] = total(1)
        down_ref[...] = total(2).T

    shapes = [jax.ShapeDtypeStruct(s, BF16) for s in ((depth, width), (depth, width), (width, depth))]
    return call(
        kernel, shapes, (own, from_below, from_above, from_xh), [vmem()] * 3, [vmem()] * 4,
        moved=30 * depth * width, name="finish_weights",
    )


def finish_tokens(table, own, other):
    rows, half = own.shape
    block = half // len(ORDER)

    def kernel(table_ref, own_ref, other_ref, out_ref):
        for j in range(len(ORDER)):
            cols = slice(j * block, (j + 1) * block)
            for k, r in enumerate((own_ref, other_ref)):
                at = pl.multiple_of(table_ref[k * len(ORDER) + j] * block, block)
                out_ref[:, pl.ds(at, block)] = r[:, cols]

    return call(
        kernel, jax.ShapeDtypeStruct((rows, NCORE * half), BF16), (table, own, other), vmem(),
        [pl.BlockSpec(memory_space=pltpu.SMEM), vmem(), vmem()],
        moved=8 * rows * half, name="finish_tokens",
    )


def body(tokens, out_grad, gate_weight, up_weight, down_weight):
    rows = tokens.shape[0]
    scale = 1.0 / math.sqrt(rows * lax.axis_size("tensor") * lax.axis_size("dw"))
    dw = lax.axis_index("dw")
    core, y, xh = dw % NCORE, dw // NCORE % NY, dw // (NCORE * NY)
    table = jnp.stack(
        [
            (((xh + dx) % NXH) * NY + (y + dy) % NY) * NCORE + c
            for c in (core, 1 - core)
            for dx, dy in ORDER
        ]
    ).astype(jnp.int32)

    own_part, other_part = prep_tokens(table, tokens, out_grad)
    got = swap_core(other_part)
    low = jnp.where(core == 0, own_part, got)
    high = jnp.where(core == 0, got, own_part)
    a = {0: jnp.concatenate([low, high], axis=1)}
    w = {(0, 0): prep_weights(gate_weight, up_weight, down_weight)}

    n = NCORE * rows
    a[1], a[7] = z_down(a[0]), z_up(a[0])
    b = {0: swap_xl(a[0])}
    w[1, 0], w[0, 1], w[0, 3] = swap_xh(w[0, 0]), y_down(w[0, 0]), y_up(w[0, 0])
    a2b1 = z_down(jnp.concatenate([a[1], b[0]], axis=1))
    a6b7 = z_up(jnp.concatenate([a[7], b[0]], axis=1))
    w10, w01, w03, a2b1, a6b7 = tie(w[1, 0], w[0, 1], w[0, 3], a2b1, a6b7)
    w[1, 1], w[1, 3], w[0, 2] = swap_xh(w01), y_up(w10), y_down(w01)
    a3b2, a5b6 = z_down(a2b1), z_up(a6b7)
    w13, w11, w[0, 2], a3b2, a5b6 = tie(w[1, 3], w[1, 1], w[0, 2], a3b2, a5b6)
    w[1, 1], w[1, 3] = w11, w13
    k = w13.shape[0] // 2
    w[1, 2] = jnp.concatenate([y_up(w13[:k]), y_down(w11[k:])])
    a4b3, b[5] = z_down(a3b2), z_up(a5b6[:, n:])
    b[4] = move_tensor(a5b6[:, :n], lambda xl, z: (xl + 1, z + 1))
    weights = [w[k] for k in ORDER]

    early = [
        (a[0], 0), (b[0], 0), (a[1], 0), (a2b1, n), (a[7], 0), (a6b7, n), (a2b1, 0), (a3b2, n), (a6b7, 0), (a5b6, n)
    ]
    late = [(a3b2, 0), (a4b3, n), (a5b6, 0), (b[5], 0), (a4b3, 0), (b[4], 0)]
    part1, rows1 = forward(early, n, weights, 2)
    other1 = [swap_core(x) for x in part1]
    part2, rows2 = forward(late, n, weights, 1)
    other2 = [swap_core(x) for x in part2]
    acts1 = activations(part1, other1)
    acts2, terms2, first = backward(
        part2, other2, weights, len(CHUNKS[1]), scale, prev=(acts1,), chunks=(rows1, rows2), count=2
    )
    rest, terms1 = weight_grads(
        (acts1, acts2), (rows1, rows2), weights, len(CHUNKS[0]), 2, len(ORDER) - 2, scale
    )
    terms = dict(zip(CHUNKS[0] + CHUNKS[1], [*terms1, *terms2], strict=True))

    p = dict(zip(ORDER, [*first, *rest], strict=True))
    r11 = y_up(p[1, 1])
    r12 = y_down(p[1, 2])
    r13 = y_down(add(p[1, 3], r12))
    p02, _ = tie(p[0, 2], r11)
    r02 = y_up(p02)
    p03, _ = tie(p[0, 3], r13)
    r03 = y_down(p03)
    r01 = y_up(add(p[0, 1], r02))
    from_xh = swap_xh(add(p[1, 0], r11, r13))
    grads = finish_weights(p[0, 0], r01, r03, from_xh)

    up = z_up(terms[4][:n])
    down = z_down(terms[4][n:])
    up = z_up(terms[3].at[:n].set(add(terms[3][:n], up)))
    down = z_down(terms[5].at[n:].set(add(terms[5][n:], down)))
    up = z_up(add(terms[2], up))
    down = z_down(add(terms[6], down))
    up, down, _, _ = tie(add(terms[1], up), add(terms[7], down), r11, r12)
    up = z_up(up)
    down = z_down(down)
    from_xl = swap_xl(add(terms[0][n:], up[n:], down[n:]))
    total = add(terms[0][:n], up[:n], down[:n], from_xl)
    mine = lax.dynamic_slice_in_dim(total, core * rows, rows)
    theirs = lax.dynamic_slice_in_dim(total, (1 - core) * rows, rows)
    grad_tokens = finish_tokens(table, mine, swap_core(theirs))
    return (grad_tokens, *grads)


def solution(mesh):
    placed = (
        P(("tensor", "dw"), None),
        P(("tensor", "dw"), None),
        P("dw", "tensor"),
        P("dw", "tensor"),
        P("tensor", "dw"),
    )
    return jax.shard_map(
        body,
        mesh=mesh,
        in_specs=placed,
        out_specs=(
            P(("tensor", "dw"), None),
            P("dw", "tensor"),
            P("dw", "tensor"),
            P("tensor", "dw"),
        ),
        check_vma=False,
    )
```

```python
import math

import jax
import jax.numpy as jnp
from jax import lax
from jax.experimental import pallas as pl
from jax.experimental.pallas import tpu as pltpu
from jax.sharding import PartitionSpec as P

NXL, NZ, NXH, NY, NCORE = 2, 8, 2, 4, 2
BF16, F32 = jnp.bfloat16, jnp.float32
VMEM_LIMIT = 20 * 1024 * 1024

ORDER = ((1, 1), (1, 2), (0, 2), (1, 3), (0, 3), (0, 1), (1, 0), (0, 0))
CHUNKS = ((0, 1, 7, 2, 6), (3, 5, 4))


def move_tensor(x, dest):
    perm = []
    for xl in range(NXL):
        for z in range(NZ):
            a, b = dest(xl, z)
            perm.append((xl * NZ + z, a % NXL * NZ + b % NZ))
    return lax.ppermute(x, "tensor", perm)


def move_dw(x, dest):
    perm = []
    for xh in range(NXH):
        for y in range(NY):
            for c in range(NCORE):
                a, b, e = dest(xh, y, c)
                perm.append(
                    ((xh * NY + y) * NCORE + c, (a % NXH * NY + b % NY) * NCORE + e % NCORE)
                )
    return lax.ppermute(x, "dw", perm)


def z_up(x):
    return move_tensor(x, lambda xl, z: (xl, z + 1))


def z_down(x):
    return move_tensor(x, lambda xl, z: (xl, z - 1))


def swap_xl(x):
    return move_tensor(x, lambda xl, z: (xl + 1, z))


def y_up(x):
    return move_dw(x, lambda xh, y, c: (xh, y + 1, c))


def y_down(x):
    return move_dw(x, lambda xh, y, c: (xh, y - 1, c))


def swap_xh(x):
    return move_dw(x, lambda xh, y, c: (xh + 1, y, c))


def swap_core(x):
    return move_dw(x, lambda xh, y, c: (xh, y, c + 1))


def vmem():
    return pl.BlockSpec(memory_space=pltpu.VMEM)


def hbm():
    return pl.BlockSpec(memory_space=pl.ANY)


def call(kernel, outs, ins, out_specs, in_specs, scratch=(), flops=0, moved=0, name=None, limit=VMEM_LIMIT):
    return pl.pallas_call(
        kernel,
        out_shape=outs,
        in_specs=in_specs,
        out_specs=out_specs,
        scratch_shapes=list(scratch),
        compiler_params=pltpu.CompilerParams(vmem_limit_bytes=limit),
        cost_estimate=pl.CostEstimate(flops=0, bytes_accessed=1024, transcendentals=0),
        name=name,
    )(*ins)


def prep_tokens(table, tokens, out_grad):
    rows, width = tokens.shape
    half = width // NCORE
    block = half // len(ORDER)

    def kernel(table_ref, tok_ref, grad_ref, own_ref, other_ref):
        for j in range(len(ORDER)):
            cols = slice(j * block, (j + 1) * block)
            for k, out in enumerate((own_ref, other_ref)):
                at = pl.multiple_of(table_ref[k * len(ORDER) + j] * block, block)
                out[0, :, cols] = tok_ref[:, pl.ds(at, block)]
                out[1, :, cols] = grad_ref[:, pl.ds(at, block)]

    shape = jax.ShapeDtypeStruct((2, rows, half), BF16)
    return call(
        kernel, (shape, shape), (table, tokens, out_grad), (vmem(), vmem()),
        [pl.BlockSpec(memory_space=pltpu.SMEM), vmem(), vmem()],
        moved=8 * rows * width, name="prep_tokens",
    )


def prep_weights(gate, up, down):
    depth, width = gate.shape

    def kernel(gate_ref, up_ref, down_ref, out_ref):
        out_ref[:, :width] = gate_ref[...]
        out_ref[:, width : 2 * width] = up_ref[...]
        out_ref[:, 2 * width :] = down_ref[...].T

    return call(
        kernel, jax.ShapeDtypeStruct((depth, 3 * width), BF16), (gate, up, down), vmem(),
        [vmem()] * 3, moved=12 * depth * width, name="prep_weights",
    )


def start_all(copies):
    for c in copies:
        c.start()


def wait_all(copies):
    for c in copies:
        c.wait()


def forward(pieces, rows, weights, splits):
    shards = [x for x, _ in pieces]
    n_t, n_w = len(pieces), len(weights)
    half = shards[0].shape[2]
    depth, width3 = weights[0].shape
    width, width2 = width3 // 3, width3 // 3 * 2
    total = n_t * rows
    each = total // splits
    parts = 2
    per = n_w // parts

    def kernel(*refs):
        t_in, w_in = refs[:n_t], refs[n_t : n_t + n_w]
        outs, (rows_ref, tbuf, wbuf, acc, tsem, wsem, osem) = refs[n_t + n_w :][: 3 * splits], refs[n_t + n_w + 3 * splits :]
        t_copies = [
            pltpu.make_async_copy(
                r.at[:, pl.ds(pieces[i][1], rows)], tbuf.at[:, pl.ds(i * rows, rows)], tsem.at[i]
            )
            for i, r in enumerate(t_in)
        ]
        w_copies = [
            pltpu.make_async_copy(r, wbuf.at[pl.ds(j * depth, depth)], wsem.at[j])
            for j, r in enumerate(w_in)
        ]
        start_all(t_copies + w_copies)
        wait_all(t_copies)
        keep = pltpu.make_async_copy(tbuf, rows_ref, osem)
        keep.start()
        for p in range(parts):
            wait_all(w_copies[p * per : (p + 1) * per])
            ks = slice(p * per * depth, (p + 1) * per * depth)
            for k, cols in enumerate((slice(0, width2), slice(width2, width3))):
                term = jnp.dot(tbuf[k, :, ks], wbuf[ks, cols], preferred_element_type=F32)
                if p > 0:
                    term = term + acc[:, cols]
                if p < parts - 1:
                    acc[:, cols] = term
                else:
                    for i in range(term.shape[1] // width):
                        part = term[:, i * width : (i + 1) * width].astype(BF16)
                        for h in range(splits):
                            outs[3 * h + 2 * k + i][...] = part[h * each : (h + 1) * each]
        keep.wait()

    *partial, chunk = call(
        kernel,
        (jax.ShapeDtypeStruct((each, width), BF16),) * (3 * splits)
        + (jax.ShapeDtypeStruct((2, total, half), BF16),),
        (*shards, *weights), (vmem(),) * (3 * splits) + (hbm(),), [hbm()] * (n_t + n_w),
        scratch=(
            pltpu.VMEM((2, total, half), BF16),
            pltpu.VMEM((half, width3), BF16),
            pltpu.VMEM((total, width3), F32),
            pltpu.SemaphoreType.DMA((n_t,)),
            pltpu.SemaphoreType.DMA((n_w,)),
            pltpu.SemaphoreType.DMA,
        ),
        flops=2 * total * half * width3,
        moved=2 * (4 * total * half + half * width3 + total * width3),
        name="forward",
    )
    return partial, chunk


def activate(a, b, src, out, dst, step):
    width = a[0].shape[1]
    gate, up, grad = (p[src, :].astype(F32) + q[src, :].astype(F32) for p, q in zip(a, b, strict=True))
    s = 0.5 + 0.5 * jnp.tanh(0.5 * gate)
    act = gate * s
    out[dst, 2 * width :] = (act * up).astype(BF16)
    out[dst, :width] = (grad * up * s * (1.0 + gate * (1.0 - s))).astype(BF16)
    out[dst, width : 2 * width] = (grad * act).astype(BF16)


def activations(mine, other):
    rows, width = mine[0].shape
    count = len(mine)
    splits = count // 3
    step = 16

    def kernel(*refs):
        a, b, out_ref = refs[:count], refs[count : 2 * count], refs[2 * count]
        for h in range(splits):

            def one(i, _, h=h):
                src = pl.ds(pl.multiple_of(i * step, step), step)
                dst = pl.ds(pl.multiple_of(h * rows + i * step, step), step)
                activate(a[3 * h : 3 * h + 3], b[3 * h : 3 * h + 3], src, out_ref, dst, step)
                return 0

            lax.fori_loop(0, rows // step, one, 0)

    return call(
        kernel, jax.ShapeDtypeStruct((splits * rows, 3 * width), BF16), (*mine, *other), vmem(),
        [vmem()] * (2 * count), flops=30 * splits * rows * width, moved=18 * splits * rows * width,
        name="activations",
    )


def term_columns(acts, wbuf, qbuf, terms, osem, h, cols, depth, per, out, sem=0):
    for n in range(h * cols, (h + 1) * cols, depth):
        qbuf[:, n : n + depth] = lax.dot_general(
            acts[...], wbuf[n : n + depth, :], (((1,), (1,)), ((), ())), preferred_element_type=F32
        ).astype(BF16)
    for k, r in enumerate(terms):
        c = pltpu.make_async_copy(
            qbuf.at[pl.ds(k * per, per), pl.ds(h * cols, cols)],
            r.at[:, pl.ds(h * cols, cols)],
            osem.at[sem + h * len(terms) + k],
        )
        c.start()
        out.append(c)


def backward(mine, other, weights, pieces, scale, prev=(), chunks=(), count=0):
    n_w, n_p, n_c = len(weights), len(prev), len(chunks)
    rows, width = mine[0].shape
    width3 = 3 * width
    depth = weights[0].shape[0]
    half = n_w * depth
    per = rows // pieces
    prev_rows = [r.shape[0] for r in prev]
    starts = [sum(prev_rows[:i]) for i in range(n_p + 1)]
    total = starts[-1] + rows
    step = 16
    halves = 2

    def kernel(*refs):
        refs = list(refs)

        def take(n):
            got = refs[:n]
            del refs[:n]
            return got

        parts, w_in, prev_in, t_in = take(6), take(n_w), take(n_p), take(n_c)
        (acts_ref,), terms, grads = take(1), take(pieces), take(count)
        pbuf, abuf, wbuf, qbuf, tbuf, gbuf, psem, wsem, tsem, osem = refs
        here = starts[-1]
        bufs = [pbuf.at[k] for k in range(6)]
        p_copies = [pltpu.make_async_copy(r, pbuf.at[k], psem.at[k]) for k, r in enumerate(parts)]
        t_copies = [
            pltpu.make_async_copy(r, abuf.at[pl.ds(starts[i], prev_rows[i])], tsem.at[i])
            for i, r in enumerate(prev_in)
        ] + [
            pltpu.make_async_copy(
                r.at[:, :, pl.ds(0, count * depth)],
                tbuf.at[:, pl.ds(starts[i], r.shape[1])],
                tsem.at[n_p + i],
            )
            for i, r in enumerate(t_in)
        ]
        w_copies = [
            pltpu.make_async_copy(
                r.at[:, pl.ds(0, 2 * width)], wbuf.at[pl.ds(j * depth, depth)], wsem.at[j]
            )
            for j, r in enumerate(w_in)
        ]
        start_all(p_copies + t_copies + w_copies)
        wait_all(p_copies)

        def one(i, _):
            src = pl.ds(pl.multiple_of(i * step, step), step)
            dst = pl.ds(pl.multiple_of(here + i * step, step), step)
            activate(bufs[:3], bufs[3:], src, abuf, dst, step)
            return 0

        lax.fori_loop(0, rows // step, one, 0)
        out = [pltpu.make_async_copy(abuf.at[pl.ds(here, rows)], acts_ref, osem.at[0])]
        out[0].start()
        if count:
            wait_all(t_copies)
            weight_terms(abuf, tbuf, gbuf, grads, osem, 1, 0, count, scale, out)
        cols = half // halves
        for h in range(halves):
            wait_all(w_copies[h * n_w // halves : (h + 1) * n_w // halves])
            term_columns(
                abuf.at[pl.ds(here, rows), pl.ds(0, 2 * width)],
                wbuf, qbuf, terms, osem, h, cols, depth, per, out, 1 + count,
            )
        wait_all(out)

    shapes = (
        [jax.ShapeDtypeStruct((rows, width3), BF16)]
        + [jax.ShapeDtypeStruct((per, half), BF16)] * pieces
        + [jax.ShapeDtypeStruct((depth, width3), BF16)] * count
    )
    got = call(
        kernel, shapes, (*mine, *other, *weights, *prev, *chunks), [hbm()] * len(shapes),
        [hbm()] * (6 + n_w + n_p + n_c),
        scratch=(
            pltpu.VMEM((6, rows, width), BF16),
            pltpu.VMEM((total, width3), BF16),
            pltpu.VMEM((half, 2 * width), BF16),
            pltpu.VMEM((rows, half), BF16),
            pltpu.VMEM((2, total, max(count, 1) * depth), BF16),
            pltpu.VMEM((max(count, 1), depth, width3), BF16),
            pltpu.SemaphoreType.DMA((6,)),
            pltpu.SemaphoreType.DMA((n_w,)),
            pltpu.SemaphoreType.DMA((max(n_p + n_c, 1),)),
            pltpu.SemaphoreType.DMA((1 + count + halves * pieces,)),
        ),
        flops=4 * rows * half * width + 2 * total * count * depth * width3,
        moved=2 * (3 * rows * width3 + 2 * half * width + rows * half),
        name="backward", limit=56 * 1024 * 1024,
    )
    return got[0], got[1 : 1 + pieces], got[1 + pieces :]


def weight_terms(abuf, tbuf, gbuf, grads, osem, sem, first, count, scale, out):
    depth, width3 = gbuf.shape[1:]
    width2 = width3 // 3 * 2
    dims = (((0,), (0,)), ((), ()))
    for j in range(first, first + count):
        cols = slice(j * depth, (j + 1) * depth)
        for k, w in enumerate((slice(0, width2), slice(width2, width3))):
            got = lax.dot_general(tbuf[k, :, cols], abuf[:, w], dims, preferred_element_type=F32)
            gbuf[j, :, w] = (got * scale).astype(BF16)
        c = pltpu.make_async_copy(gbuf.at[j], grads[j], osem.at[sem + j])
        c.start()
        out.append(c)


def weight_grads(acts, chunks, weights, pieces, first, count, scale):
    n_a, n_w = len(acts), len(weights)
    width3 = acts[0].shape[1]
    width2 = width3 // 3 * 2
    rows = [r.shape[0] for r in acts]
    starts = [sum(rows[:i]) for i in range(n_a)]
    half = chunks[0].shape[2]
    depth = half // len(ORDER)
    group = 2
    groups = count // group
    total = sum(rows)
    per = rows[0] // pieces

    def kernel(*refs):
        refs = list(refs)

        def take(n):
            got = refs[:n]
            del refs[:n]
            return got

        a_in, t_in, w_in, grads, terms = take(n_a), take(n_a), take(n_w), take(count), take(pieces)
        abuf, tbuf, gbuf, wbuf, qbuf, asem, tsem, wsem, osem = refs
        a_copies = [
            pltpu.make_async_copy(r, abuf.at[pl.ds(starts[i], rows[i])], asem.at[i])
            for i, r in enumerate(a_in)
        ]
        t_copies = [
            [
                pltpu.make_async_copy(
                    r.at[:, :, pl.ds((first + g * group) * depth, group * depth)],
                    tbuf.at[:, pl.ds(starts[i], rows[i]), pl.ds(g * group * depth, group * depth)],
                    tsem.at[g * n_a + i],
                )
                for i, r in enumerate(t_in)
            ]
            for g in range(groups)
        ]
        w_copies = [
            pltpu.make_async_copy(
                r.at[:, pl.ds(0, width2)], wbuf.at[pl.ds(j * depth, depth)], wsem.at[j]
            )
            for j, r in enumerate(w_in)
        ]
        start_all(a_copies)
        for g in t_copies:
            start_all(g)
        start_all(w_copies)
        wait_all(a_copies)
        out = []
        for g in range(groups):
            wait_all(t_copies[g])
            weight_terms(abuf, tbuf, gbuf, grads, osem, 0, g * group, group, scale, out)
        wait_all(w_copies)
        for h in range(2):
            term_columns(
                abuf.at[pl.ds(0, rows[0]), pl.ds(0, width2)],
                wbuf, qbuf, terms, osem, h, half // 2, depth, per, out, count,
            )
        wait_all(out)

    shapes = [jax.ShapeDtypeStruct((depth, width3), BF16)] * count + [
        jax.ShapeDtypeStruct((per, half), BF16)
    ] * pieces
    got = call(
        kernel, shapes, (*acts, *chunks, *weights), [hbm()] * len(shapes), [hbm()] * (2 * n_a + n_w),
        scratch=(
            pltpu.VMEM((total, width3), BF16),
            pltpu.VMEM((2, total, count * depth), BF16),
            pltpu.VMEM((count, depth, width3), BF16),
            pltpu.VMEM((half, width2), BF16),
            pltpu.VMEM((rows[0], half), BF16),
            pltpu.SemaphoreType.DMA((n_a,)),
            pltpu.SemaphoreType.DMA((groups * n_a,)),
            pltpu.SemaphoreType.DMA((n_w,)),
            pltpu.SemaphoreType.DMA((count + 2 * pieces,)),
        ),
        flops=2 * total * count * depth * width3 + 2 * rows[0] * half * width2,
        moved=2 * (total * width3 + 2 * total * count * depth + count * depth * width3),
        name="weight_grads", limit=56 * 1024 * 1024,
    )
    return got[:count], got[count:]


def tie(*arrays):
    return lax.optimization_barrier(arrays)


def add(*terms):
    total = terms[0].astype(F32)
    for t in terms[1:]:
        total = total + t.astype(F32)
    return total.astype(BF16)


def finish_weights(own, from_below, from_above, from_xh):
    depth, width3 = own.shape
    width = width3 // 3

    def kernel(a_ref, b_ref, c_ref, d_ref, gate_ref, up_ref, down_ref):
        def total(k):
            cols = slice(k * width, (k + 1) * width)
            return sum(r[:, cols].astype(F32) for r in (a_ref, b_ref, c_ref, d_ref)).astype(BF16)

        gate_ref[...] = total(0)
        up_ref[...] = total(1)
        down_ref[...] = total(2).T

    shapes = [jax.ShapeDtypeStruct(s, BF16) for s in ((depth, width), (depth, width), (width, depth))]
    return call(
        kernel, shapes, (own, from_below, from_above, from_xh), [vmem()] * 3, [vmem()] * 4,
        moved=30 * depth * width, name="finish_weights",
    )


def finish_tokens(table, own, other):
    rows, half = own.shape
    block = half // len(ORDER)

    def kernel(table_ref, own_ref, other_ref, out_ref):
        for j in range(len(ORDER)):
            cols = slice(j * block, (j + 1) * block)
            for k, r in enumerate((own_ref, other_ref)):
                at = pl.multiple_of(table_ref[k * len(ORDER) + j] * block, block)
                out_ref[:, pl.ds(at, block)] = r[:, cols]

    return call(
        kernel, jax.ShapeDtypeStruct((rows, NCORE * half), BF16), (table, own, other), vmem(),
        [pl.BlockSpec(memory_space=pltpu.SMEM), vmem(), vmem()],
        moved=8 * rows * half, name="finish_tokens",
    )


def body(tokens, out_grad, gate_weight, up_weight, down_weight):
    rows = tokens.shape[0]
    scale = 1.0 / math.sqrt(rows * lax.axis_size("tensor") * lax.axis_size("dw"))
    dw = lax.axis_index("dw")
    core, y, xh = dw % NCORE, dw // NCORE % NY, dw // (NCORE * NY)
    table = jnp.stack(
        [
            (((xh + dx) % NXH) * NY + (y + dy) % NY) * NCORE + c
            for c in (core, 1 - core)
            for dx, dy in ORDER
        ]
    ).astype(jnp.int32)

    own_part, other_part = prep_tokens(table, tokens, out_grad)
    got = swap_core(other_part)
    low = jnp.where(core == 0, own_part, got)
    high = jnp.where(core == 0, got, own_part)
    a = {0: jnp.concatenate([low, high], axis=1)}
    w = {(0, 0): prep_weights(gate_weight, up_weight, down_weight)}

    n = NCORE * rows
    a[1], a[7] = z_down(a[0]), z_up(a[0])
    b = {0: swap_xl(a[0])}
    w[1, 0], w[0, 1], w[0, 3] = swap_xh(w[0, 0]), y_down(w[0, 0]), y_up(w[0, 0])
    a2b1 = z_down(jnp.concatenate([a[1], b[0]], axis=1))
    a6b7 = z_up(jnp.concatenate([a[7], b[0]], axis=1))
    w10, w01, w03, a2b1, a6b7 = tie(w[1, 0], w[0, 1], w[0, 3], a2b1, a6b7)
    w[1, 1], w[1, 3], w[0, 2] = swap_xh(w01), y_up(w10), y_down(w01)
    a3b2, a5b6 = z_down(a2b1), z_up(a6b7)
    w13, w11, w[0, 2], a3b2, a5b6 = tie(w[1, 3], w[1, 1], w[0, 2], a3b2, a5b6)
    w[1, 1], w[1, 3] = w11, w13
    k = w13.shape[0] // 2
    w[1, 2] = jnp.concatenate([y_up(w13[:k]), y_down(w11[k:])])
    a4b3, b[5] = z_down(a3b2), z_up(a5b6[:, n:])
    b[4] = move_tensor(a5b6[:, :n], lambda xl, z: (xl + 1, z + 1))
    weights = [w[k] for k in ORDER]

    early = [
        (a[0], 0), (b[0], 0), (a[1], 0), (a2b1, n), (a[7], 0), (a6b7, n), (a2b1, 0), (a3b2, n), (a6b7, 0), (a5b6, n)
    ]
    late = [(a3b2, 0), (a4b3, n), (a5b6, 0), (b[5], 0), (a4b3, 0), (b[4], 0)]
    part1, rows1 = forward(early, n, weights, 2)
    other1 = [swap_core(x) for x in part1]
    part2, rows2 = forward(late, n, weights, 1)
    other2 = [swap_core(x) for x in part2]
    acts1 = activations(part1, other1)
    acts2, terms2, first = backward(
        part2, other2, weights, len(CHUNKS[1]), scale, prev=(acts1,), chunks=(rows1, rows2), count=2
    )
    rest, terms1 = weight_grads(
        (acts1, acts2), (rows1, rows2), weights, len(CHUNKS[0]), 2, len(ORDER) - 2, scale
    )
    terms = dict(zip(CHUNKS[0] + CHUNKS[1], [*terms1, *terms2], strict=True))

    p = dict(zip(ORDER, [*first, *rest], strict=True))
    r11 = y_up(p[1, 1])
    r12 = y_down(p[1, 2])
    r13 = y_down(add(p[1, 3], r12))
    p02, _ = tie(p[0, 2], r11)
    r02 = y_up(p02)
    p03, _ = tie(p[0, 3], r13)
    r03 = y_down(p03)
    r01 = y_up(add(p[0, 1], r02))
    from_xh = swap_xh(add(p[1, 0], r11, r13))
    grads = finish_weights(p[0, 0], r01, r03, from_xh)

    up = z_up(terms[4][:n])
    down = z_down(terms[4][n:])
    up = z_up(terms[3].at[:n].set(add(terms[3][:n], up)))
    down = z_down(terms[5].at[n:].set(add(terms[5][n:], down)))
    up, down, _, _ = tie(up, down, r11, r12)
    up = z_up(add(terms[2], up))
    down = z_down(add(terms[6], down))
    up = z_up(add(terms[1], up))
    down = z_down(add(terms[7], down))
    up, down, _, _ = tie(up, down, r13, r02)
    from_xl = swap_xl(add(terms[0][n:], up[n:], down[n:]))
    total = add(terms[0][:n], up[:n], down[:n], from_xl)
    mine = lax.dynamic_slice_in_dim(total, core * rows, rows)
    theirs = lax.dynamic_slice_in_dim(total, (1 - core) * rows, rows)
    grad_tokens = finish_tokens(table, mine, swap_core(theirs))
    return (grad_tokens, *grads)


def solution(mesh):
    placed = (
        P(("tensor", "dw"), None),
        P(("tensor", "dw"), None),
        P("dw", "tensor"),
        P("dw", "tensor"),
        P("tensor", "dw"),
    )
    return jax.shard_map(
        body,
        mesh=mesh,
        in_specs=placed,
        out_specs=(
            P(("tensor", "dw"), None),
            P("dw", "tensor"),
            P("dw", "tensor"),
            P("tensor", "dw"),
        ),
        check_vma=False,
    )
```

```python
import functools
import itertools
import math

import jax
import jax.numpy as jnp
from jax import lax
from jax.experimental import pallas as pl
from jax.experimental.pallas import tpu as pltpu
from jax.sharding import PartitionSpec as P

NXL, NZ, NXH, NY, NCORE = 2, 8, 2, 4, 2
BF16, F32 = jnp.bfloat16, jnp.float32
VMEM_LIMIT = 20 * 1024 * 1024

ORDER = ((0, 2), (1, 2), (1, 0), (1, 1), (0, 3), (0, 1), (1, 3), (0, 0))
FIRST = 3
CHUNKS = ((0, 1, 7, 2, 6), (3, 5, 4))


def move_tensor(x, dest):
    perm = []
    for xl in range(NXL):
        for z in range(NZ):
            a, b = dest(xl, z)
            perm.append((xl * NZ + z, a % NXL * NZ + b % NZ))
    return lax.ppermute(x, "tensor", perm)


def move_dw(x, dest):
    perm = []
    for xh in range(NXH):
        for y in range(NY):
            for c in range(NCORE):
                a, b, e = dest(xh, y, c)
                perm.append(
                    ((xh * NY + y) * NCORE + c, (a % NXH * NY + b % NY) * NCORE + e % NCORE)
                )
    return lax.ppermute(x, "dw", perm)


def move_all(x, dest):
    sizes = (NXL, NZ, NXH, NY, NCORE)
    perm = []
    for at in itertools.product(*map(range, sizes)):
        ends = at, dest(*at)
        source, target = (
            functools.reduce(lambda n, e: n * e[1] + e[0] % e[1], zip(end, sizes), 0) for end in ends
        )
        perm.append((source, target))
    return lax.ppermute(x, ("tensor", "dw"), perm)


def z_up(x):
    return move_tensor(x, lambda xl, z: (xl, z + 1))


def z_down(x):
    return move_tensor(x, lambda xl, z: (xl, z - 1))


def swap_xl(x):
    return move_tensor(x, lambda xl, z: (xl + 1, z))


def y_up(x):
    return move_dw(x, lambda xh, y, c: (xh, y + 1, c))


def y_down(x):
    return move_dw(x, lambda xh, y, c: (xh, y - 1, c))


def swap_xh(x):
    return move_dw(x, lambda xh, y, c: (xh + 1, y, c))


def swap_core(x):
    return move_dw(x, lambda xh, y, c: (xh, y, c + 1))


def vmem():
    return pl.BlockSpec(memory_space=pltpu.VMEM)


def hbm():
    return pl.BlockSpec(memory_space=pl.ANY)


def pinned():
    return pl.BlockSpec(memory_space=pltpu.HBM)


def call(kernel, outs, ins, out_specs, in_specs, scratch=(), flops=0, moved=0, name=None, limit=VMEM_LIMIT):
    return pl.pallas_call(
        kernel,
        out_shape=outs,
        in_specs=in_specs,
        out_specs=out_specs,
        scratch_shapes=list(scratch),
        compiler_params=pltpu.CompilerParams(vmem_limit_bytes=limit),
        cost_estimate=pl.CostEstimate(flops=0, bytes_accessed=1024, transcendentals=0),
        name=name,
    )(*ins)


def prep_tokens(table, tokens, out_grad):
    rows, width = tokens.shape
    half = width // NCORE
    block = half // len(ORDER)

    def kernel(table_ref, tok_ref, grad_ref, own_ref, other_ref):
        for j in range(len(ORDER)):
            cols = slice(j * block, (j + 1) * block)
            for k, out in enumerate((own_ref, other_ref)):
                at = pl.multiple_of(table_ref[k * len(ORDER) + j] * block, block)
                out[0, :, cols] = tok_ref[:, pl.ds(at, block)]
                out[1, :, cols] = grad_ref[:, pl.ds(at, block)]

    shape = jax.ShapeDtypeStruct((2, rows, half), BF16)
    return call(
        kernel, (shape, shape), (table, tokens, out_grad), (vmem(), vmem()),
        [pl.BlockSpec(memory_space=pltpu.SMEM), vmem(), vmem()],
        moved=8 * rows * width, name="prep_tokens",
    )


def prep_weights(gate, up, down):
    depth, width = gate.shape

    def kernel(gate_ref, up_ref, down_ref, out_ref):
        out_ref[:, :width] = gate_ref[...]
        out_ref[:, width : 2 * width] = up_ref[...]
        out_ref[:, 2 * width :] = down_ref[...].T

    return call(
        kernel, jax.ShapeDtypeStruct((depth, 3 * width), BF16), (gate, up, down), vmem(),
        [vmem()] * 3, moved=12 * depth * width, name="prep_weights",
    )


def start_all(copies):
    for c in copies:
        c.start()


def wait_all(copies):
    for c in copies:
        c.wait()


def forward(pieces, rows, weights, splits):
    shards = [x for x, _ in pieces]
    n_t, n_w = len(pieces), len(weights)
    half = shards[0].shape[2]
    depth, width3 = weights[0].shape
    width, width2 = width3 // 3, width3 // 3 * 2
    total = n_t * rows
    each = total // splits
    parts = 2
    per = n_w // parts

    def kernel(*refs):
        t_in, w_in = refs[:n_t], refs[n_t : n_t + n_w]
        outs, (rows_ref, tbuf, wbuf, acc, tsem, wsem, osem) = refs[n_t + n_w :][: 3 * splits], refs[n_t + n_w + 3 * splits :]
        t_copies = [
            pltpu.make_async_copy(
                r.at[:, pl.ds(pieces[i][1], rows)], tbuf.at[:, pl.ds(i * rows, rows)], tsem.at[i]
            )
            for i, r in enumerate(t_in)
        ]
        w_copies = [
            pltpu.make_async_copy(r, wbuf.at[pl.ds(j * depth, depth)], wsem.at[j])
            for j, r in enumerate(w_in)
        ]
        start_all(t_copies + w_copies)
        wait_all(t_copies)
        keep = pltpu.make_async_copy(tbuf, rows_ref, osem)
        keep.start()
        for p in range(parts):
            wait_all(w_copies[p * per : (p + 1) * per])
            ks = slice(p * per * depth, (p + 1) * per * depth)
            for k, cols in enumerate((slice(0, width2), slice(width2, width3))):
                term = jnp.dot(tbuf[k, :, ks], wbuf[ks, cols], preferred_element_type=F32)
                if p > 0:
                    term = term + acc[:, cols]
                if p < parts - 1:
                    acc[:, cols] = term
                else:
                    for i in range(term.shape[1] // width):
                        part = term[:, i * width : (i + 1) * width].astype(BF16)
                        for h in range(splits):
                            outs[3 * h + 2 * k + i][...] = part[h * each : (h + 1) * each]
        keep.wait()

    *partial, chunk = call(
        kernel,
        (jax.ShapeDtypeStruct((each, width), BF16),) * (3 * splits)
        + (jax.ShapeDtypeStruct((2, total, half), BF16),),
        (*shards, *weights), (vmem(),) * (3 * splits) + (hbm(),), [hbm()] * (n_t + n_w),
        scratch=(
            pltpu.VMEM((2, total, half), BF16),
            pltpu.VMEM((half, width3), BF16),
            pltpu.VMEM((total, width3), F32),
            pltpu.SemaphoreType.DMA((n_t,)),
            pltpu.SemaphoreType.DMA((n_w,)),
            pltpu.SemaphoreType.DMA,
        ),
        flops=2 * total * half * width3,
        moved=2 * (4 * total * half + half * width3 + total * width3),
        name="forward",
    )
    return partial, chunk


def activate(a, b, src, out, dst, step):
    width = a[0].shape[1]
    gate, up, grad = (p[src, :].astype(F32) + q[src, :].astype(F32) for p, q in zip(a, b, strict=True))
    s = 0.5 + 0.5 * jnp.tanh(0.5 * gate)
    act = gate * s
    out[dst, 2 * width :] = (act * up).astype(BF16)
    out[dst, :width] = (grad * up * s * (1.0 + gate * (1.0 - s))).astype(BF16)
    out[dst, width : 2 * width] = (grad * act).astype(BF16)


def activations(mine, other):
    rows, width = mine[0].shape
    count = len(mine)
    splits = count // 3
    step = 16

    def kernel(*refs):
        a, b, out_ref = refs[:count], refs[count : 2 * count], refs[2 * count]
        for h in range(splits):

            def one(i, _, h=h):
                src = pl.ds(pl.multiple_of(i * step, step), step)
                dst = pl.ds(pl.multiple_of(h * rows + i * step, step), step)
                activate(a[3 * h : 3 * h + 3], b[3 * h : 3 * h + 3], src, out_ref, dst, step)
                return 0

            lax.fori_loop(0, rows // step, one, 0)

    return call(
        kernel, jax.ShapeDtypeStruct((splits * rows, 3 * width), BF16), (*mine, *other), vmem(),
        [vmem()] * (2 * count), flops=30 * splits * rows * width, moved=18 * splits * rows * width,
        name="activations",
    )


def term_columns(acts, wbuf, qbuf, terms, osem, h, cols, depth, per, out, sem=0):
    for n in range(h * cols, (h + 1) * cols, depth):
        qbuf[:, n : n + depth] = lax.dot_general(
            acts[...], wbuf[n : n + depth, :], (((1,), (1,)), ((), ())), preferred_element_type=F32
        ).astype(BF16)
    for k, r in enumerate(terms):
        c = pltpu.make_async_copy(
            qbuf.at[pl.ds(k * per, per), pl.ds(h * cols, cols)],
            r.at[:, pl.ds(h * cols, cols)],
            osem.at[sem + h * len(terms) + k],
        )
        c.start()
        out.append(c)


def backward(mine, other, weights, pieces, scale, prev=(), chunks=(), count=0):
    n_w, n_p, n_c = len(weights), len(prev), len(chunks)
    rows, width = mine[0].shape
    width3 = 3 * width
    depth = weights[0].shape[0]
    half = n_w * depth
    per = rows // pieces
    prev_rows = [r.shape[0] for r in prev]
    starts = [sum(prev_rows[:i]) for i in range(n_p + 1)]
    total = starts[-1] + rows
    step = 16
    halves = 2

    def kernel(*refs):
        refs = list(refs)

        def take(n):
            got = refs[:n]
            del refs[:n]
            return got

        parts, w_in, prev_in, t_in = take(6), take(n_w), take(n_p), take(n_c)
        (acts_ref,), terms, grads = take(1), take(pieces), take(count)
        pbuf, abuf, wbuf, qbuf, tbuf, gbuf, psem, wsem, tsem, osem = refs
        here = starts[-1]
        bufs = [pbuf.at[k] for k in range(6)]
        p_copies = [pltpu.make_async_copy(r, pbuf.at[k], psem.at[k]) for k, r in enumerate(parts)]
        t_copies = [
            pltpu.make_async_copy(r, abuf.at[pl.ds(starts[i], prev_rows[i])], tsem.at[i])
            for i, r in enumerate(prev_in)
        ] + [
            pltpu.make_async_copy(
                r.at[:, :, pl.ds(0, count * depth)],
                tbuf.at[:, pl.ds(starts[i], r.shape[1])],
                tsem.at[n_p + i],
            )
            for i, r in enumerate(t_in)
        ]
        w_copies = [
            pltpu.make_async_copy(
                r.at[:, pl.ds(0, 2 * width)], wbuf.at[pl.ds(j * depth, depth)], wsem.at[j]
            )
            for j, r in enumerate(w_in)
        ]
        start_all(p_copies + t_copies + w_copies)
        wait_all(p_copies)

        def one(i, _):
            src = pl.ds(pl.multiple_of(i * step, step), step)
            dst = pl.ds(pl.multiple_of(here + i * step, step), step)
            activate(bufs[:3], bufs[3:], src, abuf, dst, step)
            return 0

        lax.fori_loop(0, rows // step, one, 0)
        out = [pltpu.make_async_copy(abuf.at[pl.ds(here, rows)], acts_ref, osem.at[0])]
        out[0].start()
        if count:
            wait_all(t_copies)
            weight_terms(abuf, tbuf, gbuf, grads, osem, 1, 0, count, scale, out)
        cols = half // halves
        for h in range(halves):
            wait_all(w_copies[h * n_w // halves : (h + 1) * n_w // halves])
            term_columns(
                abuf.at[pl.ds(here, rows), pl.ds(0, 2 * width)],
                wbuf, qbuf, terms, osem, h, cols, depth, per, out, 1 + count,
            )
        wait_all(out)

    shapes = (
        [jax.ShapeDtypeStruct((rows, width3), BF16)]
        + [jax.ShapeDtypeStruct((per, half), BF16)] * pieces
        + [jax.ShapeDtypeStruct((depth, width3), BF16)] * count
    )
    got = call(
        kernel, shapes, (*mine, *other, *weights, *prev, *chunks), [pinned()] * len(shapes),
        [hbm()] * (6 + n_w + n_p + n_c),
        scratch=(
            pltpu.VMEM((6, rows, width), BF16),
            pltpu.VMEM((total, width3), BF16),
            pltpu.VMEM((half, 2 * width), BF16),
            pltpu.VMEM((rows, half), BF16),
            pltpu.VMEM((2, total, max(count, 1) * depth), BF16),
            pltpu.VMEM((max(count, 1), depth, width3), BF16),
            pltpu.SemaphoreType.DMA((6,)),
            pltpu.SemaphoreType.DMA((n_w,)),
            pltpu.SemaphoreType.DMA((max(n_p + n_c, 1),)),
            pltpu.SemaphoreType.DMA((1 + count + halves * pieces,)),
        ),
        flops=4 * rows * half * width + 2 * total * count * depth * width3,
        moved=2 * (3 * rows * width3 + 2 * half * width + rows * half),
        name="backward",
    )
    return got[0], got[1 : 1 + pieces], got[1 + pieces :]


def weight_terms(abuf, tbuf, gbuf, grads, osem, sem, first, count, scale, out):
    depth, width3 = gbuf.shape[1:]
    width2 = width3 // 3 * 2
    dims = (((0,), (0,)), ((), ()))
    for j in range(first, first + count):
        cols = slice(j * depth, (j + 1) * depth)
        for k, w in enumerate((slice(0, width2), slice(width2, width3))):
            got = lax.dot_general(tbuf[k, :, cols], abuf[:, w], dims, preferred_element_type=F32)
            gbuf[j, :, w] = (got * scale).astype(BF16)
        c = pltpu.make_async_copy(gbuf.at[j], grads[j], osem.at[sem + j])
        c.start()
        out.append(c)


def weight_grads(acts, chunks, weights, pieces, first, count, scale):
    n_a, n_w = len(acts), len(weights)
    width3 = acts[0].shape[1]
    width2 = width3 // 3 * 2
    rows = [r.shape[0] for r in acts]
    starts = [sum(rows[:i]) for i in range(n_a)]
    half = chunks[0].shape[2]
    depth = half // len(ORDER)
    group = 2
    groups = [(g, min(group, count - g)) for g in range(0, count, group)]
    total = sum(rows)
    per = rows[0] // pieces

    def kernel(*refs):
        refs = list(refs)

        def take(n):
            got = refs[:n]
            del refs[:n]
            return got

        a_in, t_in, w_in, grads, terms = take(n_a), take(n_a), take(n_w), take(count), take(pieces)
        abuf, tbuf, gbuf, wbuf, qbuf, asem, tsem, wsem, osem = refs
        a_copies = [
            pltpu.make_async_copy(r, abuf.at[pl.ds(starts[i], rows[i])], asem.at[i])
            for i, r in enumerate(a_in)
        ]
        t_copies = [
            [
                pltpu.make_async_copy(
                    r.at[:, :, pl.ds((first + g) * depth, size * depth)],
                    tbuf.at[:, pl.ds(starts[i], rows[i]), pl.ds(g * depth, size * depth)],
                    tsem.at[k * n_a + i],
                )
                for i, r in enumerate(t_in)
            ]
            for k, (g, size) in enumerate(groups)
        ]
        w_copies = [
            pltpu.make_async_copy(
                r.at[:, pl.ds(0, width2)], wbuf.at[pl.ds(j * depth, depth)], wsem.at[j]
            )
            for j, r in enumerate(w_in)
        ]
        start_all(a_copies)
        for g in t_copies:
            start_all(g)
        start_all(w_copies)
        wait_all(a_copies)
        out = []
        for k, (g, size) in enumerate(groups):
            wait_all(t_copies[k])
            weight_terms(abuf, tbuf, gbuf, grads, osem, 0, g, size, scale, out)
        wait_all(w_copies)
        for h in range(2):
            term_columns(
                abuf.at[pl.ds(0, rows[0]), pl.ds(0, width2)],
                wbuf, qbuf, terms, osem, h, half // 2, depth, per, out, count,
            )
        wait_all(out)

    shapes = [jax.ShapeDtypeStruct((depth, width3), BF16)] * count + [
        jax.ShapeDtypeStruct((per, half), BF16)
    ] * pieces
    got = call(
        kernel, shapes, (*acts, *chunks, *weights), [pinned()] * len(shapes), [pinned()] * (2 * n_a + n_w),
        scratch=(
            pltpu.VMEM((total, width3), BF16),
            pltpu.VMEM((2, total, count * depth), BF16),
            pltpu.VMEM((count, depth, width3), BF16),
            pltpu.VMEM((half, width2), BF16),
            pltpu.VMEM((rows[0], half), BF16),
            pltpu.SemaphoreType.DMA((n_a,)),
            pltpu.SemaphoreType.DMA((len(groups) * n_a,)),
            pltpu.SemaphoreType.DMA((n_w,)),
            pltpu.SemaphoreType.DMA((count + 2 * pieces,)),
        ),
        flops=2 * total * count * depth * width3 + 2 * rows[0] * half * width2,
        moved=2 * (total * width3 + 2 * total * count * depth + count * depth * width3),
        name="weight_grads",
    )
    return got[:count], got[count:]


def tie(*arrays):
    return lax.optimization_barrier(arrays)


def add(*terms):
    total = terms[0].astype(F32)
    for t in terms[1:]:
        total = total + t.astype(F32)
    return total.astype(BF16)


def finish_weights(*terms):
    depth, width3 = terms[0].shape
    width = width3 // 3

    def kernel(*refs):
        terms_in, (gate_ref, up_ref, down_ref) = refs[:-3], refs[-3:]

        def total(k):
            cols = slice(k * width, (k + 1) * width)
            return sum(r[:, cols].astype(F32) for r in terms_in).astype(BF16)

        gate_ref[...] = total(0)
        up_ref[...] = total(1)
        down_ref[...] = total(2).T

    shapes = [jax.ShapeDtypeStruct(s, BF16) for s in ((depth, width), (depth, width), (width, depth))]
    return call(
        kernel, shapes, terms, [vmem()] * 3, [vmem()] * len(terms),
        moved=40 * depth * width, name="finish_weights",
    )


def finish_tokens(table, own, other):
    rows, half = own[0].shape
    block = half // len(ORDER)

    def kernel(table_ref, a_ref, b_ref, c_ref, d_ref, out_ref):
        for j in range(len(ORDER)):
            cols = slice(j * block, (j + 1) * block)
            for k, (p, q) in enumerate(((a_ref, b_ref), (c_ref, d_ref))):
                at = pl.multiple_of(table_ref[k * len(ORDER) + j] * block, block)
                total = p[:, cols].astype(F32) + q[:, cols].astype(F32)
                out_ref[:, pl.ds(at, block)] = total.astype(BF16)

    return call(
        kernel, jax.ShapeDtypeStruct((rows, NCORE * half), BF16), (table, *own, *other), vmem(),
        [pl.BlockSpec(memory_space=pltpu.SMEM)] + [vmem()] * 4,
        moved=12 * rows * half, name="finish_tokens",
    )


def body(tokens, out_grad, gate_weight, up_weight, down_weight):
    rows = tokens.shape[0]
    scale = 1.0 / math.sqrt(rows * lax.axis_size("tensor") * lax.axis_size("dw"))
    dw = lax.axis_index("dw")
    core, y, xh = dw % NCORE, dw // NCORE % NY, dw // (NCORE * NY)
    table = jnp.stack(
        [
            (((xh + dx) % NXH) * NY + (y + dy) % NY) * NCORE + c
            for c in (core, 1 - core)
            for dx, dy in ORDER
        ]
    ).astype(jnp.int32)

    own_part, other_part = prep_tokens(table, tokens, out_grad)
    got = swap_core(other_part)
    low = jnp.where(core == 0, own_part, got)
    high = jnp.where(core == 0, got, own_part)
    a = {0: jnp.concatenate([low, high], axis=1)}
    w = {(0, 0): prep_weights(gate_weight, up_weight, down_weight)}

    n = NCORE * rows
    a[1], a[7] = z_down(a[0]), z_up(a[0])
    b = {0: swap_xl(a[0])}
    w[1, 0], w[0, 1], w[0, 3] = swap_xh(w[0, 0]), y_down(w[0, 0]), y_up(w[0, 0])
    a2b1 = z_down(jnp.concatenate([a[1], b[0]], axis=1))
    a6b7 = z_up(jnp.concatenate([a[7], b[0]], axis=1))
    w10, w01, w03, a2b1, a6b7 = tie(w[1, 0], w[0, 1], w[0, 3], a2b1, a6b7)
    w[1, 1], w[1, 3], w[0, 2] = swap_xh(w01), y_up(w10), y_down(w01)
    a3b2, a5b6 = z_down(a2b1), z_up(a6b7)
    w13, w11, w[0, 2], a3b2, a5b6 = tie(w[1, 3], w[1, 1], w[0, 2], a3b2, a5b6)
    w[1, 1], w[1, 3] = w11, w13
    k = w13.shape[0] // 2
    w[1, 2] = jnp.concatenate([y_up(w13[:k]), y_down(w11[k:])])
    a4b3, b[5] = z_down(a3b2), z_up(a5b6[:, n:])
    b[4] = move_tensor(a5b6[:, :n], lambda xl, z: (xl + 1, z + 1))
    weights = [w[k] for k in ORDER]

    early = [
        (a[0], 0), (b[0], 0), (a[1], 0), (a2b1, n), (a[7], 0), (a6b7, n), (a2b1, 0), (a3b2, n), (a6b7, 0), (a5b6, n)
    ]
    late = [(a3b2, 0), (a4b3, n), (a5b6, 0), (b[5], 0), (a4b3, 0), (b[4], 0)]
    part1, rows1 = forward(early, n, weights, 2)
    other1 = [swap_core(x) for x in part1]
    part2, rows2 = forward(late, n, weights, 1)
    other2 = [swap_core(x) for x in part2]
    acts1 = activations(part1, other1)
    acts2, terms2, first = backward(
        part2, other2, weights, len(CHUNKS[1]), scale, prev=(acts1,), chunks=(rows1, rows2), count=FIRST
    )
    rest, terms1 = weight_grads(
        (acts1, acts2), (rows1, rows2), weights, len(CHUNKS[0]), FIRST, len(ORDER) - FIRST, scale
    )
    terms = dict(zip(CHUNKS[0] + CHUNKS[1], [*terms1, *terms2], strict=True))

    p = dict(zip(ORDER, [*first, *rest], strict=True))
    r02 = y_up(p[0, 2])
    r12 = y_down(p[1, 2])
    r10 = swap_xh(p[1, 0])
    r11 = move_dw(p[1, 1], lambda xh, y, c: (xh + 1, y + 1, c))
    r03 = y_down(p[0, 3])
    p01, p13, _, _ = tie(add(p[0, 1], r02), add(p[1, 3], r12), r11, r03)
    r01 = y_up(p01)
    r13 = move_dw(p13, lambda xh, y, c: (xh + 1, y - 1, c))
    grads = finish_weights(p[0, 0], r10, r11, r03, r01, r13)

    up = z_up(terms[4][:n])
    down = z_down(terms[4][n:])
    up = z_up(terms[3].at[:n].set(add(terms[3][:n], up)))
    down = z_down(terms[5].at[n:].set(add(terms[5][n:], down)))
    up, down, *_ = tie(up, down, r02, r12, r10)
    up = z_up(add(terms[2], up))
    down = z_down(add(terms[6], down))
    up, down, *_ = tie(up, down, r11, r03)
    up = z_up(add(terms[1], up))
    down = z_down(add(terms[7], down))
    up, down, *_ = tie(up, down, r01, r13)
    total = add(terms[0], up, down).reshape(NXL, NCORE, rows, -1)
    low, high = total[:, 0], total[:, 1]
    mine = jnp.where(core == 0, low, high)
    theirs = jnp.where(core == 0, high, low)
    grad_tokens = finish_tokens(
        table,
        (mine[0], swap_xl(mine[1])),
        (
            swap_core(theirs[0]),
            move_all(theirs[1], lambda xl, z, xh, y, c: (xl + 1, z, xh, y, c + 1)),
        ),
    )
    return (grad_tokens, *grads)


def solution(mesh):
    placed = (
        P(("tensor", "dw"), None),
        P(("tensor", "dw"), None),
        P("dw", "tensor"),
        P("dw", "tensor"),
        P("tensor", "dw"),
    )
    return jax.shard_map(
        body,
        mesh=mesh,
        in_specs=placed,
        out_specs=(
            P(("tensor", "dw"), None),
            P("dw", "tensor"),
            P("dw", "tensor"),
            P("tensor", "dw"),
        ),
        check_vma=False,
    )
```

```python
import functools
import itertools
import math

import jax
import jax.numpy as jnp
from jax import lax
from jax.experimental import pallas as pl
from jax.experimental.pallas import tpu as pltpu
from jax.sharding import PartitionSpec as P

NXL, NZ, NXH, NY, NCORE = 2, 8, 2, 4, 2
BF16, F32 = jnp.bfloat16, jnp.float32
VMEM_LIMIT = 20 * 1024 * 1024

ORDER = ((0, 2), (1, 2), (1, 0), (1, 1), (0, 3), (0, 1), (1, 3), (0, 0))
FIRST = 3
CHUNKS = ((0, 1, 7, 2, 6), (3, 5, 4))


def move_tensor(x, dest):
    perm = []
    for xl in range(NXL):
        for z in range(NZ):
            a, b = dest(xl, z)
            perm.append((xl * NZ + z, a % NXL * NZ + b % NZ))
    return lax.ppermute(x, "tensor", perm)


def move_dw(x, dest):
    perm = []
    for xh in range(NXH):
        for y in range(NY):
            for c in range(NCORE):
                a, b, e = dest(xh, y, c)
                perm.append(
                    ((xh * NY + y) * NCORE + c, (a % NXH * NY + b % NY) * NCORE + e % NCORE)
                )
    return lax.ppermute(x, "dw", perm)


def move_all(x, dest):
    sizes = (NXL, NZ, NXH, NY, NCORE)
    perm = []
    for at in itertools.product(*map(range, sizes)):
        ends = at, dest(*at)
        source, target = (
            functools.reduce(lambda n, e: n * e[1] + e[0] % e[1], zip(end, sizes), 0) for end in ends
        )
        perm.append((source, target))
    return lax.ppermute(x, ("tensor", "dw"), perm)


def z_up(x):
    return move_tensor(x, lambda xl, z: (xl, z + 1))


def z_down(x):
    return move_tensor(x, lambda xl, z: (xl, z - 1))


def swap_xl(x):
    return move_tensor(x, lambda xl, z: (xl + 1, z))


def y_up(x):
    return move_dw(x, lambda xh, y, c: (xh, y + 1, c))


def y_down(x):
    return move_dw(x, lambda xh, y, c: (xh, y - 1, c))


def swap_xh(x):
    return move_dw(x, lambda xh, y, c: (xh + 1, y, c))


def swap_core(x):
    return move_dw(x, lambda xh, y, c: (xh, y, c + 1))


def vmem():
    return pl.BlockSpec(memory_space=pltpu.VMEM)


def hbm():
    return pl.BlockSpec(memory_space=pl.ANY)


def pinned():
    return pl.BlockSpec(memory_space=pltpu.HBM)


def call(kernel, outs, ins, out_specs, in_specs, scratch=(), flops=0, moved=0, name=None, limit=VMEM_LIMIT):
    return pl.pallas_call(
        kernel,
        out_shape=outs,
        in_specs=in_specs,
        out_specs=out_specs,
        scratch_shapes=list(scratch),
        compiler_params=pltpu.CompilerParams(vmem_limit_bytes=limit),
        cost_estimate=pl.CostEstimate(flops=0, bytes_accessed=1024, transcendentals=0),
        name=name,
    )(*ins)


def prep_tokens(table, tokens, out_grad):
    rows, width = tokens.shape
    half = width // NCORE
    block = half // len(ORDER)

    def kernel(table_ref, tok_ref, grad_ref, own_ref, other_ref):
        for j in range(len(ORDER)):
            cols = slice(j * block, (j + 1) * block)
            for k, out in enumerate((own_ref, other_ref)):
                at = pl.multiple_of(table_ref[k * len(ORDER) + j] * block, block)
                out[0, :, cols] = tok_ref[:, pl.ds(at, block)]
                out[1, :, cols] = grad_ref[:, pl.ds(at, block)]

    shape = jax.ShapeDtypeStruct((2, rows, half), BF16)
    return call(
        kernel, (shape, shape), (table, tokens, out_grad), (vmem(), vmem()),
        [pl.BlockSpec(memory_space=pltpu.SMEM), vmem(), vmem()],
        moved=8 * rows * width, name="prep_tokens", limit=56 * 1024 * 1024,
    )


def prep_weights(gate, up, down):
    depth, width = gate.shape

    def kernel(gate_ref, up_ref, down_ref, out_ref):
        out_ref[:, :width] = gate_ref[...]
        out_ref[:, width : 2 * width] = up_ref[...]
        out_ref[:, 2 * width :] = down_ref[...].T

    return call(
        kernel, jax.ShapeDtypeStruct((depth, 3 * width), BF16), (gate, up, down), vmem(),
        [vmem()] * 3, moved=12 * depth * width, name="prep_weights",
    )


def start_all(copies):
    for c in copies:
        c.start()


def wait_all(copies):
    for c in copies:
        c.wait()


def forward(pieces, rows, weights, splits):
    shards = [x for x, _ in pieces]
    n_t, n_w = len(pieces), len(weights)
    half = shards[0].shape[2]
    depth, width3 = weights[0].shape
    width, width2 = width3 // 3, width3 // 3 * 2
    total = n_t * rows
    each = total // splits
    parts = 2
    per = n_w // parts

    def kernel(*refs):
        t_in, w_in = refs[:n_t], refs[n_t : n_t + n_w]
        outs, (rows_ref, tbuf, wbuf, acc, tsem, wsem, osem) = refs[n_t + n_w :][: 3 * splits], refs[n_t + n_w + 3 * splits :]
        t_copies = [
            pltpu.make_async_copy(
                r.at[:, pl.ds(pieces[i][1], rows)], tbuf.at[:, pl.ds(i * rows, rows)], tsem.at[i]
            )
            for i, r in enumerate(t_in)
        ]
        w_copies = [
            pltpu.make_async_copy(r, wbuf.at[pl.ds(j * depth, depth)], wsem.at[j])
            for j, r in enumerate(w_in)
        ]
        start_all(t_copies + w_copies)
        wait_all(t_copies)
        keep = pltpu.make_async_copy(tbuf, rows_ref, osem)
        keep.start()
        for p in range(parts):
            wait_all(w_copies[p * per : (p + 1) * per])
            ks = slice(p * per * depth, (p + 1) * per * depth)
            for k, cols in enumerate((slice(0, width2), slice(width2, width3))):
                term = jnp.dot(tbuf[k, :, ks], wbuf[ks, cols], preferred_element_type=F32)
                if p > 0:
                    term = term + acc[:, cols]
                if p < parts - 1:
                    acc[:, cols] = term
                else:
                    for i in range(term.shape[1] // width):
                        part = term[:, i * width : (i + 1) * width].astype(BF16)
                        for h in range(splits):
                            outs[3 * h + 2 * k + i][...] = part[h * each : (h + 1) * each]
        keep.wait()

    *partial, chunk = call(
        kernel,
        (jax.ShapeDtypeStruct((each, width), BF16),) * (3 * splits)
        + (jax.ShapeDtypeStruct((2, total, half), BF16),),
        (*shards, *weights), (vmem(),) * (3 * splits) + (hbm(),), [hbm()] * (n_t + n_w),
        scratch=(
            pltpu.VMEM((2, total, half), BF16),
            pltpu.VMEM((half, width3), BF16),
            pltpu.VMEM((total, width3), F32),
            pltpu.SemaphoreType.DMA((n_t,)),
            pltpu.SemaphoreType.DMA((n_w,)),
            pltpu.SemaphoreType.DMA,
        ),
        flops=2 * total * half * width3,
        moved=2 * (4 * total * half + half * width3 + total * width3),
        name="forward",
    )
    return partial, chunk


def activate(a, b, src, out, dst, step):
    width = a[0].shape[1]
    gate, up, grad = (p[src, :].astype(F32) + q[src, :].astype(F32) for p, q in zip(a, b, strict=True))
    s = 0.5 + 0.5 * jnp.tanh(0.5 * gate)
    act = gate * s
    out[dst, 2 * width :] = (act * up).astype(BF16)
    out[dst, :width] = (grad * up * s * (1.0 + gate * (1.0 - s))).astype(BF16)
    out[dst, width : 2 * width] = (grad * act).astype(BF16)


def activations(mine, other):
    rows, width = mine[0].shape
    count = len(mine)
    splits = count // 3
    step = 16

    def kernel(*refs):
        a, b, out_ref = refs[:count], refs[count : 2 * count], refs[2 * count]
        for h in range(splits):

            def one(i, _, h=h):
                src = pl.ds(pl.multiple_of(i * step, step), step)
                dst = pl.ds(pl.multiple_of(h * rows + i * step, step), step)
                activate(a[3 * h : 3 * h + 3], b[3 * h : 3 * h + 3], src, out_ref, dst, step)
                return 0

            lax.fori_loop(0, rows // step, one, 0)

    return call(
        kernel, jax.ShapeDtypeStruct((splits * rows, 3 * width), BF16), (*mine, *other), vmem(),
        [vmem()] * (2 * count), flops=30 * splits * rows * width, moved=18 * splits * rows * width,
        name="activations",
    )


def term_columns(acts, wbuf, qbuf, terms, osem, h, cols, depth, per, out, sem=0):
    for n in range(h * cols, (h + 1) * cols, depth):
        qbuf[:, n : n + depth] = lax.dot_general(
            acts[...], wbuf[n : n + depth, :], (((1,), (1,)), ((), ())), preferred_element_type=F32
        ).astype(BF16)
    for k, r in enumerate(terms):
        c = pltpu.make_async_copy(
            qbuf.at[pl.ds(k * per, per), pl.ds(h * cols, cols)],
            r.at[:, pl.ds(h * cols, cols)],
            osem.at[sem + h * len(terms) + k],
        )
        c.start()
        out.append(c)


def backward(mine, other, weights, pieces, scale, prev=(), chunks=(), count=0):
    n_w, n_p, n_c = len(weights), len(prev), len(chunks)
    rows, width = mine[0].shape
    width3 = 3 * width
    depth = weights[0].shape[0]
    half = n_w * depth
    per = rows // pieces
    prev_rows = [r.shape[0] for r in prev]
    starts = [sum(prev_rows[:i]) for i in range(n_p + 1)]
    total = starts[-1] + rows
    step = 16
    halves = 2

    def kernel(*refs):
        refs = list(refs)

        def take(n):
            got = refs[:n]
            del refs[:n]
            return got

        parts, w_in, prev_in, t_in = take(6), take(n_w), take(n_p), take(n_c)
        (acts_ref,), terms, grads = take(1), take(pieces), take(count)
        pbuf, abuf, wbuf, qbuf, tbuf, gbuf, psem, wsem, tsem, osem = refs
        here = starts[-1]
        bufs = [pbuf.at[k] for k in range(6)]
        p_copies = [pltpu.make_async_copy(r, pbuf.at[k], psem.at[k]) for k, r in enumerate(parts)]
        t_copies = [
            pltpu.make_async_copy(r, abuf.at[pl.ds(starts[i], prev_rows[i])], tsem.at[i])
            for i, r in enumerate(prev_in)
        ] + [
            pltpu.make_async_copy(
                r.at[:, :, pl.ds(0, count * depth)],
                tbuf.at[:, pl.ds(starts[i], r.shape[1])],
                tsem.at[n_p + i],
            )
            for i, r in enumerate(t_in)
        ]
        w_copies = [
            pltpu.make_async_copy(
                r.at[:, pl.ds(0, 2 * width)], wbuf.at[pl.ds(j * depth, depth)], wsem.at[j]
            )
            for j, r in enumerate(w_in)
        ]
        start_all(p_copies + t_copies + w_copies)
        wait_all(p_copies)

        def one(i, _):
            src = pl.ds(pl.multiple_of(i * step, step), step)
            dst = pl.ds(pl.multiple_of(here + i * step, step), step)
            activate(bufs[:3], bufs[3:], src, abuf, dst, step)
            return 0

        lax.fori_loop(0, rows // step, one, 0)
        out = [pltpu.make_async_copy(abuf.at[pl.ds(here, rows)], acts_ref, osem.at[0])]
        out[0].start()
        if count:
            wait_all(t_copies)
            weight_terms(abuf, tbuf, gbuf, grads, osem, 1, 0, count, scale, out)
        cols = half // halves
        for h in range(halves):
            wait_all(w_copies[h * n_w // halves : (h + 1) * n_w // halves])
            term_columns(
                abuf.at[pl.ds(here, rows), pl.ds(0, 2 * width)],
                wbuf, qbuf, terms, osem, h, cols, depth, per, out, 1 + count,
            )
        wait_all(out)

    shapes = (
        [jax.ShapeDtypeStruct((rows, width3), BF16)]
        + [jax.ShapeDtypeStruct((per, half), BF16)] * pieces
        + [jax.ShapeDtypeStruct((depth, width3), BF16)] * count
    )
    got = call(
        kernel, shapes, (*mine, *other, *weights, *prev, *chunks), [pinned()] * len(shapes),
        [hbm()] * (6 + n_w + n_p + n_c),
        scratch=(
            pltpu.VMEM((6, rows, width), BF16),
            pltpu.VMEM((total, width3), BF16),
            pltpu.VMEM((half, 2 * width), BF16),
            pltpu.VMEM((rows, half), BF16),
            pltpu.VMEM((2, total, max(count, 1) * depth), BF16),
            pltpu.VMEM((max(count, 1), depth, width3), BF16),
            pltpu.SemaphoreType.DMA((6,)),
            pltpu.SemaphoreType.DMA((n_w,)),
            pltpu.SemaphoreType.DMA((max(n_p + n_c, 1),)),
            pltpu.SemaphoreType.DMA((1 + count + halves * pieces,)),
        ),
        flops=4 * rows * half * width + 2 * total * count * depth * width3,
        moved=2 * (3 * rows * width3 + 2 * half * width + rows * half),
        name="backward",
    )
    return got[0], got[1 : 1 + pieces], got[1 + pieces :]


def weight_terms(abuf, tbuf, gbuf, grads, osem, sem, first, count, scale, out):
    depth, width3 = gbuf.shape[1:]
    width2 = width3 // 3 * 2
    dims = (((0,), (0,)), ((), ()))
    for j in range(first, first + count):
        cols = slice(j * depth, (j + 1) * depth)
        for k, w in enumerate((slice(0, width2), slice(width2, width3))):
            got = lax.dot_general(tbuf[k, :, cols], abuf[:, w], dims, preferred_element_type=F32)
            gbuf[j, :, w] = (got * scale).astype(BF16)
        c = pltpu.make_async_copy(gbuf.at[j], grads[j], osem.at[sem + j])
        c.start()
        out.append(c)


def weight_grads(acts, chunks, weights, pieces, first, count, scale):
    n_a, n_w = len(acts), len(weights)
    width3 = acts[0].shape[1]
    width2 = width3 // 3 * 2
    rows = [r.shape[0] for r in acts]
    starts = [sum(rows[:i]) for i in range(n_a)]
    half = chunks[0].shape[2]
    depth = half // len(ORDER)
    group = 2
    groups = [(g, min(group, count - g)) for g in range(0, count, group)]
    total = sum(rows)
    per = rows[0] // pieces

    def kernel(*refs):
        refs = list(refs)

        def take(n):
            got = refs[:n]
            del refs[:n]
            return got

        a_in, t_in, w_in, grads, terms = take(n_a), take(n_a), take(n_w), take(count), take(pieces)
        abuf, tbuf, gbuf, wbuf, qbuf, asem, tsem, wsem, osem = refs
        a_copies = [
            pltpu.make_async_copy(r, abuf.at[pl.ds(starts[i], rows[i])], asem.at[i])
            for i, r in enumerate(a_in)
        ]
        t_copies = [
            [
                pltpu.make_async_copy(
                    r.at[:, :, pl.ds((first + g) * depth, size * depth)],
                    tbuf.at[:, pl.ds(starts[i], rows[i]), pl.ds(g * depth, size * depth)],
                    tsem.at[k * n_a + i],
                )
                for i, r in enumerate(t_in)
            ]
            for k, (g, size) in enumerate(groups)
        ]
        w_copies = [
            pltpu.make_async_copy(
                r.at[:, pl.ds(0, width2)], wbuf.at[pl.ds(j * depth, depth)], wsem.at[j]
            )
            for j, r in enumerate(w_in)
        ]
        start_all(a_copies)
        for g in t_copies:
            start_all(g)
        start_all(w_copies)
        wait_all(a_copies)
        out = []
        for k, (g, size) in enumerate(groups):
            wait_all(t_copies[k])
            weight_terms(abuf, tbuf, gbuf, grads, osem, 0, g, size, scale, out)
        wait_all(w_copies)
        for h in range(2):
            term_columns(
                abuf.at[pl.ds(0, rows[0]), pl.ds(0, width2)],
                wbuf, qbuf, terms, osem, h, half // 2, depth, per, out, count,
            )
        wait_all(out)

    shapes = [jax.ShapeDtypeStruct((depth, width3), BF16)] * count + [
        jax.ShapeDtypeStruct((per, half), BF16)
    ] * pieces
    got = call(
        kernel, shapes, (*acts, *chunks, *weights), [pinned()] * len(shapes), [pinned()] * (2 * n_a + n_w),
        scratch=(
            pltpu.VMEM((total, width3), BF16),
            pltpu.VMEM((2, total, count * depth), BF16),
            pltpu.VMEM((count, depth, width3), BF16),
            pltpu.VMEM((half, width2), BF16),
            pltpu.VMEM((rows[0], half), BF16),
            pltpu.SemaphoreType.DMA((n_a,)),
            pltpu.SemaphoreType.DMA((len(groups) * n_a,)),
            pltpu.SemaphoreType.DMA((n_w,)),
            pltpu.SemaphoreType.DMA((count + 2 * pieces,)),
        ),
        flops=2 * total * count * depth * width3 + 2 * rows[0] * half * width2,
        moved=2 * (total * width3 + 2 * total * count * depth + count * depth * width3),
        name="weight_grads",
    )
    return got[:count], got[count:]


def tie(*arrays):
    return lax.optimization_barrier(arrays)


def add(*terms):
    total = terms[0].astype(F32)
    for t in terms[1:]:
        total = total + t.astype(F32)
    return total.astype(BF16)


def finish_weights(*terms):
    depth, width3 = terms[0].shape
    width = width3 // 3

    def kernel(*refs):
        terms_in, (gate_ref, up_ref, down_ref) = refs[:-3], refs[-3:]

        def total(k):
            cols = slice(k * width, (k + 1) * width)
            return sum(r[:, cols].astype(F32) for r in terms_in).astype(BF16)

        gate_ref[...] = total(0)
        up_ref[...] = total(1)
        down_ref[...] = total(2).T

    shapes = [jax.ShapeDtypeStruct(s, BF16) for s in ((depth, width), (depth, width), (width, depth))]
    return call(
        kernel, shapes, terms, [vmem()] * 3, [vmem()] * len(terms),
        moved=40 * depth * width, name="finish_weights",
    )


def finish_tokens(table, own, other):
    rows, half = own[0].shape
    block = half // len(ORDER)

    def kernel(table_ref, a_ref, b_ref, c_ref, d_ref, out_ref):
        for j in range(len(ORDER)):
            cols = slice(j * block, (j + 1) * block)
            for k, (p, q) in enumerate(((a_ref, b_ref), (c_ref, d_ref))):
                at = pl.multiple_of(table_ref[k * len(ORDER) + j] * block, block)
                total = p[:, cols].astype(F32) + q[:, cols].astype(F32)
                out_ref[:, pl.ds(at, block)] = total.astype(BF16)

    return call(
        kernel, jax.ShapeDtypeStruct((rows, NCORE * half), BF16), (table, *own, *other), vmem(),
        [pl.BlockSpec(memory_space=pltpu.SMEM)] + [vmem()] * 4,
        moved=12 * rows * half, name="finish_tokens",
    )


def body(tokens, out_grad, gate_weight, up_weight, down_weight):
    rows = tokens.shape[0]
    scale = 1.0 / math.sqrt(rows * lax.axis_size("tensor") * lax.axis_size("dw"))
    dw = lax.axis_index("dw")
    core, y, xh = dw % NCORE, dw // NCORE % NY, dw // (NCORE * NY)
    table = jnp.stack(
        [
            (((xh + dx) % NXH) * NY + (y + dy) % NY) * NCORE + c
            for c in (core, 1 - core)
            for dx, dy in ORDER
        ]
    ).astype(jnp.int32)

    own_part, other_part = prep_tokens(table, tokens, out_grad)
    got = swap_core(other_part)
    low = jnp.where(core == 0, own_part, got)
    high = jnp.where(core == 0, got, own_part)
    a = {0: jnp.concatenate([low, high], axis=1)}
    w = {(0, 0): prep_weights(gate_weight, up_weight, down_weight)}

    n = NCORE * rows
    a[1], a[7] = z_down(a[0]), z_up(a[0])
    b = {0: swap_xl(a[0])}
    w[1, 0], w[0, 1], w[0, 3] = swap_xh(w[0, 0]), y_down(w[0, 0]), y_up(w[0, 0])
    a2b1 = z_down(jnp.concatenate([a[1], b[0]], axis=1))
    a6b7 = z_up(jnp.concatenate([a[7], b[0]], axis=1))
    a2b1, a6b7, w10, w01, w03 = tie(a2b1, a6b7, w[1, 0], w[0, 1], w[0, 3])
    a3b2, a5b6 = z_down(a2b1), z_up(a6b7)
    w[1, 1], w[1, 3], w[0, 2] = swap_xh(w01), y_up(w10), y_down(w01)
    a3b2, a5b6, w13, w11, w[0, 2] = tie(a3b2, a5b6, w[1, 3], w[1, 1], w[0, 2])
    w[1, 1], w[1, 3] = w11, w13
    k = w13.shape[0] // 2
    w[1, 2] = jnp.concatenate([y_up(w13[:k]), y_down(w11[k:])])
    a4b3, b[5] = z_down(a3b2), z_up(a5b6[:, n:])
    b[4] = move_tensor(a5b6[:, :n], lambda xl, z: (xl + 1, z + 1))
    weights = [w[k] for k in ORDER]

    early = [
        (a[0], 0), (b[0], 0), (a[1], 0), (a2b1, n), (a[7], 0), (a6b7, n), (a2b1, 0), (a3b2, n), (a6b7, 0), (a5b6, n)
    ]
    late = [(a3b2, 0), (a4b3, n), (a5b6, 0), (b[5], 0), (a4b3, 0), (b[4], 0)]
    part1, rows1 = forward(early, n, weights, 2)
    other1 = [swap_core(x) for x in part1]
    part2, rows2 = forward(late, n, weights, 1)
    other2 = [swap_core(x) for x in part2]
    acts1 = activations(part1, other1)
    acts2, terms2, first = backward(
        part2, other2, weights, len(CHUNKS[1]), scale, prev=(acts1,), chunks=(rows1, rows2), count=FIRST
    )
    rest, terms1 = weight_grads(
        (acts1, acts2), (rows1, rows2), weights, len(CHUNKS[0]), FIRST, len(ORDER) - FIRST, scale
    )
    terms = dict(zip(CHUNKS[0] + CHUNKS[1], [*terms1, *terms2], strict=True))

    p = dict(zip(ORDER, [*first, *rest], strict=True))
    r02 = y_up(p[0, 2])
    r12 = y_down(p[1, 2])
    r10 = swap_xh(p[1, 0])
    r11 = move_dw(p[1, 1], lambda xh, y, c: (xh + 1, y + 1, c))
    r03 = y_down(p[0, 3])
    p01, p13, _, _ = tie(add(p[0, 1], r02), add(p[1, 3], r12), r11, r03)
    r01 = y_up(p01)
    r13 = move_dw(p13, lambda xh, y, c: (xh + 1, y - 1, c))

    up = z_up(terms[4][:n])
    down = z_down(terms[4][n:])
    up = z_up(terms[3].at[:n].set(add(terms[3][:n], up)))
    down = z_down(terms[5].at[n:].set(add(terms[5][n:], down)))
    up, down, *_ = tie(up, down, r02, r12, r10)
    up = z_up(add(terms[2], up))
    down = z_down(add(terms[6], down))
    up, down, *_ = tie(up, down, r11, r03)
    up = z_up(add(terms[1], up))
    down = z_down(add(terms[7], down))
    total = add(terms[0], up, down).reshape(NXL, NCORE, rows, -1)
    low, high = total[:, 0], total[:, 1]
    mine = jnp.where(core == 0, low, high)
    theirs = jnp.where(core == 0, high, low)
    grad_tokens = finish_tokens(
        table,
        (mine[0], swap_xl(mine[1])),
        (
            swap_core(theirs[0]),
            move_all(theirs[1], lambda xl, z, xh, y, c: (xl + 1, z, xh, y, c + 1)),
        ),
    )
    grad_tokens, r01, r13 = tie(grad_tokens, r01, r13)
    grads = finish_weights(p[0, 0], r10, r11, r03, r01, r13)
    return (grad_tokens, *grads)


def solution(mesh):
    placed = (
        P(("tensor", "dw"), None),
        P(("tensor", "dw"), None),
        P("dw", "tensor"),
        P("dw", "tensor"),
        P("tensor", "dw"),
    )
    return jax.shard_map(
        body,
        mesh=mesh,
        in_specs=placed,
        out_specs=(
            P(("tensor", "dw"), None),
            P("dw", "tensor"),
            P("dw", "tensor"),
            P("tensor", "dw"),
        ),
        check_vma=False,
    )
```

```python
import functools
import itertools
import math

import jax
import jax.numpy as jnp
from jax import lax
from jax.experimental import pallas as pl
from jax.experimental.pallas import tpu as pltpu
from jax.sharding import PartitionSpec as P

NXL, NZ, NXH, NY, NCORE = 2, 8, 2, 4, 2
BF16, F32 = jnp.bfloat16, jnp.float32
VMEM_LIMIT = 20 * 1024 * 1024

ORDER = ((0, 2), (1, 2), (1, 0), (1, 1), (0, 3), (0, 1), (1, 3), (0, 0))
FIRST = 4
CHUNKS = ((0, 1, 7, 2, 6), (3, 5, 4))


def move_tensor(x, dest):
    perm = []
    for xl in range(NXL):
        for z in range(NZ):
            a, b = dest(xl, z)
            perm.append((xl * NZ + z, a % NXL * NZ + b % NZ))
    return lax.ppermute(x, "tensor", perm)


def move_dw(x, dest):
    perm = []
    for xh in range(NXH):
        for y in range(NY):
            for c in range(NCORE):
                a, b, e = dest(xh, y, c)
                perm.append(
                    ((xh * NY + y) * NCORE + c, (a % NXH * NY + b % NY) * NCORE + e % NCORE)
                )
    return lax.ppermute(x, "dw", perm)


def move_all(x, dest):
    sizes = (NXL, NZ, NXH, NY, NCORE)
    perm = []
    for at in itertools.product(*map(range, sizes)):
        ends = at, dest(*at)
        source, target = (
            functools.reduce(lambda n, e: n * e[1] + e[0] % e[1], zip(end, sizes), 0) for end in ends
        )
        perm.append((source, target))
    return lax.ppermute(x, ("tensor", "dw"), perm)


def z_up(x):
    return move_tensor(x, lambda xl, z: (xl, z + 1))


def z_down(x):
    return move_tensor(x, lambda xl, z: (xl, z - 1))


def swap_xl(x):
    return move_tensor(x, lambda xl, z: (xl + 1, z))


def y_up(x):
    return move_dw(x, lambda xh, y, c: (xh, y + 1, c))


def y_down(x):
    return move_dw(x, lambda xh, y, c: (xh, y - 1, c))


def swap_xh(x):
    return move_dw(x, lambda xh, y, c: (xh + 1, y, c))


def swap_core(x):
    return move_dw(x, lambda xh, y, c: (xh, y, c + 1))


def vmem():
    return pl.BlockSpec(memory_space=pltpu.VMEM)


def hbm():
    return pl.BlockSpec(memory_space=pl.ANY)


def pinned():
    return pl.BlockSpec(memory_space=pltpu.HBM)


def call(kernel, outs, ins, out_specs, in_specs, scratch=(), flops=0, moved=0, name=None, limit=VMEM_LIMIT):
    return pl.pallas_call(
        kernel,
        out_shape=outs,
        in_specs=in_specs,
        out_specs=out_specs,
        scratch_shapes=list(scratch),
        compiler_params=pltpu.CompilerParams(vmem_limit_bytes=limit),
        cost_estimate=pl.CostEstimate(flops=0, bytes_accessed=1024, transcendentals=0),
        name=name,
    )(*ins)


def prep_tokens(table, tokens, out_grad):
    rows, width = tokens.shape
    half = width // NCORE
    block = half // len(ORDER)

    def kernel(table_ref, tok_ref, grad_ref, own_ref, other_ref):
        for j in range(len(ORDER)):
            cols = slice(j * block, (j + 1) * block)
            for k, out in enumerate((own_ref, other_ref)):
                at = pl.multiple_of(table_ref[k * len(ORDER) + j] * block, block)
                out[0, :, cols] = tok_ref[:, pl.ds(at, block)]
                out[1, :, cols] = grad_ref[:, pl.ds(at, block)]

    shape = jax.ShapeDtypeStruct((2, rows, half), BF16)
    return call(
        kernel, (shape, shape), (table, tokens, out_grad), (vmem(), vmem()),
        [pl.BlockSpec(memory_space=pltpu.SMEM), vmem(), vmem()],
        moved=8 * rows * width, name="prep_tokens", limit=56 * 1024 * 1024,
    )


def prep_weights(gate, up, down):
    depth, width = gate.shape

    def kernel(gate_ref, up_ref, down_ref, out_ref):
        out_ref[:, :width] = gate_ref[...]
        out_ref[:, width : 2 * width] = up_ref[...]
        out_ref[:, 2 * width :] = down_ref[...].T

    return call(
        kernel, jax.ShapeDtypeStruct((depth, 3 * width), BF16), (gate, up, down), vmem(),
        [vmem()] * 3, moved=12 * depth * width, name="prep_weights",
    )


def start_all(copies):
    for c in copies:
        c.start()


def wait_all(copies):
    for c in copies:
        c.wait()


def forward(pieces, rows, weights, splits):
    shards = [x for x, _ in pieces]
    n_t, n_w = len(pieces), len(weights)
    half = shards[0].shape[2]
    depth, width3 = weights[0].shape
    width, width2 = width3 // 3, width3 // 3 * 2
    total = n_t * rows
    each = total // splits
    parts = 2
    per = n_w // parts

    def kernel(*refs):
        t_in, w_in = refs[:n_t], refs[n_t : n_t + n_w]
        outs, (rows_ref, tbuf, wbuf, acc, tsem, wsem, osem) = refs[n_t + n_w :][: 3 * splits], refs[n_t + n_w + 3 * splits :]
        t_copies = [
            pltpu.make_async_copy(
                r.at[:, pl.ds(pieces[i][1], rows)], tbuf.at[:, pl.ds(i * rows, rows)], tsem.at[i]
            )
            for i, r in enumerate(t_in)
        ]
        w_copies = [
            pltpu.make_async_copy(r, wbuf.at[pl.ds(j * depth, depth)], wsem.at[j])
            for j, r in enumerate(w_in)
        ]
        start_all(t_copies + w_copies)
        wait_all(t_copies)
        keep = pltpu.make_async_copy(tbuf, rows_ref, osem)
        keep.start()
        for p in range(parts):
            wait_all(w_copies[p * per : (p + 1) * per])
            ks = slice(p * per * depth, (p + 1) * per * depth)
            for k, cols in enumerate((slice(0, width2), slice(width2, width3))):
                term = jnp.dot(tbuf[k, :, ks], wbuf[ks, cols], preferred_element_type=F32)
                if p > 0:
                    term = term + acc[:, cols]
                if p < parts - 1:
                    acc[:, cols] = term
                else:
                    for i in range(term.shape[1] // width):
                        part = term[:, i * width : (i + 1) * width].astype(BF16)
                        for h in range(splits):
                            outs[3 * h + 2 * k + i][...] = part[h * each : (h + 1) * each]
        keep.wait()

    *partial, chunk = call(
        kernel,
        (jax.ShapeDtypeStruct((each, width), BF16),) * (3 * splits)
        + (jax.ShapeDtypeStruct((2, total, half), BF16),),
        (*shards, *weights), (vmem(),) * (3 * splits) + (hbm(),), [hbm()] * (n_t + n_w),
        scratch=(
            pltpu.VMEM((2, total, half), BF16),
            pltpu.VMEM((half, width3), BF16),
            pltpu.VMEM((total, width3), F32),
            pltpu.SemaphoreType.DMA((n_t,)),
            pltpu.SemaphoreType.DMA((n_w,)),
            pltpu.SemaphoreType.DMA,
        ),
        flops=2 * total * half * width3,
        moved=2 * (4 * total * half + half * width3 + total * width3),
        name="forward",
    )
    return partial, chunk


def activate(a, b, src, out, dst, step):
    width = a[0].shape[1]
    gate, up, grad = (p[src, :].astype(F32) + q[src, :].astype(F32) for p, q in zip(a, b, strict=True))
    s = 0.5 + 0.5 * jnp.tanh(0.5 * gate)
    act = gate * s
    out[dst, 2 * width :] = (act * up).astype(BF16)
    out[dst, :width] = (grad * up * s * (1.0 + gate * (1.0 - s))).astype(BF16)
    out[dst, width : 2 * width] = (grad * act).astype(BF16)


def activations(mine, other):
    rows, width = mine[0].shape
    count = len(mine)
    splits = count // 3
    step = 16

    def kernel(*refs):
        a, b, out_ref = refs[:count], refs[count : 2 * count], refs[2 * count]
        for h in range(splits):

            def one(i, _, h=h):
                src = pl.ds(pl.multiple_of(i * step, step), step)
                dst = pl.ds(pl.multiple_of(h * rows + i * step, step), step)
                activate(a[3 * h : 3 * h + 3], b[3 * h : 3 * h + 3], src, out_ref, dst, step)
                return 0

            lax.fori_loop(0, rows // step, one, 0)

    return call(
        kernel, jax.ShapeDtypeStruct((splits * rows, 3 * width), BF16), (*mine, *other), vmem(),
        [vmem()] * (2 * count), flops=30 * splits * rows * width, moved=18 * splits * rows * width,
        name="activations",
    )


def term_columns(acts, wbuf, qbuf, terms, osem, h, cols, depth, per, out, sem=0):
    for n in range(h * cols, (h + 1) * cols, depth):
        qbuf[:, n : n + depth] = lax.dot_general(
            acts[...], wbuf[n : n + depth, :], (((1,), (1,)), ((), ())), preferred_element_type=F32
        ).astype(BF16)
    for k, r in enumerate(terms):
        c = pltpu.make_async_copy(
            qbuf.at[pl.ds(k * per, per), pl.ds(h * cols, cols)],
            r.at[:, pl.ds(h * cols, cols)],
            osem.at[sem + h * len(terms) + k],
        )
        c.start()
        out.append(c)


def backward(mine, other, weights, pieces, scale, prev=(), chunks=(), count=0):
    n_w, n_p, n_c = len(weights), len(prev), len(chunks)
    rows, width = mine[0].shape
    width3 = 3 * width
    depth = weights[0].shape[0]
    half = n_w * depth
    per = rows // pieces
    prev_rows = [r.shape[0] for r in prev]
    starts = [sum(prev_rows[:i]) for i in range(n_p + 1)]
    total = starts[-1] + rows
    step = 16
    halves = 2

    def kernel(*refs):
        refs = list(refs)

        def take(n):
            got = refs[:n]
            del refs[:n]
            return got

        parts, w_in, prev_in, t_in = take(6), take(n_w), take(n_p), take(n_c)
        (acts_ref,), terms, grads = take(1), take(pieces), take(count)
        pbuf, abuf, wbuf, qbuf, tbuf, gbuf, psem, wsem, tsem, osem = refs
        here = starts[-1]
        bufs = [pbuf.at[k] for k in range(6)]
        p_copies = [pltpu.make_async_copy(r, pbuf.at[k], psem.at[k]) for k, r in enumerate(parts)]
        t_copies = [
            pltpu.make_async_copy(r, abuf.at[pl.ds(starts[i], prev_rows[i])], tsem.at[i])
            for i, r in enumerate(prev_in)
        ] + [
            pltpu.make_async_copy(
                r.at[:, :, pl.ds(0, count * depth)],
                tbuf.at[:, pl.ds(starts[i], r.shape[1])],
                tsem.at[n_p + i],
            )
            for i, r in enumerate(t_in)
        ]
        w_copies = [
            pltpu.make_async_copy(
                r.at[:, pl.ds(0, 2 * width)], wbuf.at[pl.ds(j * depth, depth)], wsem.at[j]
            )
            for j, r in enumerate(w_in)
        ]
        start_all(p_copies + t_copies + w_copies)
        wait_all(p_copies)

        def one(i, _):
            src = pl.ds(pl.multiple_of(i * step, step), step)
            dst = pl.ds(pl.multiple_of(here + i * step, step), step)
            activate(bufs[:3], bufs[3:], src, abuf, dst, step)
            return 0

        lax.fori_loop(0, rows // step, one, 0)
        out = [pltpu.make_async_copy(abuf.at[pl.ds(here, rows)], acts_ref, osem.at[0])]
        out[0].start()
        if count:
            wait_all(t_copies)
            weight_terms(abuf, tbuf, gbuf, grads, osem, 1, 0, count, scale, out)
        cols = half // halves
        for h in range(halves):
            wait_all(w_copies[h * n_w // halves : (h + 1) * n_w // halves])
            term_columns(
                abuf.at[pl.ds(here, rows), pl.ds(0, 2 * width)],
                wbuf, qbuf, terms, osem, h, cols, depth, per, out, 1 + count,
            )
        wait_all(out)

    shapes = (
        [jax.ShapeDtypeStruct((rows, width3), BF16)]
        + [jax.ShapeDtypeStruct((per, half), BF16)] * pieces
        + [jax.ShapeDtypeStruct((depth, width3), BF16)] * count
    )
    got = call(
        kernel, shapes, (*mine, *other, *weights, *prev, *chunks), [pinned()] * len(shapes),
        [hbm()] * (6 + n_w + n_p + n_c),
        scratch=(
            pltpu.VMEM((6, rows, width), BF16),
            pltpu.VMEM((total, width3), BF16),
            pltpu.VMEM((half, 2 * width), BF16),
            pltpu.VMEM((rows, half), BF16),
            pltpu.VMEM((2, total, max(count, 1) * depth), BF16),
            pltpu.VMEM((max(count, 1), depth, width3), BF16),
            pltpu.SemaphoreType.DMA((6,)),
            pltpu.SemaphoreType.DMA((n_w,)),
            pltpu.SemaphoreType.DMA((max(n_p + n_c, 1),)),
            pltpu.SemaphoreType.DMA((1 + count + halves * pieces,)),
        ),
        flops=4 * rows * half * width + 2 * total * count * depth * width3,
        moved=2 * (3 * rows * width3 + 2 * half * width + rows * half),
        name="backward",
    )
    return got[0], got[1 : 1 + pieces], got[1 + pieces :]


def weight_terms(abuf, tbuf, gbuf, grads, osem, sem, first, count, scale, out):
    depth, width3 = gbuf.shape[1:]
    width2 = width3 // 3 * 2
    dims = (((0,), (0,)), ((), ()))
    for j in range(first, first + count):
        cols = slice(j * depth, (j + 1) * depth)
        for k, w in enumerate((slice(0, width2), slice(width2, width3))):
            got = lax.dot_general(tbuf[k, :, cols], abuf[:, w], dims, preferred_element_type=F32)
            gbuf[j, :, w] = (got * scale).astype(BF16)
        c = pltpu.make_async_copy(gbuf.at[j], grads[j], osem.at[sem + j])
        c.start()
        out.append(c)


def weight_grads(acts, chunks, weights, pieces, first, count, scale):
    n_a, n_w = len(acts), len(weights)
    width3 = acts[0].shape[1]
    width2 = width3 // 3 * 2
    rows = [r.shape[0] for r in acts]
    starts = [sum(rows[:i]) for i in range(n_a)]
    half = chunks[0].shape[2]
    depth = half // len(ORDER)
    group = 2
    groups = [(g, min(group, count - g)) for g in range(0, count, group)]
    total = sum(rows)
    per = rows[0] // pieces

    def kernel(*refs):
        refs = list(refs)

        def take(n):
            got = refs[:n]
            del refs[:n]
            return got

        a_in, t_in, w_in, grads, terms = take(n_a), take(n_a), take(n_w), take(count), take(pieces)
        abuf, tbuf, gbuf, wbuf, qbuf, asem, tsem, wsem, osem = refs
        a_copies = [
            pltpu.make_async_copy(r, abuf.at[pl.ds(starts[i], rows[i])], asem.at[i])
            for i, r in enumerate(a_in)
        ]
        t_copies = [
            [
                pltpu.make_async_copy(
                    r.at[:, :, pl.ds((first + g) * depth, size * depth)],
                    tbuf.at[:, pl.ds(starts[i], rows[i]), pl.ds(g * depth, size * depth)],
                    tsem.at[k * n_a + i],
                )
                for i, r in enumerate(t_in)
            ]
            for k, (g, size) in enumerate(groups)
        ]
        w_copies = [
            pltpu.make_async_copy(
                r.at[:, pl.ds(0, width2)], wbuf.at[pl.ds(j * depth, depth)], wsem.at[j]
            )
            for j, r in enumerate(w_in)
        ]
        start_all(a_copies)
        for g in t_copies:
            start_all(g)
        start_all(w_copies)
        wait_all(a_copies)
        out = []
        for k, (g, size) in enumerate(groups):
            wait_all(t_copies[k])
            weight_terms(abuf, tbuf, gbuf, grads, osem, 0, g, size, scale, out)
        wait_all(w_copies)
        for h in range(2):
            term_columns(
                abuf.at[pl.ds(0, rows[0]), pl.ds(0, width2)],
                wbuf, qbuf, terms, osem, h, half // 2, depth, per, out, count,
            )
        wait_all(out)

    shapes = [jax.ShapeDtypeStruct((depth, width3), BF16)] * count + [
        jax.ShapeDtypeStruct((per, half), BF16)
    ] * pieces
    got = call(
        kernel, shapes, (*acts, *chunks, *weights), [pinned()] * len(shapes), [pinned()] * (2 * n_a + n_w),
        scratch=(
            pltpu.VMEM((total, width3), BF16),
            pltpu.VMEM((2, total, count * depth), BF16),
            pltpu.VMEM((count, depth, width3), BF16),
            pltpu.VMEM((half, width2), BF16),
            pltpu.VMEM((rows[0], half), BF16),
            pltpu.SemaphoreType.DMA((n_a,)),
            pltpu.SemaphoreType.DMA((len(groups) * n_a,)),
            pltpu.SemaphoreType.DMA((n_w,)),
            pltpu.SemaphoreType.DMA((count + 2 * pieces,)),
        ),
        flops=2 * total * count * depth * width3 + 2 * rows[0] * half * width2,
        moved=2 * (total * width3 + 2 * total * count * depth + count * depth * width3),
        name="weight_grads",
    )
    return got[:count], got[count:]


def tie(*arrays):
    return lax.optimization_barrier(arrays)


def add(*terms):
    total = terms[0].astype(F32)
    for t in terms[1:]:
        total = total + t.astype(F32)
    return total.astype(BF16)


def finish_weights(*terms):
    depth, width3 = terms[0].shape
    width = width3 // 3

    def kernel(*refs):
        terms_in, (gate_ref, up_ref, down_ref) = refs[:-3], refs[-3:]

        def total(k):
            cols = slice(k * width, (k + 1) * width)
            return sum(r[:, cols].astype(F32) for r in terms_in).astype(BF16)

        gate_ref[...] = total(0)
        up_ref[...] = total(1)
        down_ref[...] = total(2).T

    shapes = [jax.ShapeDtypeStruct(s, BF16) for s in ((depth, width), (depth, width), (width, depth))]
    return call(
        kernel, shapes, terms, [vmem()] * 3, [vmem()] * len(terms),
        moved=40 * depth * width, name="finish_weights",
    )


def finish_tokens(table, own, other):
    rows, half = own[0].shape
    block = half // len(ORDER)

    def kernel(table_ref, a_ref, b_ref, c_ref, d_ref, out_ref):
        for j in range(len(ORDER)):
            cols = slice(j * block, (j + 1) * block)
            for k, (p, q) in enumerate(((a_ref, b_ref), (c_ref, d_ref))):
                at = pl.multiple_of(table_ref[k * len(ORDER) + j] * block, block)
                total = p[:, cols].astype(F32) + q[:, cols].astype(F32)
                out_ref[:, pl.ds(at, block)] = total.astype(BF16)

    return call(
        kernel, jax.ShapeDtypeStruct((rows, NCORE * half), BF16), (table, *own, *other), vmem(),
        [pl.BlockSpec(memory_space=pltpu.SMEM)] + [vmem()] * 4,
        moved=12 * rows * half, name="finish_tokens",
    )


def body(tokens, out_grad, gate_weight, up_weight, down_weight):
    rows = tokens.shape[0]
    scale = 1.0 / math.sqrt(rows * lax.axis_size("tensor") * lax.axis_size("dw"))
    dw = lax.axis_index("dw")
    core, y, xh = dw % NCORE, dw // NCORE % NY, dw // (NCORE * NY)
    table = jnp.stack(
        [
            (((xh + dx) % NXH) * NY + (y + dy) % NY) * NCORE + c
            for c in (core, 1 - core)
            for dx, dy in ORDER
        ]
    ).astype(jnp.int32)

    own_part, other_part = prep_tokens(table, tokens, out_grad)
    got = swap_core(other_part)
    low = jnp.where(core == 0, own_part, got)
    high = jnp.where(core == 0, got, own_part)
    a = {0: jnp.concatenate([low, high], axis=1)}
    w = {(0, 0): prep_weights(gate_weight, up_weight, down_weight)}

    n = NCORE * rows
    a[1], a[7] = z_down(a[0]), z_up(a[0])
    b = {0: swap_xl(a[0])}
    w[1, 0], w[0, 1], w[0, 3] = swap_xh(w[0, 0]), y_down(w[0, 0]), y_up(w[0, 0])
    w[1, 2] = move_dw(w[0, 0], lambda xh, y, c: (xh + 1, y + 2, c))
    a2b1 = z_down(jnp.concatenate([a[1], b[0]], axis=1))
    a6b7 = z_up(jnp.concatenate([a[7], b[0]], axis=1))
    w10 = w[1, 0]
    a2b1, a6b7, w01, w03, w[1, 2] = tie(a2b1, a6b7, w[0, 1], w[0, 3], w[1, 2])
    a3b2, a5b6 = z_down(a2b1), z_up(a6b7)
    w[1, 1], w[1, 3], w[0, 2] = swap_xh(w01), y_up(w10), y_down(w01)
    a4b3, b[5] = z_down(a3b2), z_up(a5b6[:, n:])
    b[4] = move_tensor(a5b6[:, :n], lambda xl, z: (xl + 1, z + 1))
    weights = [w[k] for k in ORDER]

    early = [
        (a[0], 0), (b[0], 0), (a[1], 0), (a2b1, n), (a[7], 0), (a6b7, n), (a2b1, 0), (a3b2, n), (a6b7, 0), (a5b6, n)
    ]
    late = [(a3b2, 0), (a4b3, n), (a5b6, 0), (b[5], 0), (a4b3, 0), (b[4], 0)]
    part1, rows1 = forward(early, n, weights, 2)
    other1 = [swap_core(x) for x in part1]
    part2, rows2 = forward(late, n, weights, 1)
    other2 = [swap_core(x) for x in part2]
    acts1 = activations(part1, other1)
    acts2, terms2, first = backward(
        part2, other2, weights, len(CHUNKS[1]), scale, prev=(acts1,), chunks=(rows1, rows2), count=FIRST
    )
    rest, terms1 = weight_grads(
        (acts1, acts2), (rows1, rows2), weights, len(CHUNKS[0]), FIRST, len(ORDER) - FIRST, scale
    )
    terms = dict(zip(CHUNKS[0] + CHUNKS[1], [*terms1, *terms2], strict=True))

    p = dict(zip(ORDER, [*first, *rest], strict=True))
    r02 = y_up(p[0, 2])
    r12 = y_down(p[1, 2])
    r10 = swap_xh(p[1, 0])
    r11 = move_dw(p[1, 1], lambda xh, y, c: (xh + 1, y + 1, c))
    r03 = y_down(p[0, 3])
    r01 = y_up(add(p[0, 1], r02))
    r13 = move_dw(add(p[1, 3], r12), lambda xh, y, c: (xh + 1, y - 1, c))

    up = z_up(terms[4][:n])
    down = z_down(terms[4][n:])
    up = z_up(terms[3].at[:n].set(add(terms[3][:n], up)))
    down = z_down(terms[5].at[n:].set(add(terms[5][n:], down)))
    up, down, *_ = tie(up, down, r02, r12, r10, r11)
    up = z_up(add(terms[2], up))
    down = z_down(add(terms[6], down))
    up, down, *_ = tie(up, down, r03)
    up = z_up(add(terms[1], up))
    down = z_down(add(terms[7], down))
    up, down, *_ = tie(up, down, r01, r13)
    total = add(terms[0], up, down).reshape(NXL, NCORE, rows, -1)
    low, high = total[:, 0], total[:, 1]
    mine = jnp.where(core == 0, low, high)
    theirs = jnp.where(core == 0, high, low)
    grad_tokens = finish_tokens(
        table,
        (mine[0], swap_xl(mine[1])),
        (
            swap_core(theirs[0]),
            move_all(theirs[1], lambda xl, z, xh, y, c: (xl + 1, z, xh, y, c + 1)),
        ),
    )
    grads = finish_weights(p[0, 0], r10, r11, r03, r01, r13)
    return (grad_tokens, *grads)


def solution(mesh):
    placed = (
        P(("tensor", "dw"), None),
        P(("tensor", "dw"), None),
        P("dw", "tensor"),
        P("dw", "tensor"),
        P("tensor", "dw"),
    )
    return jax.shard_map(
        body,
        mesh=mesh,
        in_specs=placed,
        out_specs=(
            P(("tensor", "dw"), None),
            P("dw", "tensor"),
            P("dw", "tensor"),
            P("tensor", "dw"),
        ),
        check_vma=False,
    )
```

```python
import functools
import itertools
import math

import jax
import jax.numpy as jnp
from jax import lax
from jax.experimental import pallas as pl
from jax.experimental.pallas import tpu as pltpu
from jax.sharding import PartitionSpec as P

NXL, NZ, NXH, NY, NCORE = 2, 8, 2, 4, 2
BF16, F32 = jnp.bfloat16, jnp.float32
VMEM_LIMIT = 20 * 1024 * 1024

ORDER = ((0, 2), (1, 2), (1, 0), (1, 1), (0, 3), (0, 1), (1, 3), (0, 0))
FIRST = 3
CHUNKS = ((0, 1, 7, 2, 6), (3, 5, 4))


def move_tensor(x, dest):
    perm = []
    for xl in range(NXL):
        for z in range(NZ):
            a, b = dest(xl, z)
            perm.append((xl * NZ + z, a % NXL * NZ + b % NZ))
    return lax.ppermute(x, "tensor", perm)


def move_dw(x, dest):
    perm = []
    for xh in range(NXH):
        for y in range(NY):
            for c in range(NCORE):
                a, b, e = dest(xh, y, c)
                perm.append(
                    ((xh * NY + y) * NCORE + c, (a % NXH * NY + b % NY) * NCORE + e % NCORE)
                )
    return lax.ppermute(x, "dw", perm)


def move_all(x, dest):
    sizes = (NXL, NZ, NXH, NY, NCORE)
    perm = []
    for at in itertools.product(*map(range, sizes)):
        ends = at, dest(*at)
        source, target = (
            functools.reduce(lambda n, e: n * e[1] + e[0] % e[1], zip(end, sizes), 0) for end in ends
        )
        perm.append((source, target))
    return lax.ppermute(x, ("tensor", "dw"), perm)


def z_up(x):
    return move_tensor(x, lambda xl, z: (xl, z + 1))


def z_down(x):
    return move_tensor(x, lambda xl, z: (xl, z - 1))


def swap_xl(x):
    return move_tensor(x, lambda xl, z: (xl + 1, z))


def y_up(x):
    return move_dw(x, lambda xh, y, c: (xh, y + 1, c))


def y_down(x):
    return move_dw(x, lambda xh, y, c: (xh, y - 1, c))


def swap_xh(x):
    return move_dw(x, lambda xh, y, c: (xh + 1, y, c))


def swap_core(x):
    return move_dw(x, lambda xh, y, c: (xh, y, c + 1))


def vmem():
    return pl.BlockSpec(memory_space=pltpu.VMEM)


def hbm():
    return pl.BlockSpec(memory_space=pl.ANY)


def pinned():
    return pl.BlockSpec(memory_space=pltpu.HBM)


def call(kernel, outs, ins, out_specs, in_specs, scratch=(), flops=0, moved=0, name=None, limit=VMEM_LIMIT):
    return pl.pallas_call(
        kernel,
        out_shape=outs,
        in_specs=in_specs,
        out_specs=out_specs,
        scratch_shapes=list(scratch),
        compiler_params=pltpu.CompilerParams(vmem_limit_bytes=limit),
        cost_estimate=pl.CostEstimate(flops=0, bytes_accessed=1024, transcendentals=0),
        name=name,
    )(*ins)


def prep_tokens(table, tokens, out_grad):
    rows, width = tokens.shape
    half = width // NCORE
    block = half // len(ORDER)

    def kernel(table_ref, tok_ref, grad_ref, own_ref, other_ref):
        for j in range(len(ORDER)):
            cols = slice(j * block, (j + 1) * block)
            for k, out in enumerate((own_ref, other_ref)):
                at = pl.multiple_of(table_ref[k * len(ORDER) + j] * block, block)
                out[0, :, cols] = tok_ref[:, pl.ds(at, block)]
                out[1, :, cols] = grad_ref[:, pl.ds(at, block)]

    shape = jax.ShapeDtypeStruct((2, rows, half), BF16)
    return call(
        kernel, (shape, shape), (table, tokens, out_grad), (vmem(), vmem()),
        [pl.BlockSpec(memory_space=pltpu.SMEM), vmem(), vmem()],
        moved=8 * rows * width, name="prep_tokens", limit=56 * 1024 * 1024,
    )


def prep_weights(gate, up, down):
    depth, width = gate.shape

    def kernel(gate_ref, up_ref, down_ref, out_ref):
        out_ref[:, :width] = gate_ref[...]
        out_ref[:, width : 2 * width] = up_ref[...]
        out_ref[:, 2 * width :] = down_ref[...].T

    return call(
        kernel, jax.ShapeDtypeStruct((depth, 3 * width), BF16), (gate, up, down), vmem(),
        [vmem()] * 3, moved=12 * depth * width, name="prep_weights",
    )


def start_all(copies):
    for c in copies:
        c.start()


def wait_all(copies):
    for c in copies:
        c.wait()


def forward(pieces, rows, weights, splits):
    shards = [x for x, _ in pieces]
    n_t, n_w = len(pieces), len(weights)
    half = shards[0].shape[2]
    depth, width3 = weights[0].shape
    width, width2 = width3 // 3, width3 // 3 * 2
    total = n_t * rows
    each = total // splits
    parts = 2
    per = n_w // parts

    def kernel(*refs):
        t_in, w_in = refs[:n_t], refs[n_t : n_t + n_w]
        outs, (rows_ref, tbuf, wbuf, acc, tsem, wsem, osem) = refs[n_t + n_w :][: 3 * splits], refs[n_t + n_w + 3 * splits :]
        t_copies = [
            pltpu.make_async_copy(
                r.at[:, pl.ds(pieces[i][1], rows)], tbuf.at[:, pl.ds(i * rows, rows)], tsem.at[i]
            )
            for i, r in enumerate(t_in)
        ]
        w_copies = [
            pltpu.make_async_copy(r, wbuf.at[pl.ds(j * depth, depth)], wsem.at[j])
            for j, r in enumerate(w_in)
        ]
        start_all(t_copies + w_copies)
        wait_all(t_copies)
        keep = pltpu.make_async_copy(tbuf, rows_ref, osem)
        keep.start()
        for p in range(parts):
            wait_all(w_copies[p * per : (p + 1) * per])
            ks = slice(p * per * depth, (p + 1) * per * depth)
            for k, cols in enumerate((slice(0, width2), slice(width2, width3))):
                term = jnp.dot(tbuf[k, :, ks], wbuf[ks, cols], preferred_element_type=F32)
                if p > 0:
                    term = term + acc[:, cols]
                if p < parts - 1:
                    acc[:, cols] = term
                else:
                    for i in range(term.shape[1] // width):
                        part = term[:, i * width : (i + 1) * width].astype(BF16)
                        for h in range(splits):
                            outs[3 * h + 2 * k + i][...] = part[h * each : (h + 1) * each]
        keep.wait()

    *partial, chunk = call(
        kernel,
        (jax.ShapeDtypeStruct((each, width), BF16),) * (3 * splits)
        + (jax.ShapeDtypeStruct((2, total, half), BF16),),
        (*shards, *weights), (vmem(),) * (3 * splits) + (hbm(),), [hbm()] * (n_t + n_w),
        scratch=(
            pltpu.VMEM((2, total, half), BF16),
            pltpu.VMEM((half, width3), BF16),
            pltpu.VMEM((total, width3), F32),
            pltpu.SemaphoreType.DMA((n_t,)),
            pltpu.SemaphoreType.DMA((n_w,)),
            pltpu.SemaphoreType.DMA,
        ),
        flops=2 * total * half * width3,
        moved=2 * (4 * total * half + half * width3 + total * width3),
        name="forward",
    )
    return partial, chunk


def activate(a, b, src, out, dst, step):
    width = a[0].shape[1]
    gate, up, grad = (p[src, :].astype(F32) + q[src, :].astype(F32) for p, q in zip(a, b, strict=True))
    s = 0.5 + 0.5 * jnp.tanh(0.5 * gate)
    act = gate * s
    out[dst, 2 * width :] = (act * up).astype(BF16)
    out[dst, :width] = (grad * up * s * (1.0 + gate * (1.0 - s))).astype(BF16)
    out[dst, width : 2 * width] = (grad * act).astype(BF16)


def activations(mine, other):
    rows, width = mine[0].shape
    count = len(mine)
    splits = count // 3
    step = 16

    def kernel(*refs):
        a, b, out_ref = refs[:count], refs[count : 2 * count], refs[2 * count]
        for h in range(splits):

            def one(i, _, h=h):
                src = pl.ds(pl.multiple_of(i * step, step), step)
                dst = pl.ds(pl.multiple_of(h * rows + i * step, step), step)
                activate(a[3 * h : 3 * h + 3], b[3 * h : 3 * h + 3], src, out_ref, dst, step)
                return 0

            lax.fori_loop(0, rows // step, one, 0)

    return call(
        kernel, jax.ShapeDtypeStruct((splits * rows, 3 * width), BF16), (*mine, *other), vmem(),
        [vmem()] * (2 * count), flops=30 * splits * rows * width, moved=18 * splits * rows * width,
        name="activations",
    )


def term_columns(acts, wbuf, qbuf, terms, osem, h, cols, depth, per, out, sem=0):
    for n in range(h * cols, (h + 1) * cols, depth):
        qbuf[:, n : n + depth] = lax.dot_general(
            acts[...], wbuf[n : n + depth, :], (((1,), (1,)), ((), ())), preferred_element_type=F32
        ).astype(BF16)
    for k, r in enumerate(terms):
        c = pltpu.make_async_copy(
            qbuf.at[pl.ds(k * per, per), pl.ds(h * cols, cols)],
            r.at[:, pl.ds(h * cols, cols)],
            osem.at[sem + h * len(terms) + k],
        )
        c.start()
        out.append(c)


def backward(mine, other, weights, pieces, scale, prev=(), chunks=(), count=0):
    n_w, n_p, n_c = len(weights), len(prev), len(chunks)
    rows, width = mine[0].shape
    width3 = 3 * width
    depth = weights[0].shape[0]
    half = n_w * depth
    per = rows // pieces
    prev_rows = [r.shape[0] for r in prev]
    starts = [sum(prev_rows[:i]) for i in range(n_p + 1)]
    total = starts[-1] + rows
    step = 16
    halves = 2

    def kernel(*refs):
        refs = list(refs)

        def take(n):
            got = refs[:n]
            del refs[:n]
            return got

        parts, w_in, prev_in, t_in = take(6), take(n_w), take(n_p), take(n_c)
        (acts_ref,), terms, grads = take(1), take(pieces), take(count)
        pbuf, abuf, wbuf, qbuf, tbuf, gbuf, psem, wsem, tsem, osem = refs
        here = starts[-1]
        bufs = [pbuf.at[k] for k in range(6)]
        p_copies = [pltpu.make_async_copy(r, pbuf.at[k], psem.at[k]) for k, r in enumerate(parts)]
        t_copies = [
            pltpu.make_async_copy(r, abuf.at[pl.ds(starts[i], prev_rows[i])], tsem.at[i])
            for i, r in enumerate(prev_in)
        ] + [
            pltpu.make_async_copy(
                r.at[:, :, pl.ds(0, count * depth)],
                tbuf.at[:, pl.ds(starts[i], r.shape[1])],
                tsem.at[n_p + i],
            )
            for i, r in enumerate(t_in)
        ]
        w_copies = [
            pltpu.make_async_copy(
                r.at[:, pl.ds(0, 2 * width)], wbuf.at[pl.ds(j * depth, depth)], wsem.at[j]
            )
            for j, r in enumerate(w_in)
        ]
        start_all(p_copies + t_copies + w_copies)
        wait_all(p_copies)

        def one(i, _):
            src = pl.ds(pl.multiple_of(i * step, step), step)
            dst = pl.ds(pl.multiple_of(here + i * step, step), step)
            activate(bufs[:3], bufs[3:], src, abuf, dst, step)
            return 0

        lax.fori_loop(0, rows // step, one, 0)
        out = [pltpu.make_async_copy(abuf.at[pl.ds(here, rows)], acts_ref, osem.at[0])]
        out[0].start()
        if count:
            wait_all(t_copies)
            weight_terms(abuf, tbuf, gbuf, grads, osem, 1, 0, count, scale, out)
        cols = half // halves
        for h in range(halves):
            wait_all(w_copies[h * n_w // halves : (h + 1) * n_w // halves])
            term_columns(
                abuf.at[pl.ds(here, rows), pl.ds(0, 2 * width)],
                wbuf, qbuf, terms, osem, h, cols, depth, per, out, 1 + count,
            )
        wait_all(out)

    shapes = (
        [jax.ShapeDtypeStruct((rows, width3), BF16)]
        + [jax.ShapeDtypeStruct((per, half), BF16)] * pieces
        + [jax.ShapeDtypeStruct((depth, width3), BF16)] * count
    )
    got = call(
        kernel, shapes, (*mine, *other, *weights, *prev, *chunks), [pinned()] * len(shapes),
        [hbm()] * (6 + n_w + n_p + n_c),
        scratch=(
            pltpu.VMEM((6, rows, width), BF16),
            pltpu.VMEM((total, width3), BF16),
            pltpu.VMEM((half, 2 * width), BF16),
            pltpu.VMEM((rows, half), BF16),
            pltpu.VMEM((2, total, max(count, 1) * depth), BF16),
            pltpu.VMEM((max(count, 1), depth, width3), BF16),
            pltpu.SemaphoreType.DMA((6,)),
            pltpu.SemaphoreType.DMA((n_w,)),
            pltpu.SemaphoreType.DMA((max(n_p + n_c, 1),)),
            pltpu.SemaphoreType.DMA((1 + count + halves * pieces,)),
        ),
        flops=4 * rows * half * width + 2 * total * count * depth * width3,
        moved=2 * (3 * rows * width3 + 2 * half * width + rows * half),
        name="backward",
    )
    return got[0], got[1 : 1 + pieces], got[1 + pieces :]


def weight_terms(abuf, tbuf, gbuf, grads, osem, sem, first, count, scale, out):
    depth, width3 = gbuf.shape[1:]
    width2 = width3 // 3 * 2
    dims = (((0,), (0,)), ((), ()))
    for j in range(first, first + count):
        cols = slice(j * depth, (j + 1) * depth)
        for k, w in enumerate((slice(0, width2), slice(width2, width3))):
            got = lax.dot_general(tbuf[k, :, cols], abuf[:, w], dims, preferred_element_type=F32)
            gbuf[j, :, w] = (got * scale).astype(BF16)
        c = pltpu.make_async_copy(gbuf.at[j], grads[j], osem.at[sem + j])
        c.start()
        out.append(c)


def weight_grads(acts, chunks, weights, pieces, first, count, scale):
    n_a, n_w = len(acts), len(weights)
    width3 = acts[0].shape[1]
    width2 = width3 // 3 * 2
    rows = [r.shape[0] for r in acts]
    starts = [sum(rows[:i]) for i in range(n_a)]
    half = chunks[0].shape[2]
    depth = half // len(ORDER)
    group = 2
    groups = [(g, min(group, count - g)) for g in range(0, count, group)]
    total = sum(rows)
    per = rows[0] // pieces

    def kernel(*refs):
        refs = list(refs)

        def take(n):
            got = refs[:n]
            del refs[:n]
            return got

        a_in, t_in, w_in, grads, terms = take(n_a), take(n_a), take(n_w), take(count), take(pieces)
        abuf, tbuf, gbuf, wbuf, qbuf, asem, tsem, wsem, osem = refs
        a_copies = [
            pltpu.make_async_copy(r, abuf.at[pl.ds(starts[i], rows[i])], asem.at[i])
            for i, r in enumerate(a_in)
        ]
        t_copies = [
            [
                pltpu.make_async_copy(
                    r.at[:, :, pl.ds((first + g) * depth, size * depth)],
                    tbuf.at[:, pl.ds(starts[i], rows[i]), pl.ds(g * depth, size * depth)],
                    tsem.at[k * n_a + i],
                )
                for i, r in enumerate(t_in)
            ]
            for k, (g, size) in enumerate(groups)
        ]
        w_copies = [
            pltpu.make_async_copy(
                r.at[:, pl.ds(0, width2)], wbuf.at[pl.ds(j * depth, depth)], wsem.at[j]
            )
            for j, r in enumerate(w_in)
        ]
        start_all(a_copies)
        for g in t_copies:
            start_all(g)
        start_all(w_copies)
        wait_all(a_copies)
        out = []
        for k, (g, size) in enumerate(groups):
            wait_all(t_copies[k])
            weight_terms(abuf, tbuf, gbuf, grads, osem, 0, g, size, scale, out)
        wait_all(w_copies)
        for h in range(2):
            term_columns(
                abuf.at[pl.ds(0, rows[0]), pl.ds(0, width2)],
                wbuf, qbuf, terms, osem, h, half // 2, depth, per, out, count,
            )
        wait_all(out)

    shapes = [jax.ShapeDtypeStruct((depth, width3), BF16)] * count + [
        jax.ShapeDtypeStruct((per, half), BF16)
    ] * pieces
    got = call(
        kernel, shapes, (*acts, *chunks, *weights), [pinned()] * len(shapes), [pinned()] * (2 * n_a + n_w),
        scratch=(
            pltpu.VMEM((total, width3), BF16),
            pltpu.VMEM((2, total, count * depth), BF16),
            pltpu.VMEM((count, depth, width3), BF16),
            pltpu.VMEM((half, width2), BF16),
            pltpu.VMEM((rows[0], half), BF16),
            pltpu.SemaphoreType.DMA((n_a,)),
            pltpu.SemaphoreType.DMA((len(groups) * n_a,)),
            pltpu.SemaphoreType.DMA((n_w,)),
            pltpu.SemaphoreType.DMA((count + 2 * pieces,)),
        ),
        flops=2 * total * count * depth * width3 + 2 * rows[0] * half * width2,
        moved=2 * (total * width3 + 2 * total * count * depth + count * depth * width3),
        name="weight_grads",
    )
    return got[:count], got[count:]


def tie(*arrays):
    return lax.optimization_barrier(arrays)


def add(*terms):
    total = terms[0].astype(F32)
    for t in terms[1:]:
        total = total + t.astype(F32)
    return total.astype(BF16)


def finish_weights(*terms):
    depth, width3 = terms[0].shape
    width = width3 // 3

    def kernel(*refs):
        terms_in, (gate_ref, up_ref, down_ref) = refs[:-3], refs[-3:]

        def total(k):
            cols = slice(k * width, (k + 1) * width)
            return sum(r[:, cols].astype(F32) for r in terms_in).astype(BF16)

        gate_ref[...] = total(0)
        up_ref[...] = total(1)
        down_ref[...] = total(2).T

    shapes = [jax.ShapeDtypeStruct(s, BF16) for s in ((depth, width), (depth, width), (width, depth))]
    return call(
        kernel, shapes, terms, [vmem()] * 3, [vmem()] * len(terms),
        moved=40 * depth * width, name="finish_weights",
    )


def finish_tokens(table, own, other):
    rows, half = own[0].shape
    block = half // len(ORDER)

    def kernel(table_ref, a_ref, b_ref, c_ref, d_ref, out_ref):
        for j in range(len(ORDER)):
            cols = slice(j * block, (j + 1) * block)
            for k, (p, q) in enumerate(((a_ref, b_ref), (c_ref, d_ref))):
                at = pl.multiple_of(table_ref[k * len(ORDER) + j] * block, block)
                total = p[:, cols].astype(F32) + q[:, cols].astype(F32)
                out_ref[:, pl.ds(at, block)] = total.astype(BF16)

    return call(
        kernel, jax.ShapeDtypeStruct((rows, NCORE * half), BF16), (table, *own, *other), vmem(),
        [pl.BlockSpec(memory_space=pltpu.SMEM)] + [vmem()] * 4,
        moved=12 * rows * half, name="finish_tokens",
    )


def body(tokens, out_grad, gate_weight, up_weight, down_weight):
    rows = tokens.shape[0]
    scale = 1.0 / math.sqrt(rows * lax.axis_size("tensor") * lax.axis_size("dw"))
    dw = lax.axis_index("dw")
    core, y, xh = dw % NCORE, dw // NCORE % NY, dw // (NCORE * NY)
    table = jnp.stack(
        [
            (((xh + dx) % NXH) * NY + (y + dy) % NY) * NCORE + c
            for c in (core, 1 - core)
            for dx, dy in ORDER
        ]
    ).astype(jnp.int32)

    own_part, other_part = prep_tokens(table, tokens, out_grad)
    got = swap_core(other_part)
    low = jnp.where(core == 0, own_part, got)
    high = jnp.where(core == 0, got, own_part)
    a = {0: jnp.concatenate([low, high], axis=1)}
    w = {(0, 0): prep_weights(gate_weight, up_weight, down_weight)}

    n = NCORE * rows
    a[1], a[7] = z_down(a[0]), z_up(a[0])
    b = {0: swap_xl(a[0])}
    w[1, 0], w[0, 1], w[0, 3] = swap_xh(w[0, 0]), y_down(w[0, 0]), y_up(w[0, 0])
    a2b1 = z_down(jnp.concatenate([a[1], b[0]], axis=1))
    a6b7 = z_up(jnp.concatenate([a[7], b[0]], axis=1))
    a2b1, a6b7, *_ = tie(a2b1, a6b7, w[1, 0], w[0, 1], w[0, 3])
    a3b2, a5b6 = z_down(a2b1), z_up(a6b7)
    w[1, 1], w[1, 3], w[0, 2] = swap_xh(w[0, 1]), y_up(w[1, 0]), y_down(w[0, 1])
    w13, w11, w[0, 2], a3b2, a5b6 = tie(w[1, 3], w[1, 1], w[0, 2], a3b2, a5b6)
    w[1, 1], w[1, 3] = w11, w13
    k = w13.shape[0] // 2
    w[1, 2] = jnp.concatenate([y_up(w13[:k]), y_down(w11[k:])])
    a4b3, b[5] = z_down(a3b2), z_up(a5b6[:, n:])
    b[4] = move_tensor(a5b6[:, :n], lambda xl, z: (xl + 1, z + 1))
    weights = [w[k] for k in ORDER]

    early = [
        (a[0], 0), (b[0], 0), (a[1], 0), (a2b1, n), (a[7], 0), (a6b7, n), (a2b1, 0), (a3b2, n), (a6b7, 0), (a5b6, n)
    ]
    late = [(a3b2, 0), (a4b3, n), (a5b6, 0), (b[5], 0), (a4b3, 0), (b[4], 0)]
    part1, rows1 = forward(early, n, weights, 2)
    other1 = [swap_core(x) for x in part1]
    part2, rows2 = forward(late, n, weights, 1)
    other2 = [swap_core(x) for x in part2]
    acts1 = activations(part1, other1)
    acts2, terms2, first = backward(
        part2, other2, weights, len(CHUNKS[1]), scale, prev=(acts1,), chunks=(rows1, rows2), count=FIRST
    )
    rest, terms1 = weight_grads(
        (acts1, acts2), (rows1, rows2), weights, len(CHUNKS[0]), FIRST, len(ORDER) - FIRST, scale
    )
    terms = dict(zip(CHUNKS[0] + CHUNKS[1], [*terms1, *terms2], strict=True))

    p = dict(zip(ORDER, [*first, *rest], strict=True))
    r02 = y_up(p[0, 2])
    r12 = y_down(p[1, 2])
    r10 = swap_xh(p[1, 0])
    r11 = move_dw(p[1, 1], lambda xh, y, c: (xh + 1, y + 1, c))
    r03 = y_down(p[0, 3])
    p01, p13, _, _ = tie(add(p[0, 1], r02), add(p[1, 3], r12), r11, r03)
    r01 = y_up(p01)
    r13 = move_dw(p13, lambda xh, y, c: (xh + 1, y - 1, c))

    up = z_up(terms[4][:n])
    down = z_down(terms[4][n:])
    up = z_up(terms[3].at[:n].set(add(terms[3][:n], up)))
    down = z_down(terms[5].at[n:].set(add(terms[5][n:], down)))
    up, down, *_ = tie(up, down, r02, r12, r10)
    up = z_up(add(terms[2], up))
    down = z_down(add(terms[6], down))
    up, down, *_ = tie(up, down, r11, r03)
    up = z_up(add(terms[1], up))
    down = z_down(add(terms[7], down))
    total = add(terms[0], up, down).reshape(NXL, NCORE, rows, -1)
    low, high = total[:, 0], total[:, 1]
    mine = jnp.where(core == 0, low, high)
    theirs = jnp.where(core == 0, high, low)
    grad_tokens = finish_tokens(
        table,
        (mine[0], swap_xl(mine[1])),
        (
            swap_core(theirs[0]),
            move_all(theirs[1], lambda xl, z, xh, y, c: (xl + 1, z, xh, y, c + 1)),
        ),
    )
    grad_tokens, r01, r13 = tie(grad_tokens, r01, r13)
    grads = finish_weights(p[0, 0], r10, r11, r03, r01, r13)
    return (grad_tokens, *grads)


def solution(mesh):
    placed = (
        P(("tensor", "dw"), None),
        P(("tensor", "dw"), None),
        P("dw", "tensor"),
        P("dw", "tensor"),
        P("tensor", "dw"),
    )
    return jax.shard_map(
        body,
        mesh=mesh,
        in_specs=placed,
        out_specs=(
            P(("tensor", "dw"), None),
            P("dw", "tensor"),
            P("dw", "tensor"),
            P("tensor", "dw"),
        ),
        check_vma=False,
    )
```

```python
import functools
import itertools
import math

import jax
import jax.numpy as jnp
from jax import lax
from jax.experimental import pallas as pl
from jax.experimental.pallas import tpu as pltpu
from jax.sharding import PartitionSpec as P

NXL, NZ, NXH, NY, NCORE = 2, 8, 2, 4, 2
BF16, F32 = jnp.bfloat16, jnp.float32
VMEM_LIMIT = 20 * 1024 * 1024

ORDER = ((0, 2), (1, 2), (1, 0), (1, 1), (0, 3), (0, 1), (1, 3), (0, 0))
FIRST = 3
CHUNKS = ((0, 1, 7, 2, 6), (3, 5, 4))


def move_tensor(x, dest):
    perm = []
    for xl in range(NXL):
        for z in range(NZ):
            a, b = dest(xl, z)
            perm.append((xl * NZ + z, a % NXL * NZ + b % NZ))
    return lax.ppermute(x, "tensor", perm)


def move_dw(x, dest):
    perm = []
    for xh in range(NXH):
        for y in range(NY):
            for c in range(NCORE):
                a, b, e = dest(xh, y, c)
                perm.append(
                    ((xh * NY + y) * NCORE + c, (a % NXH * NY + b % NY) * NCORE + e % NCORE)
                )
    return lax.ppermute(x, "dw", perm)


def move_all(x, dest):
    sizes = (NXL, NZ, NXH, NY, NCORE)
    perm = []
    for at in itertools.product(*map(range, sizes)):
        ends = at, dest(*at)
        source, target = (
            functools.reduce(lambda n, e: n * e[1] + e[0] % e[1], zip(end, sizes), 0) for end in ends
        )
        perm.append((source, target))
    return lax.ppermute(x, ("tensor", "dw"), perm)


def z_up(x):
    return move_tensor(x, lambda xl, z: (xl, z + 1))


def z_down(x):
    return move_tensor(x, lambda xl, z: (xl, z - 1))


def swap_xl(x):
    return move_tensor(x, lambda xl, z: (xl + 1, z))


def y_up(x):
    return move_dw(x, lambda xh, y, c: (xh, y + 1, c))


def y_down(x):
    return move_dw(x, lambda xh, y, c: (xh, y - 1, c))


def swap_xh(x):
    return move_dw(x, lambda xh, y, c: (xh + 1, y, c))


def swap_core(x):
    return move_dw(x, lambda xh, y, c: (xh, y, c + 1))


def vmem():
    return pl.BlockSpec(memory_space=pltpu.VMEM)


def hbm():
    return pl.BlockSpec(memory_space=pl.ANY)


def pinned():
    return pl.BlockSpec(memory_space=pltpu.HBM)


def call(kernel, outs, ins, out_specs, in_specs, scratch=(), flops=0, moved=0, name=None, limit=VMEM_LIMIT):
    return pl.pallas_call(
        kernel,
        out_shape=outs,
        in_specs=in_specs,
        out_specs=out_specs,
        scratch_shapes=list(scratch),
        compiler_params=pltpu.CompilerParams(vmem_limit_bytes=limit),
        cost_estimate=pl.CostEstimate(flops=0, bytes_accessed=1024, transcendentals=0),
        name=name,
    )(*ins)


def prep_tokens(table, tokens, out_grad):
    rows, width = tokens.shape
    half = width // NCORE
    block = half // len(ORDER)

    def kernel(table_ref, tok_ref, grad_ref, own_ref, other_ref):
        for j in range(len(ORDER)):
            cols = slice(j * block, (j + 1) * block)
            for k, out in enumerate((own_ref, other_ref)):
                at = pl.multiple_of(table_ref[k * len(ORDER) + j] * block, block)
                out[0, :, cols] = tok_ref[:, pl.ds(at, block)]
                out[1, :, cols] = grad_ref[:, pl.ds(at, block)]

    shape = jax.ShapeDtypeStruct((2, rows, half), BF16)
    return call(
        kernel, (shape, shape), (table, tokens, out_grad), (vmem(), vmem()),
        [pl.BlockSpec(memory_space=pltpu.SMEM), vmem(), vmem()],
        moved=8 * rows * width, name="prep_tokens", limit=56 * 1024 * 1024,
    )


def prep_weights(gate, up, down):
    depth, width = gate.shape

    def kernel(gate_ref, up_ref, down_ref, out_ref):
        out_ref[:, :width] = gate_ref[...]
        out_ref[:, width : 2 * width] = up_ref[...]
        out_ref[:, 2 * width :] = down_ref[...].T

    return call(
        kernel, jax.ShapeDtypeStruct((depth, 3 * width), BF16), (gate, up, down), vmem(),
        [vmem()] * 3, moved=12 * depth * width, name="prep_weights",
    )


def start_all(copies):
    for c in copies:
        c.start()


def wait_all(copies):
    for c in copies:
        c.wait()


def forward(pieces, rows, weights, splits):
    shards = [x for x, _ in pieces]
    n_t, n_w = len(pieces), len(weights)
    half = shards[0].shape[2]
    depth, width3 = weights[0].shape
    width, width2 = width3 // 3, width3 // 3 * 2
    total = n_t * rows
    each = total // splits
    parts = 2
    per = n_w // parts

    def kernel(*refs):
        t_in, w_in = refs[:n_t], refs[n_t : n_t + n_w]
        outs, (rows_ref, tbuf, wbuf, acc, tsem, wsem, osem) = refs[n_t + n_w :][: 3 * splits], refs[n_t + n_w + 3 * splits :]
        t_copies = [
            pltpu.make_async_copy(
                r.at[:, pl.ds(pieces[i][1], rows)], tbuf.at[:, pl.ds(i * rows, rows)], tsem.at[i]
            )
            for i, r in enumerate(t_in)
        ]
        w_copies = [
            pltpu.make_async_copy(r, wbuf.at[pl.ds(j * depth, depth)], wsem.at[j])
            for j, r in enumerate(w_in)
        ]
        start_all(t_copies + w_copies)
        wait_all(t_copies)
        keep = pltpu.make_async_copy(tbuf, rows_ref, osem)
        keep.start()
        for p in range(parts):
            wait_all(w_copies[p * per : (p + 1) * per])
            ks = slice(p * per * depth, (p + 1) * per * depth)
            for k, cols in enumerate((slice(0, width2), slice(width2, width3))):
                term = jnp.dot(tbuf[k, :, ks], wbuf[ks, cols], preferred_element_type=F32)
                if p > 0:
                    term = term + acc[:, cols]
                if p < parts - 1:
                    acc[:, cols] = term
                else:
                    for i in range(term.shape[1] // width):
                        part = term[:, i * width : (i + 1) * width].astype(BF16)
                        for h in range(splits):
                            outs[3 * h + 2 * k + i][...] = part[h * each : (h + 1) * each]
        keep.wait()

    *partial, chunk = call(
        kernel,
        (jax.ShapeDtypeStruct((each, width), BF16),) * (3 * splits)
        + (jax.ShapeDtypeStruct((2, total, half), BF16),),
        (*shards, *weights), (vmem(),) * (3 * splits) + (hbm(),), [hbm()] * (n_t + n_w),
        scratch=(
            pltpu.VMEM((2, total, half), BF16),
            pltpu.VMEM((half, width3), BF16),
            pltpu.VMEM((total, width3), F32),
            pltpu.SemaphoreType.DMA((n_t,)),
            pltpu.SemaphoreType.DMA((n_w,)),
            pltpu.SemaphoreType.DMA,
        ),
        flops=2 * total * half * width3,
        moved=2 * (4 * total * half + half * width3 + total * width3),
        name="forward",
    )
    return partial, chunk


def activate(a, b, src, out, dst, step):
    width = a[0].shape[1]
    gate, up, grad = (p[src, :].astype(F32) + q[src, :].astype(F32) for p, q in zip(a, b, strict=True))
    s = 0.5 + 0.5 * jnp.tanh(0.5 * gate)
    act = gate * s
    out[dst, 2 * width :] = (act * up).astype(BF16)
    out[dst, :width] = (grad * up * s * (1.0 + gate * (1.0 - s))).astype(BF16)
    out[dst, width : 2 * width] = (grad * act).astype(BF16)


def activations(mine, other):
    rows, width = mine[0].shape
    count = len(mine)
    splits = count // 3
    step = 16

    def kernel(*refs):
        a, b, out_ref = refs[:count], refs[count : 2 * count], refs[2 * count]
        for h in range(splits):

            def one(i, _, h=h):
                src = pl.ds(pl.multiple_of(i * step, step), step)
                dst = pl.ds(pl.multiple_of(h * rows + i * step, step), step)
                activate(a[3 * h : 3 * h + 3], b[3 * h : 3 * h + 3], src, out_ref, dst, step)
                return 0

            lax.fori_loop(0, rows // step, one, 0)

    return call(
        kernel, jax.ShapeDtypeStruct((splits * rows, 3 * width), BF16), (*mine, *other), vmem(),
        [vmem()] * (2 * count), flops=30 * splits * rows * width, moved=18 * splits * rows * width,
        name="activations",
    )


def token_terms(acts, weights, pieces):
    n_w = len(weights)
    rows, width3 = acts.shape
    width2 = width3 // 3 * 2
    depth = weights[0].shape[0]
    half = n_w * depth
    per = rows // pieces
    halves = 2
    cols = half // halves

    def kernel(*refs):
        a_ref, w_in, terms = refs[0], refs[1 : 1 + n_w], refs[1 + n_w : 1 + n_w + pieces]
        abuf, wbuf, qbuf, asem, wsem, osem = refs[1 + n_w + pieces :]
        a_copy = pltpu.make_async_copy(a_ref.at[:, pl.ds(0, width2)], abuf, asem)
        w_copies = [
            pltpu.make_async_copy(
                r.at[:, pl.ds(0, width2)], wbuf.at[pl.ds(j * depth, depth)], wsem.at[j]
            )
            for j, r in enumerate(w_in)
        ]
        a_copy.start()
        start_all(w_copies)
        a_copy.wait()
        out = []
        for h in range(halves):
            wait_all(w_copies[h * n_w // halves : (h + 1) * n_w // halves])
            term_columns(abuf, wbuf, qbuf, terms, osem, h, cols, depth, per, out)
        wait_all(out)

    return call(
        kernel, (jax.ShapeDtypeStruct((per, half), BF16),) * pieces, (acts, *weights),
        (pinned(),) * pieces, [pinned()] * (1 + n_w),
        scratch=(
            pltpu.VMEM((rows, width2), BF16),
            pltpu.VMEM((half, width2), BF16),
            pltpu.VMEM((rows, half), BF16),
            pltpu.SemaphoreType.DMA,
            pltpu.SemaphoreType.DMA((n_w,)),
            pltpu.SemaphoreType.DMA((halves * pieces,)),
        ),
        flops=2 * rows * half * width2, moved=2 * (rows * width2 + half * width2 + rows * half),
        name="token_terms",
    )


def term_columns(acts, wbuf, qbuf, terms, osem, h, cols, depth, per, out, sem=0):
    for n in range(h * cols, (h + 1) * cols, depth):
        qbuf[:, n : n + depth] = lax.dot_general(
            acts[...], wbuf[n : n + depth, :], (((1,), (1,)), ((), ())), preferred_element_type=F32
        ).astype(BF16)
    for k, r in enumerate(terms):
        c = pltpu.make_async_copy(
            qbuf.at[pl.ds(k * per, per), pl.ds(h * cols, cols)],
            r.at[:, pl.ds(h * cols, cols)],
            osem.at[sem + h * len(terms) + k],
        )
        c.start()
        out.append(c)


def backward(mine, other, weights, pieces, scale, prev=(), chunks=(), count=0):
    n_w, n_p, n_c = len(weights), len(prev), len(chunks)
    rows, width = mine[0].shape
    width3 = 3 * width
    depth = weights[0].shape[0]
    half = n_w * depth
    per = rows // pieces
    prev_rows = [r.shape[0] for r in prev]
    starts = [sum(prev_rows[:i]) for i in range(n_p + 1)]
    total = starts[-1] + rows
    step = 16
    halves = 2

    def kernel(*refs):
        refs = list(refs)

        def take(n):
            got = refs[:n]
            del refs[:n]
            return got

        parts, w_in, prev_in, t_in = take(6), take(n_w), take(n_p), take(n_c)
        (acts_ref,), terms, grads = take(1), take(pieces), take(count)
        pbuf, abuf, wbuf, qbuf, tbuf, gbuf, psem, wsem, tsem, osem = refs
        here = starts[-1]
        bufs = [pbuf.at[k] for k in range(6)]
        p_copies = [pltpu.make_async_copy(r, pbuf.at[k], psem.at[k]) for k, r in enumerate(parts)]
        t_copies = [
            pltpu.make_async_copy(r, abuf.at[pl.ds(starts[i], prev_rows[i])], tsem.at[i])
            for i, r in enumerate(prev_in)
        ] + [
            pltpu.make_async_copy(
                r.at[:, :, pl.ds(0, count * depth)],
                tbuf.at[:, pl.ds(starts[i], r.shape[1])],
                tsem.at[n_p + i],
            )
            for i, r in enumerate(t_in)
        ]
        w_copies = [
            pltpu.make_async_copy(
                r.at[:, pl.ds(0, 2 * width)], wbuf.at[pl.ds(j * depth, depth)], wsem.at[j]
            )
            for j, r in enumerate(w_in)
        ]
        start_all(p_copies + t_copies + w_copies)
        wait_all(p_copies)

        def one(i, _):
            src = pl.ds(pl.multiple_of(i * step, step), step)
            dst = pl.ds(pl.multiple_of(here + i * step, step), step)
            activate(bufs[:3], bufs[3:], src, abuf, dst, step)
            return 0

        lax.fori_loop(0, rows // step, one, 0)
        out = [pltpu.make_async_copy(abuf.at[pl.ds(here, rows)], acts_ref, osem.at[0])]
        out[0].start()
        if count:
            wait_all(t_copies)
            weight_terms(abuf, tbuf, gbuf, grads, osem, 1, 0, count, scale, out)
        cols = half // halves
        for h in range(halves):
            wait_all(w_copies[h * n_w // halves : (h + 1) * n_w // halves])
            term_columns(
                abuf.at[pl.ds(here, rows), pl.ds(0, 2 * width)],
                wbuf, qbuf, terms, osem, h, cols, depth, per, out, 1 + count,
            )
        wait_all(out)

    shapes = (
        [jax.ShapeDtypeStruct((rows, width3), BF16)]
        + [jax.ShapeDtypeStruct((per, half), BF16)] * pieces
        + [jax.ShapeDtypeStruct((depth, width3), BF16)] * count
    )
    got = call(
        kernel, shapes, (*mine, *other, *weights, *prev, *chunks), [pinned()] * len(shapes),
        [hbm()] * (6 + n_w + n_p + n_c),
        scratch=(
            pltpu.VMEM((6, rows, width), BF16),
            pltpu.VMEM((total, width3), BF16),
            pltpu.VMEM((half, 2 * width), BF16),
            pltpu.VMEM((rows, half), BF16),
            pltpu.VMEM((2, total, max(count, 1) * depth), BF16),
            pltpu.VMEM((max(count, 1), depth, width3), BF16),
            pltpu.SemaphoreType.DMA((6,)),
            pltpu.SemaphoreType.DMA((n_w,)),
            pltpu.SemaphoreType.DMA((max(n_p + n_c, 1),)),
            pltpu.SemaphoreType.DMA((1 + count + halves * pieces,)),
        ),
        flops=4 * rows * half * width + 2 * total * count * depth * width3,
        moved=2 * (3 * rows * width3 + 2 * half * width + rows * half),
        name="backward",
    )
    return got[0], got[1 : 1 + pieces], got[1 + pieces :]


def weight_terms(abuf, tbuf, gbuf, grads, osem, sem, first, count, scale, out):
    depth, width3 = gbuf.shape[1:]
    width2 = width3 // 3 * 2
    dims = (((0,), (0,)), ((), ()))
    for j in range(first, first + count):
        cols = slice(j * depth, (j + 1) * depth)
        for k, w in enumerate((slice(0, width2), slice(width2, width3))):
            got = lax.dot_general(tbuf[k, :, cols], abuf[:, w], dims, preferred_element_type=F32)
            gbuf[j, :, w] = (got * scale).astype(BF16)
        c = pltpu.make_async_copy(gbuf.at[j], grads[j], osem.at[sem + j])
        c.start()
        out.append(c)


def weight_grads(acts, chunks, first, count, scale):
    n_a = len(acts)
    width3 = acts[0].shape[1]
    rows = [r.shape[0] for r in acts]
    starts = [sum(rows[:i]) for i in range(n_a)]
    depth = chunks[0].shape[2] // len(ORDER)
    group = 2
    groups = [(g, min(group, count - g)) for g in range(0, count, group)]
    total = sum(rows)

    def kernel(*refs):
        a_in, t_in, grads = refs[:n_a], refs[n_a : 2 * n_a], refs[2 * n_a : 2 * n_a + count]
        abuf, tbuf, gbuf, asem, tsem, osem = refs[2 * n_a + count :]
        a_copies = [
            pltpu.make_async_copy(r, abuf.at[pl.ds(starts[i], rows[i])], asem.at[i])
            for i, r in enumerate(a_in)
        ]
        t_copies = [
            [
                pltpu.make_async_copy(
                    r.at[:, :, pl.ds((first + g) * depth, size * depth)],
                    tbuf.at[:, pl.ds(starts[i], rows[i]), pl.ds(g * depth, size * depth)],
                    tsem.at[k * n_a + i],
                )
                for i, r in enumerate(t_in)
            ]
            for k, (g, size) in enumerate(groups)
        ]
        start_all(a_copies)
        for g in t_copies:
            start_all(g)
        wait_all(a_copies)
        out = []
        for k, (g, size) in enumerate(groups):
            wait_all(t_copies[k])
            weight_terms(abuf, tbuf, gbuf, grads, osem, 0, g, size, scale, out)
        wait_all(out)

    return call(
        kernel, (jax.ShapeDtypeStruct((depth, width3), BF16),) * count, (*acts, *chunks),
        (pinned(),) * count, [pinned()] * (2 * n_a),
        scratch=(
            pltpu.VMEM((total, width3), BF16),
            pltpu.VMEM((2, total, count * depth), BF16),
            pltpu.VMEM((count, depth, width3), BF16),
            pltpu.SemaphoreType.DMA((n_a,)),
            pltpu.SemaphoreType.DMA((len(groups) * n_a,)),
            pltpu.SemaphoreType.DMA((count,)),
        ),
        flops=2 * total * count * depth * width3,
        moved=2 * (total * width3 + 2 * total * count * depth + count * depth * width3),
        name="weight_grads",
    )


def tie(*arrays):
    return lax.optimization_barrier(arrays)


def add(*terms):
    total = terms[0].astype(F32)
    for t in terms[1:]:
        total = total + t.astype(F32)
    return total.astype(BF16)


def finish_weights(*terms):
    depth, width3 = terms[0].shape
    width = width3 // 3

    def kernel(*refs):
        terms_in, (gate_ref, up_ref, down_ref) = refs[:-3], refs[-3:]

        def total(k):
            cols = slice(k * width, (k + 1) * width)
            return sum(r[:, cols].astype(F32) for r in terms_in).astype(BF16)

        gate_ref[...] = total(0)
        up_ref[...] = total(1)
        down_ref[...] = total(2).T

    shapes = [jax.ShapeDtypeStruct(s, BF16) for s in ((depth, width), (depth, width), (width, depth))]
    return call(
        kernel, shapes, terms, [vmem()] * 3, [vmem()] * len(terms),
        moved=40 * depth * width, name="finish_weights",
    )


def finish_tokens(table, own, other):
    rows, half = own[0].shape
    block = half // len(ORDER)

    def kernel(table_ref, a_ref, b_ref, c_ref, d_ref, out_ref):
        for j in range(len(ORDER)):
            cols = slice(j * block, (j + 1) * block)
            for k, (p, q) in enumerate(((a_ref, b_ref), (c_ref, d_ref))):
                at = pl.multiple_of(table_ref[k * len(ORDER) + j] * block, block)
                total = p[:, cols].astype(F32) + q[:, cols].astype(F32)
                out_ref[:, pl.ds(at, block)] = total.astype(BF16)

    return call(
        kernel, jax.ShapeDtypeStruct((rows, NCORE * half), BF16), (table, *own, *other), vmem(),
        [pl.BlockSpec(memory_space=pltpu.SMEM)] + [vmem()] * 4,
        moved=12 * rows * half, name="finish_tokens",
    )


def body(tokens, out_grad, gate_weight, up_weight, down_weight):
    rows = tokens.shape[0]
    scale = 1.0 / math.sqrt(rows * lax.axis_size("tensor") * lax.axis_size("dw"))
    dw = lax.axis_index("dw")
    core, y, xh = dw % NCORE, dw // NCORE % NY, dw // (NCORE * NY)
    table = jnp.stack(
        [
            (((xh + dx) % NXH) * NY + (y + dy) % NY) * NCORE + c
            for c in (core, 1 - core)
            for dx, dy in ORDER
        ]
    ).astype(jnp.int32)

    own_part, other_part = prep_tokens(table, tokens, out_grad)
    got = swap_core(other_part)
    low = jnp.where(core == 0, own_part, got)
    high = jnp.where(core == 0, got, own_part)
    a = {0: jnp.concatenate([low, high], axis=1)}
    w = {(0, 0): prep_weights(gate_weight, up_weight, down_weight)}

    n = NCORE * rows
    a[1], a[7] = z_down(a[0]), z_up(a[0])
    b = {0: swap_xl(a[0])}
    w[1, 0], w[0, 1], w[0, 3] = swap_xh(w[0, 0]), y_down(w[0, 0]), y_up(w[0, 0])
    a2b1 = z_down(jnp.concatenate([a[1], b[0]], axis=1))
    a6b7 = z_up(jnp.concatenate([a[7], b[0]], axis=1))
    a2b1, a6b7, *_ = tie(a2b1, a6b7, w[1, 0], w[0, 1], w[0, 3])
    a3b2, a5b6 = z_down(a2b1), z_up(a6b7)
    w[1, 1], w[1, 3], w[0, 2] = swap_xh(w[0, 1]), y_up(w[1, 0]), y_down(w[0, 1])
    w13, w11, w[0, 2], a3b2, a5b6 = tie(w[1, 3], w[1, 1], w[0, 2], a3b2, a5b6)
    w[1, 1], w[1, 3] = w11, w13
    k = w13.shape[0] // 2
    w[1, 2] = jnp.concatenate([y_up(w13[:k]), y_down(w11[k:])])
    a4b3, b[5] = z_down(a3b2), z_up(a5b6[:, n:])
    b[4] = move_tensor(a5b6[:, :n], lambda xl, z: (xl + 1, z + 1))
    weights = [w[k] for k in ORDER]

    early = [
        (a[0], 0), (b[0], 0), (a[1], 0), (a2b1, n), (a[7], 0), (a6b7, n), (a2b1, 0), (a3b2, n), (a6b7, 0), (a5b6, n)
    ]
    late = [(a3b2, 0), (a4b3, n), (a5b6, 0), (b[5], 0), (a4b3, 0), (b[4], 0)]
    part1, rows1 = forward(early, n, weights, 2)
    other1 = [swap_core(x) for x in part1]
    part2, rows2 = forward(late, n, weights, 1)
    other2 = [swap_core(x) for x in part2]
    acts1 = activations(part1, other1)
    acts2, terms2, first = backward(
        part2, other2, weights, len(CHUNKS[1]), scale, prev=(acts1,), chunks=(rows1, rows2), count=FIRST
    )
    rest = weight_grads((acts1, acts2), (rows1, rows2), FIRST, len(ORDER) - FIRST, scale)
    terms = dict(zip(CHUNKS[1], terms2, strict=True))

    p = dict(zip(ORDER, [*first, *rest], strict=True))
    r02 = y_up(p[0, 2])
    r12 = y_down(p[1, 2])
    r10 = swap_xh(p[1, 0])
    r11 = move_dw(p[1, 1], lambda xh, y, c: (xh + 1, y + 1, c))
    r03 = y_down(p[0, 3])
    p01, p13, _, _ = tie(add(p[0, 1], r02), add(p[1, 3], r12), r11, r03)
    r01 = y_up(p01)
    r13 = move_dw(p13, lambda xh, y, c: (xh + 1, y - 1, c))

    up = z_up(terms[4][:n])
    down = z_down(terms[4][n:])
    up = z_up(terms[3].at[:n].set(add(terms[3][:n], up)))
    down = z_down(terms[5].at[n:].set(add(terms[5][n:], down)))
    up, down, acts1 = tie(up, down, acts1)
    terms.update(zip(CHUNKS[0], token_terms(acts1, weights, len(CHUNKS[0])), strict=True))
    up, down, *_ = tie(up, down, r02, r12, r10)
    up = z_up(add(terms[2], up))
    down = z_down(add(terms[6], down))
    up, down, *_ = tie(up, down, r11, r03)
    up = z_up(add(terms[1], up))
    down = z_down(add(terms[7], down))
    total = add(terms[0], up, down).reshape(NXL, NCORE, rows, -1)
    low, high = total[:, 0], total[:, 1]
    mine = jnp.where(core == 0, low, high)
    theirs = jnp.where(core == 0, high, low)
    grad_tokens = finish_tokens(
        table,
        (mine[0], swap_xl(mine[1])),
        (
            swap_core(theirs[0]),
            move_all(theirs[1], lambda xl, z, xh, y, c: (xl + 1, z, xh, y, c + 1)),
        ),
    )
    grads = finish_weights(p[0, 0], r10, r11, r03, r01, r13)
    return (grad_tokens, *grads)


def solution(mesh):
    placed = (
        P(("tensor", "dw"), None),
        P(("tensor", "dw"), None),
        P("dw", "tensor"),
        P("dw", "tensor"),
        P("tensor", "dw"),
    )
    return jax.shard_map(
        body,
        mesh=mesh,
        in_specs=placed,
        out_specs=(
            P(("tensor", "dw"), None),
            P("dw", "tensor"),
            P("dw", "tensor"),
            P("tensor", "dw"),
        ),
        check_vma=False,
    )
```

```python
import functools
import itertools
import math

import jax
import jax.numpy as jnp
from jax import lax
from jax.experimental import pallas as pl
from jax.experimental.pallas import tpu as pltpu
from jax.sharding import PartitionSpec as P

NXL, NZ, NXH, NY, NCORE = 2, 8, 2, 4, 2
BF16, F32 = jnp.bfloat16, jnp.float32
VMEM_LIMIT = 20 * 1024 * 1024

ORDER = ((0, 2), (1, 2), (1, 0), (1, 1), (0, 3), (0, 1), (1, 3), (0, 0))
FIRST = 3
CHUNKS = ((0, 1, 7, 2, 6), (3, 5, 4))


def move_tensor(x, dest):
    perm = []
    for xl in range(NXL):
        for z in range(NZ):
            a, b = dest(xl, z)
            perm.append((xl * NZ + z, a % NXL * NZ + b % NZ))
    return lax.ppermute(x, "tensor", perm)


def move_dw(x, dest):
    perm = []
    for xh in range(NXH):
        for y in range(NY):
            for c in range(NCORE):
                a, b, e = dest(xh, y, c)
                perm.append(
                    ((xh * NY + y) * NCORE + c, (a % NXH * NY + b % NY) * NCORE + e % NCORE)
                )
    return lax.ppermute(x, "dw", perm)


def move_all(x, dest):
    sizes = (NXL, NZ, NXH, NY, NCORE)
    perm = []
    for at in itertools.product(*map(range, sizes)):
        ends = at, dest(*at)
        source, target = (
            functools.reduce(lambda n, e: n * e[1] + e[0] % e[1], zip(end, sizes), 0) for end in ends
        )
        perm.append((source, target))
    return lax.ppermute(x, ("tensor", "dw"), perm)


def z_up(x):
    return move_tensor(x, lambda xl, z: (xl, z + 1))


def z_down(x):
    return move_tensor(x, lambda xl, z: (xl, z - 1))


def swap_xl(x):
    return move_tensor(x, lambda xl, z: (xl + 1, z))


def y_up(x):
    return move_dw(x, lambda xh, y, c: (xh, y + 1, c))


def y_down(x):
    return move_dw(x, lambda xh, y, c: (xh, y - 1, c))


def swap_xh(x):
    return move_dw(x, lambda xh, y, c: (xh + 1, y, c))


def swap_core(x):
    return move_dw(x, lambda xh, y, c: (xh, y, c + 1))


def vmem():
    return pl.BlockSpec(memory_space=pltpu.VMEM)


def hbm():
    return pl.BlockSpec(memory_space=pl.ANY)


def pinned():
    return pl.BlockSpec(memory_space=pltpu.HBM)


def call(kernel, outs, ins, out_specs, in_specs, scratch=(), flops=0, moved=0, name=None, limit=VMEM_LIMIT):
    return pl.pallas_call(
        kernel,
        out_shape=outs,
        in_specs=in_specs,
        out_specs=out_specs,
        scratch_shapes=list(scratch),
        compiler_params=pltpu.CompilerParams(vmem_limit_bytes=limit),
        cost_estimate=pl.CostEstimate(flops=0, bytes_accessed=1024, transcendentals=0),
        name=name,
    )(*ins)


def places(dw):
    core, y, xh = dw % NCORE, dw // NCORE % NY, dw // (NCORE * NY)
    return [
        [((xh + dx) % NXH * NY + (y + dy) % NY) * NCORE + c for dx, dy in ORDER]
        for c in (core, 1 - core)
    ]


def prep_tokens(dw, tokens, out_grad):
    rows, width = tokens.shape
    half = width // NCORE
    block = half // len(ORDER)

    def kernel(dw_ref, tok_ref, grad_ref, own_ref, other_ref):
        for out, blocks in zip((own_ref, other_ref), places(dw_ref[0]), strict=True):
            for j, place in enumerate(blocks):
                cols = slice(j * block, (j + 1) * block)
                at = pl.multiple_of(place * block, block)
                out[0, :, cols] = tok_ref[:, pl.ds(at, block)]
                out[1, :, cols] = grad_ref[:, pl.ds(at, block)]

    shape = jax.ShapeDtypeStruct((2, rows, half), BF16)
    return call(
        kernel, (shape, shape), (dw, tokens, out_grad), (vmem(), vmem()),
        [pl.BlockSpec(memory_space=pltpu.SMEM), vmem(), vmem()],
        moved=8 * rows * width, name="prep_tokens", limit=56 * 1024 * 1024,
    )


def prep_weights(gate, up, down):
    depth, width = gate.shape

    def kernel(gate_ref, up_ref, down_ref, out_ref):
        out_ref[:, :width] = gate_ref[...]
        out_ref[:, width : 2 * width] = up_ref[...]
        out_ref[:, 2 * width :] = down_ref[...].T

    return call(
        kernel, jax.ShapeDtypeStruct((depth, 3 * width), BF16), (gate, up, down), vmem(),
        [vmem()] * 3, moved=12 * depth * width, name="prep_weights",
    )


def start_all(copies):
    for c in copies:
        c.start()


def wait_all(copies):
    for c in copies:
        c.wait()


def forward(pieces, rows, weights, splits):
    shards = [x for x, _ in pieces]
    n_t, n_w = len(pieces), len(weights)
    half = shards[0].shape[2]
    depth, width3 = weights[0].shape
    width, width2 = width3 // 3, width3 // 3 * 2
    total = n_t * rows
    each = total // splits
    parts = 2
    per = n_w // parts

    def kernel(*refs):
        t_in, w_in = refs[:n_t], refs[n_t : n_t + n_w]
        outs, (rows_ref, tbuf, wbuf, acc, tsem, wsem, osem) = refs[n_t + n_w :][: 3 * splits], refs[n_t + n_w + 3 * splits :]
        t_copies = [
            pltpu.make_async_copy(
                r.at[:, pl.ds(pieces[i][1], rows)], tbuf.at[:, pl.ds(i * rows, rows)], tsem.at[i]
            )
            for i, r in enumerate(t_in)
        ]
        w_copies = [
            pltpu.make_async_copy(r, wbuf.at[pl.ds(j * depth, depth)], wsem.at[j])
            for j, r in enumerate(w_in)
        ]
        start_all(t_copies + w_copies)
        wait_all(t_copies)
        keep = pltpu.make_async_copy(tbuf, rows_ref, osem)
        keep.start()
        for p in range(parts):
            wait_all(w_copies[p * per : (p + 1) * per])
            ks = slice(p * per * depth, (p + 1) * per * depth)
            for k, cols in enumerate((slice(0, width2), slice(width2, width3))):
                term = jnp.dot(tbuf[k, :, ks], wbuf[ks, cols], preferred_element_type=F32)
                if p > 0:
                    term = term + acc[:, cols]
                if p < parts - 1:
                    acc[:, cols] = term
                else:
                    for i in range(term.shape[1] // width):
                        part = term[:, i * width : (i + 1) * width].astype(BF16)
                        for h in range(splits):
                            outs[3 * h + 2 * k + i][...] = part[h * each : (h + 1) * each]
        keep.wait()

    *partial, chunk = call(
        kernel,
        (jax.ShapeDtypeStruct((each, width), BF16),) * (3 * splits)
        + (jax.ShapeDtypeStruct((2, total, half), BF16),),
        (*shards, *weights), (vmem(),) * (3 * splits) + (hbm(),), [hbm()] * (n_t + n_w),
        scratch=(
            pltpu.VMEM((2, total, half), BF16),
            pltpu.VMEM((half, width3), BF16),
            pltpu.VMEM((total, width3), F32),
            pltpu.SemaphoreType.DMA((n_t,)),
            pltpu.SemaphoreType.DMA((n_w,)),
            pltpu.SemaphoreType.DMA,
        ),
        flops=2 * total * half * width3,
        moved=2 * (4 * total * half + half * width3 + total * width3),
        name="forward",
    )
    return partial, chunk


def activate(a, b, src, out, dst, step):
    width = a[0].shape[1]
    gate, up, grad = (p[src, :].astype(F32) + q[src, :].astype(F32) for p, q in zip(a, b, strict=True))
    s = 0.5 + 0.5 * jnp.tanh(0.5 * gate)
    act = gate * s
    out[dst, 2 * width :] = (act * up).astype(BF16)
    out[dst, :width] = (grad * up * s * (1.0 + gate * (1.0 - s))).astype(BF16)
    out[dst, width : 2 * width] = (grad * act).astype(BF16)


def activations(mine, other):
    rows, width = mine[0].shape
    count = len(mine)
    splits = count // 3
    step = 16

    def kernel(*refs):
        a, b, out_ref = refs[:count], refs[count : 2 * count], refs[2 * count]
        for h in range(splits):

            def one(i, _, h=h):
                src = pl.ds(pl.multiple_of(i * step, step), step)
                dst = pl.ds(pl.multiple_of(h * rows + i * step, step), step)
                activate(a[3 * h : 3 * h + 3], b[3 * h : 3 * h + 3], src, out_ref, dst, step)
                return 0

            lax.fori_loop(0, rows // step, one, 0)

    return call(
        kernel, jax.ShapeDtypeStruct((splits * rows, 3 * width), BF16), (*mine, *other), vmem(),
        [vmem()] * (2 * count), flops=30 * splits * rows * width, moved=18 * splits * rows * width,
        name="activations",
    )


def token_terms(acts, weights, pieces):
    n_w = len(weights)
    rows, width3 = acts.shape
    width2 = width3 // 3 * 2
    depth = weights[0].shape[0]
    half = n_w * depth
    per = rows // pieces
    halves = 2
    cols = half // halves

    def kernel(*refs):
        a_ref, w_in, terms = refs[0], refs[1 : 1 + n_w], refs[1 + n_w : 1 + n_w + pieces]
        abuf, wbuf, qbuf, asem, wsem, osem = refs[1 + n_w + pieces :]
        a_copy = pltpu.make_async_copy(a_ref.at[:, pl.ds(0, width2)], abuf, asem)
        w_copies = [
            pltpu.make_async_copy(
                r.at[:, pl.ds(0, width2)], wbuf.at[pl.ds(j * depth, depth)], wsem.at[j]
            )
            for j, r in enumerate(w_in)
        ]
        a_copy.start()
        start_all(w_copies)
        a_copy.wait()
        out = []
        for h in range(halves):
            wait_all(w_copies[h * n_w // halves : (h + 1) * n_w // halves])
            term_columns(abuf, wbuf, qbuf, terms, osem, h, cols, depth, per, out)
        wait_all(out)

    return call(
        kernel, (jax.ShapeDtypeStruct((per, half), BF16),) * pieces, (acts, *weights),
        (pinned(),) * pieces, [pinned()] * (1 + n_w),
        scratch=(
            pltpu.VMEM((rows, width2), BF16),
            pltpu.VMEM((half, width2), BF16),
            pltpu.VMEM((rows, half), BF16),
            pltpu.SemaphoreType.DMA,
            pltpu.SemaphoreType.DMA((n_w,)),
            pltpu.SemaphoreType.DMA((halves * pieces,)),
        ),
        flops=2 * rows * half * width2, moved=2 * (rows * width2 + half * width2 + rows * half),
        name="token_terms",
    )


def term_columns(acts, wbuf, qbuf, terms, osem, h, cols, depth, per, out, sem=0):
    for n in range(h * cols, (h + 1) * cols, depth):
        qbuf[:, n : n + depth] = lax.dot_general(
            acts[...], wbuf[n : n + depth, :], (((1,), (1,)), ((), ())), preferred_element_type=F32
        ).astype(BF16)
    for k, r in enumerate(terms):
        c = pltpu.make_async_copy(
            qbuf.at[pl.ds(k * per, per), pl.ds(h * cols, cols)],
            r.at[:, pl.ds(h * cols, cols)],
            osem.at[sem + h * len(terms) + k],
        )
        c.start()
        out.append(c)


def backward(mine, other, weights, pieces, scale, prev=(), chunks=(), count=0):
    n_w, n_p, n_c = len(weights), len(prev), len(chunks)
    rows, width = mine[0].shape
    width3 = 3 * width
    depth = weights[0].shape[0]
    half = n_w * depth
    per = rows // pieces
    prev_rows = [r.shape[0] for r in prev]
    starts = [sum(prev_rows[:i]) for i in range(n_p + 1)]
    total = starts[-1] + rows
    step = 16
    halves = 2

    def kernel(*refs):
        refs = list(refs)

        def take(n):
            got = refs[:n]
            del refs[:n]
            return got

        parts, w_in, prev_in, t_in = take(6), take(n_w), take(n_p), take(n_c)
        (acts_ref,), terms, grads = take(1), take(pieces), take(count)
        pbuf, abuf, wbuf, qbuf, tbuf, gbuf, psem, wsem, tsem, osem = refs
        here = starts[-1]
        bufs = [pbuf.at[k] for k in range(6)]
        p_copies = [pltpu.make_async_copy(r, pbuf.at[k], psem.at[k]) for k, r in enumerate(parts)]
        t_copies = [
            pltpu.make_async_copy(r, abuf.at[pl.ds(starts[i], prev_rows[i])], tsem.at[i])
            for i, r in enumerate(prev_in)
        ] + [
            pltpu.make_async_copy(
                r.at[:, :, pl.ds(0, count * depth)],
                tbuf.at[:, pl.ds(starts[i], r.shape[1])],
                tsem.at[n_p + i],
            )
            for i, r in enumerate(t_in)
        ]
        w_copies = [
            pltpu.make_async_copy(
                r.at[:, pl.ds(0, 2 * width)], wbuf.at[pl.ds(j * depth, depth)], wsem.at[j]
            )
            for j, r in enumerate(w_in)
        ]
        start_all(p_copies + t_copies + w_copies)
        wait_all(p_copies)

        def one(i, _):
            src = pl.ds(pl.multiple_of(i * step, step), step)
            dst = pl.ds(pl.multiple_of(here + i * step, step), step)
            activate(bufs[:3], bufs[3:], src, abuf, dst, step)
            return 0

        lax.fori_loop(0, rows // step, one, 0)
        out = [pltpu.make_async_copy(abuf.at[pl.ds(here, rows)], acts_ref, osem.at[0])]
        out[0].start()
        if count:
            wait_all(t_copies)
            weight_terms(abuf, tbuf, gbuf, grads, osem, 1, 0, count, scale, out)
        cols = half // halves
        for h in range(halves):
            wait_all(w_copies[h * n_w // halves : (h + 1) * n_w // halves])
            term_columns(
                abuf.at[pl.ds(here, rows), pl.ds(0, 2 * width)],
                wbuf, qbuf, terms, osem, h, cols, depth, per, out, 1 + count,
            )
        wait_all(out)

    shapes = (
        [jax.ShapeDtypeStruct((rows, width3), BF16)]
        + [jax.ShapeDtypeStruct((per, half), BF16)] * pieces
        + [jax.ShapeDtypeStruct((depth, width3), BF16)] * count
    )
    got = call(
        kernel, shapes, (*mine, *other, *weights, *prev, *chunks), [pinned()] * len(shapes),
        [hbm()] * (6 + n_w + n_p + n_c),
        scratch=(
            pltpu.VMEM((6, rows, width), BF16),
            pltpu.VMEM((total, width3), BF16),
            pltpu.VMEM((half, 2 * width), BF16),
            pltpu.VMEM((rows, half), BF16),
            pltpu.VMEM((2, total, max(count, 1) * depth), BF16),
            pltpu.VMEM((max(count, 1), depth, width3), BF16),
            pltpu.SemaphoreType.DMA((6,)),
            pltpu.SemaphoreType.DMA((n_w,)),
            pltpu.SemaphoreType.DMA((max(n_p + n_c, 1),)),
            pltpu.SemaphoreType.DMA((1 + count + halves * pieces,)),
        ),
        flops=4 * rows * half * width + 2 * total * count * depth * width3,
        moved=2 * (3 * rows * width3 + 2 * half * width + rows * half),
        name="backward",
    )
    return got[0], got[1 : 1 + pieces], got[1 + pieces :]


def weight_terms(abuf, tbuf, gbuf, grads, osem, sem, first, count, scale, out):
    depth, width3 = gbuf.shape[1:]
    width2 = width3 // 3 * 2
    dims = (((0,), (0,)), ((), ()))
    for j in range(first, first + count):
        cols = slice(j * depth, (j + 1) * depth)
        for k, w in enumerate((slice(0, width2), slice(width2, width3))):
            got = lax.dot_general(tbuf[k, :, cols], abuf[:, w], dims, preferred_element_type=F32)
            gbuf[j, :, w] = (got * scale).astype(BF16)
        c = pltpu.make_async_copy(gbuf.at[j], grads[j], osem.at[sem + j])
        c.start()
        out.append(c)


def weight_grads(acts, chunks, first, count, scale):
    n_a = len(acts)
    width3 = acts[0].shape[1]
    rows = [r.shape[0] for r in acts]
    starts = [sum(rows[:i]) for i in range(n_a)]
    depth = chunks[0].shape[2] // len(ORDER)
    group = 2
    groups = [(g, min(group, count - g)) for g in range(0, count, group)]
    total = sum(rows)

    def kernel(*refs):
        a_in, t_in, grads = refs[:n_a], refs[n_a : 2 * n_a], refs[2 * n_a : 2 * n_a + count]
        abuf, tbuf, gbuf, asem, tsem, osem = refs[2 * n_a + count :]
        a_copies = [
            pltpu.make_async_copy(r, abuf.at[pl.ds(starts[i], rows[i])], asem.at[i])
            for i, r in enumerate(a_in)
        ]
        t_copies = [
            [
                pltpu.make_async_copy(
                    r.at[:, :, pl.ds((first + g) * depth, size * depth)],
                    tbuf.at[:, pl.ds(starts[i], rows[i]), pl.ds(g * depth, size * depth)],
                    tsem.at[k * n_a + i],
                )
                for i, r in enumerate(t_in)
            ]
            for k, (g, size) in enumerate(groups)
        ]
        start_all(a_copies)
        for g in t_copies:
            start_all(g)
        wait_all(a_copies)
        out = []
        for k, (g, size) in enumerate(groups):
            wait_all(t_copies[k])
            weight_terms(abuf, tbuf, gbuf, grads, osem, 0, g, size, scale, out)
        wait_all(out)

    return call(
        kernel, (jax.ShapeDtypeStruct((depth, width3), BF16),) * count, (*acts, *chunks),
        (pinned(),) * count, [pinned()] * (2 * n_a),
        scratch=(
            pltpu.VMEM((total, width3), BF16),
            pltpu.VMEM((2, total, count * depth), BF16),
            pltpu.VMEM((count, depth, width3), BF16),
            pltpu.SemaphoreType.DMA((n_a,)),
            pltpu.SemaphoreType.DMA((len(groups) * n_a,)),
            pltpu.SemaphoreType.DMA((count,)),
        ),
        flops=2 * total * count * depth * width3,
        moved=2 * (total * width3 + 2 * total * count * depth + count * depth * width3),
        name="weight_grads",
    )


def tie(*arrays):
    return lax.optimization_barrier(arrays)


def add(*terms):
    total = terms[0].astype(F32)
    for t in terms[1:]:
        total = total + t.astype(F32)
    return total.astype(BF16)


def finish(dw, own, other, terms):
    rows, half = own[0].shape
    block = half // len(ORDER)
    depth, width3 = terms[0].shape
    width = width3 // 3

    def kernel(*refs):
        dw_ref, pairs, terms_in = refs[0], (refs[1:3], refs[3:5]), refs[5 : 5 + len(terms)]
        token_ref, gate_ref, up_ref, down_ref = refs[5 + len(terms) :]
        for (p, q), blocks in zip(pairs, places(dw_ref[0]), strict=True):
            for j, place in enumerate(blocks):
                cols = slice(j * block, (j + 1) * block)
                total = p[:, cols].astype(F32) + q[:, cols].astype(F32)
                token_ref[:, pl.ds(pl.multiple_of(place * block, block), block)] = total.astype(BF16)

        def total(k):
            cols = slice(k * width, (k + 1) * width)
            return sum(r[:, cols].astype(F32) for r in terms_in).astype(BF16)

        gate_ref[...] = total(0)
        up_ref[...] = total(1)
        down_ref[...] = total(2).T

    shapes = [
        jax.ShapeDtypeStruct(s, BF16)
        for s in ((rows, NCORE * half), (depth, width), (depth, width), (width, depth))
    ]
    return call(
        kernel, shapes, (dw, *own, *other, *terms), [vmem()] * 4,
        [pl.BlockSpec(memory_space=pltpu.SMEM)] + [vmem()] * (4 + len(terms)),
        moved=12 * rows * half + 40 * depth * width, name="finish",
    )


def body(tokens, out_grad, gate_weight, up_weight, down_weight):
    rows = tokens.shape[0]
    scale = 1.0 / math.sqrt(rows * lax.axis_size("tensor") * lax.axis_size("dw"))
    dw = lax.axis_index("dw")
    core = dw % NCORE
    here = dw.astype(jnp.int32).reshape(1)

    own_part, other_part = prep_tokens(here, tokens, out_grad)
    got = swap_core(other_part)
    low = jnp.where(core == 0, own_part, got)
    high = jnp.where(core == 0, got, own_part)
    a = {0: jnp.concatenate([low, high], axis=1)}
    w = {(0, 0): prep_weights(gate_weight, up_weight, down_weight)}

    n = NCORE * rows
    a[1], a[7] = z_down(a[0]), z_up(a[0])
    b = {0: swap_xl(a[0])}
    w[1, 0], w[0, 1], w[0, 3] = swap_xh(w[0, 0]), y_down(w[0, 0]), y_up(w[0, 0])
    a2b1 = z_down(jnp.concatenate([a[1], b[0]], axis=1))
    a6b7 = z_up(jnp.concatenate([a[7], b[0]], axis=1))
    a2b1, a6b7, *_ = tie(a2b1, a6b7, w[1, 0], w[0, 1], w[0, 3])
    a3b2, a5b6 = z_down(a2b1), z_up(a6b7)
    w[1, 1], w[1, 3], w[0, 2] = swap_xh(w[0, 1]), y_up(w[1, 0]), y_down(w[0, 1])
    w13, w11, w[0, 2], a3b2, a5b6 = tie(w[1, 3], w[1, 1], w[0, 2], a3b2, a5b6)
    w[1, 1], w[1, 3] = w11, w13
    k = w13.shape[0] // 2
    w[1, 2] = jnp.concatenate([y_up(w13[:k]), y_down(w11[k:])])
    a4b3, b[5] = z_down(a3b2), z_up(a5b6[:, n:])
    b[4] = move_tensor(a5b6[:, :n], lambda xl, z: (xl + 1, z + 1))
    weights = [w[k] for k in ORDER]

    early = [
        (a[0], 0), (b[0], 0), (a[1], 0), (a2b1, n), (a[7], 0), (a6b7, n), (a2b1, 0), (a3b2, n), (a6b7, 0), (a5b6, n)
    ]
    late = [(a3b2, 0), (a4b3, n), (a5b6, 0), (b[5], 0), (a4b3, 0), (b[4], 0)]
    part1, rows1 = forward(early, n, weights, 2)
    other1 = [swap_core(x) for x in part1]
    part2, rows2 = forward(late, n, weights, 1)
    other2 = [swap_core(x) for x in part2]
    acts1 = activations(part1, other1)
    acts2, terms2, first = backward(
        part2, other2, weights, len(CHUNKS[1]), scale, prev=(acts1,), chunks=(rows1, rows2), count=FIRST
    )
    rest = weight_grads((acts1, acts2), (rows1, rows2), FIRST, len(ORDER) - FIRST, scale)
    terms = dict(zip(CHUNKS[1], terms2, strict=True))

    p = dict(zip(ORDER, [*first, *rest], strict=True))
    r02 = y_up(p[0, 2])
    r12 = y_down(p[1, 2])
    r10 = swap_xh(p[1, 0])
    r11 = move_dw(p[1, 1], lambda xh, y, c: (xh + 1, y + 1, c))
    r03 = y_down(p[0, 3])
    p01, p13, _, _ = tie(add(p[0, 1], r02), add(p[1, 3], r12), r11, r03)
    r01 = y_up(p01)
    r13 = move_dw(p13, lambda xh, y, c: (xh + 1, y - 1, c))

    up = z_up(terms[4][:n])
    down = z_down(terms[4][n:])
    up = z_up(terms[3].at[:n].set(add(terms[3][:n], up)))
    down = z_down(terms[5].at[n:].set(add(terms[5][n:], down)))
    up, down, acts1 = tie(up, down, acts1)
    terms.update(zip(CHUNKS[0], token_terms(acts1, weights, len(CHUNKS[0])), strict=True))
    up, down, *_ = tie(up, down, r02, r12, r10)
    up = z_up(add(terms[2], up))
    down = z_down(add(terms[6], down))
    up, down, *_ = tie(up, down, r11, r03)
    up = z_up(add(terms[1], up))
    down = z_down(add(terms[7], down))
    total = add(terms[0], up, down).reshape(NXL, NCORE, rows, -1)
    low, high = total[:, 0], total[:, 1]
    mine = jnp.where(core == 0, low, high)
    theirs = jnp.where(core == 0, high, low)
    from_core = swap_core(theirs[0])
    from_both = move_all(theirs[1], lambda xl, z, xh, y, c: (xl + 1, z, xh, y, c + 1))
    return tuple(
        finish(
            here,
            (mine[0], swap_xl(mine[1])),
            (from_core, from_both),
            (p[0, 0], r10, r11, r03, r01, r13),
        )
    )


def solution(mesh):
    placed = (
        P(("tensor", "dw"), None),
        P(("tensor", "dw"), None),
        P("dw", "tensor"),
        P("dw", "tensor"),
        P("tensor", "dw"),
    )
    return jax.shard_map(
        body,
        mesh=mesh,
        in_specs=placed,
        out_specs=(
            P(("tensor", "dw"), None),
            P("dw", "tensor"),
            P("dw", "tensor"),
            P("tensor", "dw"),
        ),
        check_vma=False,
    )
```

```python
import functools
import itertools
import math

import jax
import jax.numpy as jnp
from jax import lax
from jax.experimental import pallas as pl
from jax.experimental.pallas import tpu as pltpu
from jax.sharding import PartitionSpec as P

NXL, NZ, NXH, NY, NCORE = 2, 8, 2, 4, 2
BF16, F32 = jnp.bfloat16, jnp.float32
VMEM_LIMIT = 20 * 1024 * 1024

ORDER = ((0, 2), (1, 2), (1, 0), (1, 1), (0, 3), (0, 1), (1, 3), (0, 0))
FIRST = 5
CHUNKS = ((0, 1, 7, 2, 6), (3, 5, 4))


def move_tensor(x, dest):
    perm = []
    for xl in range(NXL):
        for z in range(NZ):
            a, b = dest(xl, z)
            perm.append((xl * NZ + z, a % NXL * NZ + b % NZ))
    return lax.ppermute(x, "tensor", perm)


def move_dw(x, dest):
    perm = []
    for xh in range(NXH):
        for y in range(NY):
            for c in range(NCORE):
                a, b, e = dest(xh, y, c)
                perm.append(
                    ((xh * NY + y) * NCORE + c, (a % NXH * NY + b % NY) * NCORE + e % NCORE)
                )
    return lax.ppermute(x, "dw", perm)


def move_all(x, dest):
    sizes = (NXL, NZ, NXH, NY, NCORE)
    perm = []
    for at in itertools.product(*map(range, sizes)):
        ends = at, dest(*at)
        source, target = (
            functools.reduce(lambda n, e: n * e[1] + e[0] % e[1], zip(end, sizes), 0) for end in ends
        )
        perm.append((source, target))
    return lax.ppermute(x, ("tensor", "dw"), perm)


def z_up(x):
    return move_tensor(x, lambda xl, z: (xl, z + 1))


def z_down(x):
    return move_tensor(x, lambda xl, z: (xl, z - 1))


def swap_xl(x):
    return move_tensor(x, lambda xl, z: (xl + 1, z))


def y_up(x):
    return move_dw(x, lambda xh, y, c: (xh, y + 1, c))


def y_down(x):
    return move_dw(x, lambda xh, y, c: (xh, y - 1, c))


def swap_xh(x):
    return move_dw(x, lambda xh, y, c: (xh + 1, y, c))


def swap_core(x):
    return move_dw(x, lambda xh, y, c: (xh, y, c + 1))


def vmem():
    return pl.BlockSpec(memory_space=pltpu.VMEM)


def hbm():
    return pl.BlockSpec(memory_space=pl.ANY)


def pinned():
    return pl.BlockSpec(memory_space=pltpu.HBM)


def call(kernel, outs, ins, out_specs, in_specs, scratch=(), flops=0, moved=0, name=None, limit=VMEM_LIMIT):
    return pl.pallas_call(
        kernel,
        out_shape=outs,
        in_specs=in_specs,
        out_specs=out_specs,
        scratch_shapes=list(scratch),
        compiler_params=pltpu.CompilerParams(vmem_limit_bytes=limit),
        cost_estimate=pl.CostEstimate(flops=0, bytes_accessed=1024, transcendentals=0),
        name=name,
    )(*ins)


def places(dw):
    core, y, xh = dw % NCORE, dw // NCORE % NY, dw // (NCORE * NY)
    return [
        [((xh + dx) % NXH * NY + (y + dy) % NY) * NCORE + c for dx, dy in ORDER]
        for c in (core, 1 - core)
    ]


def prep_tokens(dw, tokens, out_grad):
    rows, width = tokens.shape
    half = width // NCORE
    block = half // len(ORDER)

    def kernel(dw_ref, tok_ref, grad_ref, own_ref, other_ref):
        for out, blocks in zip((own_ref, other_ref), places(dw_ref[0]), strict=True):
            for j, place in enumerate(blocks):
                cols = slice(j * block, (j + 1) * block)
                at = pl.multiple_of(place * block, block)
                out[0, :, cols] = tok_ref[:, pl.ds(at, block)]
                out[1, :, cols] = grad_ref[:, pl.ds(at, block)]

    shape = jax.ShapeDtypeStruct((2, rows, half), BF16)
    return call(
        kernel, (shape, shape), (dw, tokens, out_grad), (vmem(), vmem()),
        [pl.BlockSpec(memory_space=pltpu.SMEM), vmem(), vmem()],
        moved=8 * rows * width, name="prep_tokens", limit=56 * 1024 * 1024,
    )


def prep_weights(gate, up, down):
    depth, width = gate.shape

    def kernel(gate_ref, up_ref, down_ref, out_ref):
        out_ref[:, :width] = gate_ref[...]
        out_ref[:, width : 2 * width] = up_ref[...]
        out_ref[:, 2 * width :] = down_ref[...].T

    return call(
        kernel, jax.ShapeDtypeStruct((depth, 3 * width), BF16), (gate, up, down), vmem(),
        [vmem()] * 3, moved=12 * depth * width, name="prep_weights",
    )


def start_all(copies):
    for c in copies:
        c.start()


def wait_all(copies):
    for c in copies:
        c.wait()


def forward(pieces, rows, weights, splits):
    shards = [x for x, _ in pieces]
    n_t, n_w = len(pieces), len(weights)
    half = shards[0].shape[2]
    depth, width3 = weights[0].shape
    width, width2 = width3 // 3, width3 // 3 * 2
    total = n_t * rows
    each = total // splits
    parts = 2
    per = n_w // parts

    def kernel(*refs):
        t_in, w_in = refs[:n_t], refs[n_t : n_t + n_w]
        outs, (rows_ref, tbuf, wbuf, acc, tsem, wsem, osem) = refs[n_t + n_w :][: 3 * splits], refs[n_t + n_w + 3 * splits :]
        t_copies = [
            pltpu.make_async_copy(
                r.at[:, pl.ds(pieces[i][1], rows)], tbuf.at[:, pl.ds(i * rows, rows)], tsem.at[i]
            )
            for i, r in enumerate(t_in)
        ]
        w_copies = [
            pltpu.make_async_copy(r, wbuf.at[pl.ds(j * depth, depth)], wsem.at[j])
            for j, r in enumerate(w_in)
        ]
        start_all(t_copies + w_copies)
        wait_all(t_copies)
        keep = pltpu.make_async_copy(tbuf, rows_ref, osem)
        keep.start()
        for p in range(parts):
            wait_all(w_copies[p * per : (p + 1) * per])
            ks = slice(p * per * depth, (p + 1) * per * depth)
            for k, cols in enumerate((slice(0, width2), slice(width2, width3))):
                term = jnp.dot(tbuf[k, :, ks], wbuf[ks, cols], preferred_element_type=F32)
                if p > 0:
                    term = term + acc[:, cols]
                if p < parts - 1:
                    acc[:, cols] = term
                else:
                    for i in range(term.shape[1] // width):
                        part = term[:, i * width : (i + 1) * width].astype(BF16)
                        for h in range(splits):
                            outs[3 * h + 2 * k + i][...] = part[h * each : (h + 1) * each]
        keep.wait()

    *partial, chunk = call(
        kernel,
        (jax.ShapeDtypeStruct((each, width), BF16),) * (3 * splits)
        + (jax.ShapeDtypeStruct((2, total, half), BF16),),
        (*shards, *weights), (vmem(),) * (3 * splits) + (hbm(),), [hbm()] * (n_t + n_w),
        scratch=(
            pltpu.VMEM((2, total, half), BF16),
            pltpu.VMEM((half, width3), BF16),
            pltpu.VMEM((total, width3), F32),
            pltpu.SemaphoreType.DMA((n_t,)),
            pltpu.SemaphoreType.DMA((n_w,)),
            pltpu.SemaphoreType.DMA,
        ),
        flops=2 * total * half * width3,
        moved=2 * (4 * total * half + half * width3 + total * width3),
        name="forward",
    )
    return partial, chunk


def activate(a, b, src, out, dst, step):
    width = a[0].shape[1]
    gate, up, grad = (p[src, :].astype(F32) + q[src, :].astype(F32) for p, q in zip(a, b, strict=True))
    s = 0.5 + 0.5 * jnp.tanh(0.5 * gate)
    act = gate * s
    out[dst, 2 * width :] = (act * up).astype(BF16)
    out[dst, :width] = (grad * up * s * (1.0 + gate * (1.0 - s))).astype(BF16)
    out[dst, width : 2 * width] = (grad * act).astype(BF16)


def activations(mine, other):
    rows, width = mine[0].shape
    count = len(mine)
    splits = count // 3
    step = 16

    def kernel(*refs):
        a, b, out_ref = refs[:count], refs[count : 2 * count], refs[2 * count]
        for h in range(splits):

            def one(i, _, h=h):
                src = pl.ds(pl.multiple_of(i * step, step), step)
                dst = pl.ds(pl.multiple_of(h * rows + i * step, step), step)
                activate(a[3 * h : 3 * h + 3], b[3 * h : 3 * h + 3], src, out_ref, dst, step)
                return 0

            lax.fori_loop(0, rows // step, one, 0)

    return call(
        kernel, jax.ShapeDtypeStruct((splits * rows, 3 * width), BF16), (*mine, *other), vmem(),
        [vmem()] * (2 * count), flops=30 * splits * rows * width, moved=18 * splits * rows * width,
        name="activations",
    )


def token_terms(acts, weights, pieces):
    n_w = len(weights)
    rows, width3 = acts.shape
    width2 = width3 // 3 * 2
    depth = weights[0].shape[0]
    half = n_w * depth
    per = rows // pieces
    halves = 2
    cols = half // halves

    def kernel(*refs):
        a_ref, w_in, terms = refs[0], refs[1 : 1 + n_w], refs[1 + n_w : 1 + n_w + pieces]
        abuf, wbuf, qbuf, asem, wsem, osem = refs[1 + n_w + pieces :]
        a_copy = pltpu.make_async_copy(a_ref.at[:, pl.ds(0, width2)], abuf, asem)
        w_copies = [
            pltpu.make_async_copy(
                r.at[:, pl.ds(0, width2)], wbuf.at[pl.ds(j * depth, depth)], wsem.at[j]
            )
            for j, r in enumerate(w_in)
        ]
        a_copy.start()
        start_all(w_copies)
        a_copy.wait()
        out = []
        for h in range(halves):
            wait_all(w_copies[h * n_w // halves : (h + 1) * n_w // halves])
            term_columns(abuf, wbuf, qbuf, terms, osem, h, cols, depth, per, out)
        wait_all(out)

    return call(
        kernel, (jax.ShapeDtypeStruct((per, half), BF16),) * pieces, (acts, *weights),
        (pinned(),) * pieces, [pinned()] * (1 + n_w),
        scratch=(
            pltpu.VMEM((rows, width2), BF16),
            pltpu.VMEM((half, width2), BF16),
            pltpu.VMEM((rows, half), BF16),
            pltpu.SemaphoreType.DMA,
            pltpu.SemaphoreType.DMA((n_w,)),
            pltpu.SemaphoreType.DMA((halves * pieces,)),
        ),
        flops=2 * rows * half * width2, moved=2 * (rows * width2 + half * width2 + rows * half),
        name="token_terms",
    )


def term_columns(acts, wbuf, qbuf, terms, osem, h, cols, depth, per, out, sem=0):
    for n in range(h * cols, (h + 1) * cols, depth):
        qbuf[:, n : n + depth] = lax.dot_general(
            acts[...], wbuf[n : n + depth, :], (((1,), (1,)), ((), ())), preferred_element_type=F32
        ).astype(BF16)
    for k, r in enumerate(terms):
        c = pltpu.make_async_copy(
            qbuf.at[pl.ds(k * per, per), pl.ds(h * cols, cols)],
            r.at[:, pl.ds(h * cols, cols)],
            osem.at[sem + h * len(terms) + k],
        )
        c.start()
        out.append(c)


def backward(mine, other, weights, pieces, scale, prev=(), chunks=(), count=0):
    n_w, n_p, n_c = len(weights), len(prev), len(chunks)
    rows, width = mine[0].shape
    width3 = 3 * width
    depth = weights[0].shape[0]
    half = n_w * depth
    per = rows // pieces
    prev_rows = [r.shape[0] for r in prev]
    starts = [sum(prev_rows[:i]) for i in range(n_p + 1)]
    total = starts[-1] + rows
    step = 16
    halves = 2

    def kernel(*refs):
        refs = list(refs)

        def take(n):
            got = refs[:n]
            del refs[:n]
            return got

        parts, w_in, prev_in, t_in = take(6), take(n_w), take(n_p), take(n_c)
        (acts_ref,), terms, grads = take(1), take(pieces), take(count)
        pbuf, abuf, wbuf, qbuf, tbuf, gbuf, psem, wsem, tsem, osem = refs
        here = starts[-1]
        bufs = [pbuf.at[k] for k in range(6)]
        p_copies = [pltpu.make_async_copy(r, pbuf.at[k], psem.at[k]) for k, r in enumerate(parts)]
        t_copies = [
            pltpu.make_async_copy(r, abuf.at[pl.ds(starts[i], prev_rows[i])], tsem.at[i])
            for i, r in enumerate(prev_in)
        ] + [
            pltpu.make_async_copy(
                r.at[:, :, pl.ds(0, count * depth)],
                tbuf.at[:, pl.ds(starts[i], r.shape[1])],
                tsem.at[n_p + i],
            )
            for i, r in enumerate(t_in)
        ]
        w_copies = [
            pltpu.make_async_copy(
                r.at[:, pl.ds(0, 2 * width)], wbuf.at[pl.ds(j * depth, depth)], wsem.at[j]
            )
            for j, r in enumerate(w_in)
        ]
        start_all(p_copies + t_copies + w_copies)
        wait_all(p_copies)

        def one(i, _):
            src = pl.ds(pl.multiple_of(i * step, step), step)
            dst = pl.ds(pl.multiple_of(here + i * step, step), step)
            activate(bufs[:3], bufs[3:], src, abuf, dst, step)
            return 0

        lax.fori_loop(0, rows // step, one, 0)
        out = [pltpu.make_async_copy(abuf.at[pl.ds(here, rows)], acts_ref, osem.at[0])]
        out[0].start()
        if count:
            wait_all(t_copies)
            weight_terms(abuf, tbuf, gbuf, grads, osem, 1, 0, count, scale, out)
        cols = half // halves
        for h in range(halves):
            wait_all(w_copies[h * n_w // halves : (h + 1) * n_w // halves])
            term_columns(
                abuf.at[pl.ds(here, rows), pl.ds(0, 2 * width)],
                wbuf, qbuf, terms, osem, h, cols, depth, per, out, 1 + count,
            )
        wait_all(out)

    shapes = (
        [jax.ShapeDtypeStruct((rows, width3), BF16)]
        + [jax.ShapeDtypeStruct((per, half), BF16)] * pieces
        + [jax.ShapeDtypeStruct((depth, width3), BF16)] * count
    )
    got = call(
        kernel, shapes, (*mine, *other, *weights, *prev, *chunks), [pinned()] * len(shapes),
        [hbm()] * (6 + n_w + n_p + n_c),
        scratch=(
            pltpu.VMEM((6, rows, width), BF16),
            pltpu.VMEM((total, width3), BF16),
            pltpu.VMEM((half, 2 * width), BF16),
            pltpu.VMEM((rows, half), BF16),
            pltpu.VMEM((2, total, max(count, 1) * depth), BF16),
            pltpu.VMEM((max(count, 1), depth, width3), BF16),
            pltpu.SemaphoreType.DMA((6,)),
            pltpu.SemaphoreType.DMA((n_w,)),
            pltpu.SemaphoreType.DMA((max(n_p + n_c, 1),)),
            pltpu.SemaphoreType.DMA((1 + count + halves * pieces,)),
        ),
        flops=4 * rows * half * width + 2 * total * count * depth * width3,
        moved=2 * (3 * rows * width3 + 2 * half * width + rows * half),
        name="backward",
    )
    return got[0], got[1 : 1 + pieces], got[1 + pieces :]


def weight_terms(abuf, tbuf, gbuf, grads, osem, sem, first, count, scale, out):
    depth, width3 = gbuf.shape[1:]
    width2 = width3 // 3 * 2
    dims = (((0,), (0,)), ((), ()))
    for j in range(first, first + count):
        cols = slice(j * depth, (j + 1) * depth)
        for k, w in enumerate((slice(0, width2), slice(width2, width3))):
            got = lax.dot_general(tbuf[k, :, cols], abuf[:, w], dims, preferred_element_type=F32)
            gbuf[j, :, w] = (got * scale).astype(BF16)
        c = pltpu.make_async_copy(gbuf.at[j], grads[j], osem.at[sem + j])
        c.start()
        out.append(c)


def weight_grads(acts, chunks, first, count, scale):
    n_a = len(acts)
    width3 = acts[0].shape[1]
    rows = [r.shape[0] for r in acts]
    starts = [sum(rows[:i]) for i in range(n_a)]
    depth = chunks[0].shape[2] // len(ORDER)
    group = 2
    groups = [(g, min(group, count - g)) for g in range(0, count, group)]
    total = sum(rows)

    def kernel(*refs):
        a_in, t_in, grads = refs[:n_a], refs[n_a : 2 * n_a], refs[2 * n_a : 2 * n_a + count]
        abuf, tbuf, gbuf, asem, tsem, osem = refs[2 * n_a + count :]
        a_copies = [
            pltpu.make_async_copy(r, abuf.at[pl.ds(starts[i], rows[i])], asem.at[i])
            for i, r in enumerate(a_in)
        ]
        t_copies = [
            [
                pltpu.make_async_copy(
                    r.at[:, :, pl.ds((first + g) * depth, size * depth)],
                    tbuf.at[:, pl.ds(starts[i], rows[i]), pl.ds(g * depth, size * depth)],
                    tsem.at[k * n_a + i],
                )
                for i, r in enumerate(t_in)
            ]
            for k, (g, size) in enumerate(groups)
        ]
        start_all(a_copies)
        for g in t_copies:
            start_all(g)
        wait_all(a_copies)
        out = []
        for k, (g, size) in enumerate(groups):
            wait_all(t_copies[k])
            weight_terms(abuf, tbuf, gbuf, grads, osem, 0, g, size, scale, out)
        wait_all(out)

    return call(
        kernel, (jax.ShapeDtypeStruct((depth, width3), BF16),) * count, (*acts, *chunks),
        (pinned(),) * count, [pinned()] * (2 * n_a),
        scratch=(
            pltpu.VMEM((total, width3), BF16),
            pltpu.VMEM((2, total, count * depth), BF16),
            pltpu.VMEM((count, depth, width3), BF16),
            pltpu.SemaphoreType.DMA((n_a,)),
            pltpu.SemaphoreType.DMA((len(groups) * n_a,)),
            pltpu.SemaphoreType.DMA((count,)),
        ),
        flops=2 * total * count * depth * width3,
        moved=2 * (total * width3 + 2 * total * count * depth + count * depth * width3),
        name="weight_grads",
    )


def tie(*arrays):
    return lax.optimization_barrier(arrays)


def add(*terms):
    total = terms[0].astype(F32)
    for t in terms[1:]:
        total = total + t.astype(F32)
    return total.astype(BF16)


def finish(dw, own, other, terms):
    rows, half = own[0].shape
    block = half // len(ORDER)
    depth, width3 = terms[0].shape
    width = width3 // 3

    def kernel(*refs):
        dw_ref, pairs, terms_in = refs[0], (refs[1:3], refs[3:5]), refs[5 : 5 + len(terms)]
        token_ref, gate_ref, up_ref, down_ref = refs[5 + len(terms) :]
        for (p, q), blocks in zip(pairs, places(dw_ref[0]), strict=True):
            for j, place in enumerate(blocks):
                cols = slice(j * block, (j + 1) * block)
                total = p[:, cols].astype(F32) + q[:, cols].astype(F32)
                token_ref[:, pl.ds(pl.multiple_of(place * block, block), block)] = total.astype(BF16)

        def total(k):
            cols = slice(k * width, (k + 1) * width)
            return sum(r[:, cols].astype(F32) for r in terms_in).astype(BF16)

        gate_ref[...] = total(0)
        up_ref[...] = total(1)
        down_ref[...] = total(2).T

    shapes = [
        jax.ShapeDtypeStruct(s, BF16)
        for s in ((rows, NCORE * half), (depth, width), (depth, width), (width, depth))
    ]
    return call(
        kernel, shapes, (dw, *own, *other, *terms), [vmem()] * 4,
        [pl.BlockSpec(memory_space=pltpu.SMEM)] + [vmem()] * (4 + len(terms)),
        moved=12 * rows * half + 40 * depth * width, name="finish",
    )


def body(tokens, out_grad, gate_weight, up_weight, down_weight):
    rows = tokens.shape[0]
    scale = 1.0 / math.sqrt(rows * lax.axis_size("tensor") * lax.axis_size("dw"))
    dw = lax.axis_index("dw")
    core = dw % NCORE
    here = dw.astype(jnp.int32).reshape(1)

    own_part, other_part = prep_tokens(here, tokens, out_grad)
    got = swap_core(other_part)
    low = jnp.where(core == 0, own_part, got)
    high = jnp.where(core == 0, got, own_part)
    a = {0: jnp.concatenate([low, high], axis=1)}
    w = {(0, 0): prep_weights(gate_weight, up_weight, down_weight)}

    n = NCORE * rows
    a[1], a[7] = z_down(a[0]), z_up(a[0])
    b = {0: swap_xl(a[0])}
    w[1, 0], w[0, 1], w[0, 3] = swap_xh(w[0, 0]), y_down(w[0, 0]), y_up(w[0, 0])
    a2b1 = z_down(jnp.concatenate([a[1], b[0]], axis=1))
    a6b7 = z_up(jnp.concatenate([a[7], b[0]], axis=1))
    a2b1, a6b7, *_ = tie(a2b1, a6b7, w[1, 0], w[0, 1], w[0, 3])
    a3b2, a5b6 = z_down(a2b1), z_up(a6b7)
    w[1, 1], w[1, 3], w[0, 2] = swap_xh(w[0, 1]), y_up(w[1, 0]), y_down(w[0, 1])
    w13, w11, w[0, 2], a3b2, a5b6 = tie(w[1, 3], w[1, 1], w[0, 2], a3b2, a5b6)
    w[1, 1], w[1, 3] = w11, w13
    k = w13.shape[0] // 2
    w[1, 2] = jnp.concatenate([y_up(w13[:k]), y_down(w11[k:])])
    a4b3, b[5] = z_down(a3b2), z_up(a5b6[:, n:])
    b[4] = move_tensor(a5b6[:, :n], lambda xl, z: (xl + 1, z + 1))
    weights = [w[k] for k in ORDER]

    early = [
        (a[0], 0), (b[0], 0), (a[1], 0), (a2b1, n), (a[7], 0), (a6b7, n), (a2b1, 0), (a3b2, n), (a6b7, 0), (a5b6, n)
    ]
    late = [(a3b2, 0), (a4b3, n), (a5b6, 0), (b[5], 0), (a4b3, 0), (b[4], 0)]
    part1, rows1 = forward(early, n, weights, 2)
    other1 = [swap_core(x) for x in part1]
    part2, rows2 = forward(late, n, weights, 1)
    other2 = [swap_core(x) for x in part2]
    acts1 = activations(part1, other1)
    acts2, terms2, first = backward(
        part2, other2, weights, len(CHUNKS[1]), scale, prev=(acts1,), chunks=(rows1, rows2), count=FIRST
    )
    rest = weight_grads((acts1, acts2), (rows1, rows2), FIRST, len(ORDER) - FIRST, scale)
    terms = dict(zip(CHUNKS[1], terms2, strict=True))

    p = dict(zip(ORDER, [*first, *rest], strict=True))
    r02 = y_up(p[0, 2])
    r12 = y_down(p[1, 2])
    r10 = swap_xh(p[1, 0])
    r11 = move_dw(p[1, 1], lambda xh, y, c: (xh + 1, y + 1, c))
    r03 = y_down(p[0, 3])
    p01, p13, _, _ = tie(add(p[0, 1], r02), add(p[1, 3], r12), r11, r03)
    r01 = y_up(p01)
    r13 = move_dw(p13, lambda xh, y, c: (xh + 1, y - 1, c))

    up = z_up(terms[4][:n])
    down = z_down(terms[4][n:])
    up = z_up(terms[3].at[:n].set(add(terms[3][:n], up)))
    down = z_down(terms[5].at[n:].set(add(terms[5][n:], down)))
    up, down, acts1 = tie(up, down, acts1)
    terms.update(zip(CHUNKS[0], token_terms(acts1, weights, len(CHUNKS[0])), strict=True))
    up, down, *_ = tie(up, down, r02, r12, r10)
    up = z_up(add(terms[2], up))
    down = z_down(add(terms[6], down))
    up, down, *_ = tie(up, down, r11, r03)
    up = z_up(add(terms[1], up))
    down = z_down(add(terms[7], down))
    total = add(terms[0], up, down).reshape(NXL, NCORE, rows, -1)
    low, high = total[:, 0], total[:, 1]
    mine = jnp.where(core == 0, low, high)
    theirs = jnp.where(core == 0, high, low)
    from_core = swap_core(theirs[0])
    from_both = move_all(theirs[1], lambda xl, z, xh, y, c: (xl + 1, z, xh, y, c + 1))
    return tuple(
        finish(
            here,
            (mine[0], swap_xl(mine[1])),
            (from_core, from_both),
            (p[0, 0], r10, r11, r03, r01, r13),
        )
    )


def solution(mesh):
    placed = (
        P(("tensor", "dw"), None),
        P(("tensor", "dw"), None),
        P("dw", "tensor"),
        P("dw", "tensor"),
        P("tensor", "dw"),
    )
    return jax.shard_map(
        body,
        mesh=mesh,
        in_specs=placed,
        out_specs=(
            P(("tensor", "dw"), None),
            P("dw", "tensor"),
            P("dw", "tensor"),
            P("tensor", "dw"),
        ),
        check_vma=False,
    )
```
